256 devices in a mesh: ctx: 16 (over y_hi, z), exp: 8 (over x, core), dp: 2 (over y_lo).
Axes of the slice: x: 4, y: 4 (y_hi: 2, y_lo: 2; y = y_hi * 2 + y_lo), z: 8, core: 2. Of those that a mesh axis runs over, the one named last changes fastest.
Arguments:
- residual: bfloat16 [4096, 4096], P(('dp', 'ctx', 'exp')), parts along dimension 0, may hold values from -0.59765625 to 0.59765625
- encoded_query_rows: bfloat16 [4096, 4096], P(('dp', 'ctx'), 'exp'), parts along dimension 0, may hold values from -256 to 256
- quantized_key_rows: bfloat16 [4096, 512], P(('dp', 'ctx')), parts along dimension 0, may hold values from -8 to 8
- quantized_value_rows: bfloat16 [4096, 512], P(('dp', 'ctx')), parts along dimension 0, may hold values from -6 to 6
- key_block_exponent: int32 [64, 4], P(('dp', 'ctx')), parts along dimension 0, may hold values from -2 to 1
- value_block_exponent: int32 [64, 4], P(('dp', 'ctx')), parts along dimension 0, may hold values from -2 to 1
- block_order: int32 [16], replicated, may hold values from 0 to 15, each once
- out_weight: bfloat16 [4096, 4096], P('exp', 'ctx'), may hold values from -0.09375 to 0.09375
- norm_gain: float32 [4096], replicated, may hold values from 0.1 to 1.9
- expert_ids: int32 [4096, 8], P(('dp', 'ctx', 'exp')), parts along dimension 0, may hold values from 0 to 63, all different within a row; in each aligned block of 16 rows (0 to 15, 16 to 31, ...) at most 3 rows name the same one
- route_weight: float32 [4096, 8], P(('dp', 'ctx', 'exp')), parts along dimension 0, may hold values from 0.05 to 0.25
- gate_weight: bfloat16 [128, 4096, 384], P(('ctx', 'exp')), may hold values from -0.09375 to 0.09375
- gate_scale: int32 [128, 32, 3], P(('ctx', 'exp')), may hold values from -1 to 1
- up_weight: bfloat16 [128, 4096, 384], P(('ctx', 'exp')), may hold values from -0.09375 to 0.09375
- up_scale: int32 [128, 32, 3], P(('ctx', 'exp')), may hold values from -1 to 1
- down_weight: bfloat16 [128, 384, 4096], P(('ctx', 'exp')), may hold values from -0.21875 to 0.21875
- down_scale: int32 [128, 3, 32], P(('ctx', 'exp')), may hold values from -1 to 1
Outputs:
- layer_out: bfloat16 [4096, 4096], P(('dp', 'ctx', 'exp')), parts along dimension 0
The draws below stay inside these ranges and needn't reach their ends.
There are 2 independent parts, one for each index of `dp`. The reference program is written for one: setup_inputs(seed, part) draws one part's arguments, and reference() takes and returns one part's arrays. A program takes and returns all parts, laid end to end along the dimension named above; an argument that names none is the same for every part. Nothing has to cross between parts.
Inputs may be any that keep to these rules, and one draw needn't show every extreme that they name: `expert_ids`: each row names 8 different experts. Among the rows of one device (16 aligned rows), no expert is named by more than 3 rows, a bound that some block reaches. `block_order`: A permutation of the ctx indices.
All inputs are finite; a program needn't handle non-finite values.
Results may differ from the reference program's by a relative error of at most 0.03.
Values may be sent and summed in bfloat16 or wider, within the bound.
A program may use at most 128 MiB of HBM per device.

```python
import math
import jax
import jax.numpy as jnp
import numpy as np
from jax import lax

D = 4096
QUERY_HEADS = 32
KEY_VALUE_HEADS = 4
HEAD_SIZE = 128
FF = 768
TOP = 8
SCALE_POSITIONS = 64
WB = 128
TOK_DEV = 16
CONTEXT_SPAN = 128
SEQUENCE_TOKENS = 2048
EXP = 64
CAP = 3
N_CTX = 16


def common_keys(key):
    return jnp.clip(jax.random.normal(key, (SEQUENCE_TOKENS, KEY_VALUE_HEADS * HEAD_SIZE), jnp.float32), -6.0, 6.0)


def draw_quantized_key_rows(key, part):
    start_offset = common_keys(key)
    return start_offset.astype(jnp.bfloat16)


def draw_encoded_query_rows(key, part):
    key = jax.random.fold_in(key, 7)
    first_key = jax.random.fold_in(key, 0)
    queries = jnp.clip(jax.random.normal(first_key, (SEQUENCE_TOKENS, QUERY_HEADS * HEAD_SIZE), jnp.float32), -6.0, 6.0)
    return queries.astype(jnp.bfloat16)


def place_ends(values, key, least, largest):
    shape = values.shape
    place = [jax.random.randint(jax.random.fold_in(key, axis), (), 0, shape[axis]) for axis in range(len(shape))]
    values = values.at[tuple(place)].set(least)
    longest = shape.index(max(shape))
    place[longest] = (place[longest] + 1) % shape[longest]
    return values.at[tuple(place)].set(largest)


def levels(key, shape, cuts, smallest, high):
    def one(dim, parts):
        steps = jax.random.uniform(jax.random.fold_in(jax.random.fold_in(key, 6), dim), (parts,), jnp.float32, smallest / len(cuts), high / len(cuts))
        return jnp.repeat(jnp.exp(steps), shape[dim] // parts).reshape((-1,) + (1,) * (len(shape) - dim - 1))

    level = one(*cuts[0])
    for cut in cuts[1:]:
        level = level * one(*cut)
    return level


def deal_out(key, own, number, rows, number_of, top, reach, lean):
    ranking = jax.random.permutation(key, number_of)
    heavy_load, ordinary = load_shares(number_of, rows * top, reach, lean, True), load_shares(number_of, rows * top, reach, lean, False)
    places = jnp.arange(number_of)

    def named(sizes, rotation):
        used = int((sizes > 0).sum())
        fixed = max(1, used // 4)
        shifted = fixed + (places - fixed + rotation * (used - fixed)) % max(1, number_of - fixed)
        return jnp.zeros((number_of,), jnp.int32).at[ranking[jnp.where(places < fixed, places, shifted)]].set(jnp.asarray(sizes, jnp.int32))

    sizes = jnp.where(number % 4 == 0, named(heavy_load, number // 4), named(ordinary, number - number // 4 - 1))
    mixed = jax.random.permutation(jax.random.fold_in(own, 3), number_of)
    source_of, receiver = mixed[0:number_of // 2 * 2:2], mixed[1:number_of // 2 * 2:2]
    margin = jnp.minimum(sizes[source_of] - 1, reach - sizes[receiver]) // 2
    margin = jnp.where((source_of == ranking[0]) | (receiver == ranking[0]) | (sizes[receiver] == 0), 0, jnp.maximum(margin, 0))
    shifted = jax.random.randint(jax.random.fold_in(own, 4), (number_of // 2,), 0, 1 << 20) % (margin + 1)
    sizes = sizes.at[source_of].add(-shifted).at[receiver].add(shifted)
    items = jnp.searchsorted(jnp.cumsum(sizes), jnp.arange(rows * top), side="right").astype(jnp.int32)
    listing = items.reshape(top, rows).T
    listing = listing[jax.random.permutation(jax.random.fold_in(own, 1), rows)]
    rotation = jax.random.randint(jax.random.fold_in(own, 2), (rows, 1), 0, top)
    return jnp.take_along_axis(listing, (jnp.arange(top)[None, :] + rotation) % top, axis=1)


def load_shares(amount, total, most, slope, full):
    loads = [(1 << 20) // math.isqrt(standing ** slope) + 1 for standing in range(1, amount + 1)]
    largest = most if full else min(most, max(-(-total // amount), total * loads[0] // sum(loads)))
    least = 1 if total - largest >= amount - 1 else 0
    counts, rest = [largest] + [least] * (amount - 1), total - largest - least * (amount - 1)
    while rest > 0:
        movable = [i for i in range(1, amount) if counts[i] < largest] or [i for i in range(1, amount) if counts[i] < most]
        whole, left = sum([loads[i] for i in movable]), rest
        for i in movable:
            more = min(most - counts[i], max(1, left * loads[i] // whole), rest)
            counts[i] = counts[i] + more
            rest = rest - more
    return np.array(counts)


def noise(stream_key, dims, deviation, most, cuts=(), kind=jnp.bfloat16):
    loudness = levels(stream_key, dims, cuts, -0.22, 0.18) if cuts else 1.0
    entries = jax.random.normal(stream_key, dims, jnp.float32) * deviation * loudness
    return jnp.minimum(jnp.maximum(entries, -most), most).astype(kind)


def setup_inputs(seed: int = 0, part: int = 0) -> dict:
    splits = jax.random.split(jax.random.key(seed), 18)
    own_keys = jax.random.split(jax.random.fold_in(splits[17], part), 18)
    residual = noise(own_keys[0], (SEQUENCE_TOKENS, D), 0.1, 0.59765625, ((0, 128),))
    encoded_query_rows = draw_encoded_query_rows(jax.random.fold_in(jax.random.fold_in(splits[17], part), 71), part)
    quantized_key_rows = draw_quantized_key_rows(jax.random.fold_in(jax.random.fold_in(splits[17], part), 71), part)
    quantized_value_rows = noise(own_keys[3], (SEQUENCE_TOKENS, KEY_VALUE_HEADS * HEAD_SIZE), 1.0, 6.0, ((0, 16),))
    key_block_exponent = place_ends(jax.random.randint(own_keys[4], (SEQUENCE_TOKENS // SCALE_POSITIONS, KEY_VALUE_HEADS), -2, 2), jax.random.fold_in(own_keys[4], 1), -2, 1).astype(jnp.int32)
    value_block_exponent = place_ends(jax.random.randint(own_keys[5], (SEQUENCE_TOKENS // SCALE_POSITIONS, KEY_VALUE_HEADS), -2, 2), jax.random.fold_in(own_keys[5], 1), -2, 1).astype(jnp.int32)
    block_order = jax.random.permutation(splits[6], N_CTX).astype(jnp.int32)
    out_weight = noise(splits[7], (QUERY_HEADS * HEAD_SIZE, D), (QUERY_HEADS * HEAD_SIZE) ** -0.5, 0.09375, ((0, 8), (1, 16)))
    norm_gain = jnp.clip(1.0 + 0.18 * jax.random.normal(splits[8], (D,), jnp.float32), 0.1, 1.9)
    expert_ids_keys = jax.random.split(jax.random.fold_in(own_keys[9], 1), SEQUENCE_TOKENS // TOK_DEV)
    expert_ids_turns = jax.random.permutation(jax.random.fold_in(own_keys[9], 3), SEQUENCE_TOKENS // TOK_DEV)
    expert_ids = jax.vmap(lambda own, number: deal_out(jax.random.fold_in(own_keys[9], 2), own, number, TOK_DEV, EXP, TOP, CAP, 2))(expert_ids_keys, expert_ids_turns).reshape((SEQUENCE_TOKENS, TOP))
    route_weight = jnp.clip(0.05 + 0.2 * jax.random.uniform(own_keys[10], (SEQUENCE_TOKENS, TOP), jnp.float32) ** levels(own_keys[10], (SEQUENCE_TOKENS, TOP), ((0, 128),), -0.2, 0.2), 0.05, 0.25)
    gate_weight = noise(splits[11], (2 * EXP, D, FF // 2), D ** -0.5, 0.09375, ((0, 128),))
    gate_scale = place_ends(jax.random.randint(splits[12], (2 * EXP, D // WB, FF // 2 // WB), -1, 2), jax.random.fold_in(splits[12], 1), -1, 1).astype(jnp.int32)
    up_weight = noise(splits[13], (2 * EXP, D, FF // 2), D ** -0.5, 0.09375, ((0, 128),))
    up_scale = place_ends(jax.random.randint(splits[14], (2 * EXP, D // WB, FF // 2 // WB), -1, 2), jax.random.fold_in(splits[14], 1), -1, 1).astype(jnp.int32)
    down_weight = noise(splits[15], (2 * EXP, FF // 2, D), FF ** -0.5, 0.21875, ((0, 128),))
    down_scale = place_ends(jax.random.randint(splits[16], (2 * EXP, FF // 2 // WB, D // WB), -1, 2), jax.random.fold_in(splits[16], 1), -1, 1).astype(jnp.int32)
    return dict(residual=residual, encoded_query_rows=encoded_query_rows, quantized_key_rows=quantized_key_rows, quantized_value_rows=quantized_value_rows, key_block_exponent=key_block_exponent, value_block_exponent=value_block_exponent, block_order=block_order, out_weight=out_weight, norm_gain=norm_gain, expert_ids=expert_ids, route_weight=route_weight, gate_weight=gate_weight, gate_scale=gate_scale, up_weight=up_weight, up_scale=up_scale, down_weight=down_weight, down_scale=down_scale)


def pow_two(exponent, lowest, highest):
    result_sum = jnp.zeros(exponent.shape, jnp.float32)
    for power_of in range(lowest, highest + 1):
        result_sum = result_sum + jnp.where(exponent == power_of, 2.0 ** power_of, 0.0)
    return result_sum

def dequant(values, exponents, lowest, highest):
    row_blocks = exponents.shape[-2]
    col_blocks = exponents.shape[-1]
    row_rep = values.shape[-2] // row_blocks
    col_rep = values.shape[-1] // col_blocks
    factor = pow_two(exponents, lowest, highest).astype(jnp.bfloat16)
    shaped = values.reshape(values.shape[:-2] + (row_blocks, row_rep, col_blocks, col_rep))
    return (shaped * factor[..., :, None, :, None]).reshape(values.shape)

def reference(residual, encoded_query_rows, quantized_key_rows, quantized_value_rows, key_block_exponent, value_block_exponent, block_order, out_weight, norm_gain, expert_ids, route_weight, gate_weight, gate_scale, up_weight, up_scale, down_weight, down_scale):
    query_group_width = QUERY_HEADS // KEY_VALUE_HEADS
    row_ids = jnp.arange(SEQUENCE_TOKENS, dtype=jnp.int32)
    places = block_order[row_ids // CONTEXT_SPAN] * CONTEXT_SPAN + row_ids % CONTEXT_SPAN
    key_multiplier = jnp.repeat(pow_two(key_block_exponent, -2, 1), SCALE_POSITIONS, axis=0)
    value_multiplier = jnp.repeat(pow_two(value_block_exponent, -2, 1), SCALE_POSITIONS, axis=0)
    key_restored = (quantized_key_rows.astype(jnp.float32).reshape(SEQUENCE_TOKENS, KEY_VALUE_HEADS, HEAD_SIZE) * key_multiplier[:, :, None]).astype(jnp.bfloat16)
    value_restored = (quantized_value_rows.astype(jnp.float32).reshape(SEQUENCE_TOKENS, KEY_VALUE_HEADS, HEAD_SIZE) * value_multiplier[:, :, None]).astype(jnp.bfloat16)
    key_float = key_restored.astype(jnp.float32)
    value_float = value_restored.astype(jnp.float32)
    query_tiles = encoded_query_rows.reshape(N_CTX, CONTEXT_SPAN, KEY_VALUE_HEADS, query_group_width, HEAD_SIZE)
    query_places = places.reshape(N_CTX, CONTEXT_SPAN)
    inv_scale = 1.0 / math.sqrt(HEAD_SIZE)

    def attend_block(inputs):
        query_block, query_place = inputs
        scores = jnp.einsum('qgjd,kgd->gjqk', query_block.astype(jnp.float32), key_float) * inv_scale
        visible_mask = places[None, None, None, :] <= query_place[None, None, :, None]
        scores = jnp.where(visible_mask, scores, -1e+30)
        row_max = lax.optimization_barrier(jnp.max(scores, axis=-1, keepdims=True))
        exp_vals = jnp.where(visible_mask, jnp.exp(scores - row_max), 0.0)
        row_sum = lax.optimization_barrier(jnp.sum(exp_vals, axis=-1))
        rounded = lax.optimization_barrier(exp_vals.astype(jnp.bfloat16)).astype(jnp.float32)
        head_mix = jnp.einsum('gjqk,kgd->qgjd', rounded, value_float)
        return (head_mix / jnp.transpose(row_sum, (2, 0, 1))[:, :, :, None]).astype(jnp.bfloat16)
    attended = lax.map(attend_block, (query_tiles, query_places)).reshape(SEQUENCE_TOKENS, QUERY_HEADS * HEAD_SIZE)
    state = residual.astype(jnp.float32) + jnp.dot(attended, out_weight, preferred_element_type=jnp.float32)
    mean_sq = lax.optimization_barrier(jnp.mean(state * state, axis=-1, keepdims=True))
    normed = (state * lax.rsqrt(mean_sq + 1e-06) * norm_gain).astype(jnp.bfloat16)
    source_count = SEQUENCE_TOKENS // TOK_DEV
    copies = TOK_DEV * TOP
    grouped_ids = expert_ids.reshape(source_count, copies)
    onehot = (grouped_ids[:, :, None] == jnp.arange(EXP, dtype=jnp.int32)[None, None, :]).astype(jnp.int32)
    before = jnp.cumsum(onehot, axis=1) - onehot
    slot_ids = lax.optimization_barrier(jnp.sum(before * onehot, axis=2))
    source = jnp.arange(source_count, dtype=jnp.int32)[:, None]
    token_ids = source * TOK_DEV + jnp.arange(copies, dtype=jnp.int32)[None, :] // TOP
    target = (grouped_ids * (source_count * CAP) + source * CAP + slot_ids).reshape(-1)
    slot_table = jnp.full((EXP * source_count * CAP,), SEQUENCE_TOKENS, jnp.int32).at[target].set(token_ids.reshape(-1)).reshape(EXP, source_count * CAP)
    slot_probs = jnp.zeros((EXP * source_count * CAP,), jnp.float32).at[target].set(route_weight.reshape(-1)).reshape(EXP, source_count * CAP)
    padded = jnp.concatenate([normed, jnp.zeros((1, D), jnp.bfloat16)], axis=0)

    def expert_step(accumulated, inputs):
        number, row_index, weight_row = inputs
        first = (2 * number).astype(jnp.int32)
        gate_pair = dequant(lax.dynamic_slice_in_dim(gate_weight, first, 2, 0), lax.dynamic_slice_in_dim(gate_scale, first, 2, 0), -1, 1)
        up_pair = dequant(lax.dynamic_slice_in_dim(up_weight, first, 2, 0), lax.dynamic_slice_in_dim(up_scale, first, 2, 0), -1, 1)
        down_pair = dequant(lax.dynamic_slice_in_dim(down_weight, first, 2, 0), lax.dynamic_slice_in_dim(down_scale, first, 2, 0), -1, 1)
        gate_full = jnp.concatenate([gate_pair[0], gate_pair[1]], axis=1)
        up_full = jnp.concatenate([up_pair[0], up_pair[1]], axis=1)
        down_full = jnp.concatenate([down_pair[0], down_pair[1]], axis=0)
        row_vals = padded[row_index]
        gate_act = jnp.dot(row_vals, gate_full, preferred_element_type=jnp.float32)
        up_act = jnp.dot(row_vals, up_full, preferred_element_type=jnp.float32)
        hidden = (jax.nn.silu(gate_act) * up_act).astype(jnp.bfloat16)
        expert_out = jnp.dot(hidden, down_full, preferred_element_type=jnp.float32).astype(jnp.bfloat16)
        accumulated = accumulated.at[row_index].add(weight_row[:, None] * expert_out.astype(jnp.float32))
        return (accumulated, None)
    numbers = jnp.arange(EXP, dtype=jnp.int32)
    accumulated, unused = lax.scan(expert_step, jnp.zeros((SEQUENCE_TOKENS + 1, D), jnp.float32), (numbers, slot_table, slot_probs))
    return (state + accumulated[:SEQUENCE_TOKENS]).astype(jnp.bfloat16)
```

```python
import math

import jax
import jax.numpy as jnp
from jax import lax
from jax.experimental import pallas as pl
from jax.experimental.pallas import tpu as pltpu
from jax.sharding import PartitionSpec as P

QUERY_HEADS = 32
KEY_VALUE_HEADS = 4
HEAD_SIZE = 128
TOP = 8
SCALE_POSITIONS = 64


def from_partner(array, axis, bit):
    return lax.ppermute(array, axis, [(i, i ^ 1 << bit) for i in range(lax.axis_size(axis))])


def pow_two(exponent, lowest, highest):
    result_sum = jnp.zeros(exponent.shape, jnp.float32)
    for power_of in range(lowest, highest + 1):
        result_sum = result_sum + jnp.where(exponent == power_of, 2.0**power_of, 0.0)
    return result_sum


MESH = pl.DeviceIdType.MESH
F32 = jnp.float32
BF16 = jnp.bfloat16
NQ = 2


def contract_first(lhs, rhs):
    return lax.dot_general(lhs, rhs, (((0,), (0,)), ((), ())), preferred_element_type=F32)


def remote(src, dst, send_sem, recv_sem, device):
    return pltpu.make_async_remote_copy(
        src_ref=src,
        dst_ref=dst,
        send_sem=send_sem,
        recv_sem=recv_sem,
        device_id=device,
        device_id_type=MESH,
    )


class Place:
    def __init__(self):
        self.ctx = lax.axis_index("ctx")
        self.exp = lax.axis_index("exp")
        self.dp = lax.axis_index("dp")
        self.z = self.ctx % 8
        self.yh = self.ctx // 8
        self.x = self.exp // 2
        self.k = self.exp % 2
        self.plane = self.yh * 4 + self.x

    def at_z(self, dz, dk=0):
        z = (self.z + dz) % 8
        k = (self.k + dk) % 2
        return {"ctx": self.yh * 8 + z, "exp": self.x * 2 + k, "dp": self.dp}

    def at_plane(self, dx, dy):
        x = (self.x + dx) % 4
        yh = (self.yh + dy) % 2
        dp = (self.dp + dy) % 2
        return {"ctx": yh * 8 + self.z, "exp": x * 2 + self.k, "dp": dp}, yh * 4 + x

    def plane_from(self, dx, dy):
        return ((self.yh + 2 - dy) % 2) * 4 + (self.x + 4 - dx) % 4

    def other_core(self):
        return {"ctx": self.ctx, "exp": self.x * 2 + (1 - self.k), "dp": self.dp}


PLANE = [(dx, dy) for dy in range(2) for dx in range(4)]


def moe_kernel(
    x_ref,
    st_ref,
    meta_ref,
    gw_ref,
    uw_ref,
    dw_ref,
    gs_ref,
    us_ref,
    ds_ref,
    out_ref,
    meta_in,
    xg,
    ys,
    yr,
    xo,
    raw_g,
    raw_u,
    raw_d,
    deq_g,
    deq_u,
    deq_d,
    down_in,
    hid,
    hid_in,
    os_,
    orr,
    comb,
    sr,
    rr,
    sl,
    rl,
    fin,
    fin_in,
    w_sem,
    meta_s,
    meta_r,
    zr_s,
    zr_r,
    zl_s,
    zl_r,
    pd_s,
    pd_r,
    fw_s,
    fw_r,
    one_s,
    one_r,
    ps_s,
    ps_r,
    br_s,
    br_r,
    bl_s,
    bl_r,
    fn_s,
    fn_r,
):
    me = Place()
    z, k = me.z, me.k
    ch = xg.shape[-1]
    partner = me.other_core()
    right, left = me.at_z(1), me.at_z(7)
    sends = []

    loads = [
        pltpu.make_async_copy(src, dst, w_sem.at[i])
        for i, (src, dst) in enumerate(((gw_ref, raw_g), (uw_ref, raw_u), (dw_ref, raw_d)))
    ]
    for load in loads:
        load.start()

    barrier = pltpu.get_barrier_semaphore()
    for i in range(1, 16):
        pl.semaphore_signal(barrier, inc=1, device_id=me.at_z(i // 2, i % 2), device_id_type=MESH)
    for dx, dy in PLANE[1:]:
        pl.semaphore_signal(barrier, inc=1, device_id=me.at_plane(dx, dy)[0], device_id_type=MESH)
    pl.semaphore_wait(barrier, 22)

    def start(copy):
        copy.start()
        sends.append(copy)

    for q in range(NQ):
        xg[q, z] = x_ref[:, q * ch : (q + 1) * ch]

    def ring(q, step, rightward):
        block = (z + 8 - step) % 8 if rightward else (z + step) % 8
        s_sem, r_sem = (zr_s, zr_r) if rightward else (zl_s, zl_r)
        there = right if rightward else left
        return remote(xg.at[q, block], xg.at[q, block], s_sem.at[q, step], r_sem.at[q, step], there)

    def ring_wait(q, step, rightward):
        block = (z + 7 - step) % 8 if rightward else (z + 1 + step) % 8
        s_sem, r_sem = (zr_s, zr_r) if rightward else (zl_s, zl_r)
        there = right if rightward else left
        remote(
            xg.at[q, block], xg.at[q, block], s_sem.at[q, step], r_sem.at[q, step], there
        ).wait_recv()

    for q in range(NQ):
        start(ring(q, 0, True))
        start(ring(q, 0, False))
    for i in range(1, 16):
        dz, dk = i // 2, i % 2
        start(
            remote(
                meta_ref.at[(z + dz) % 8],
                meta_in.at[i],
                meta_s.at[i],
                meta_r.at[i],
                me.at_z(dz, dk),
            )
        )
    meta_in[0] = meta_ref[z]

    def scaled(raw, scale, deq):
        def body(c, carry):
            for half in range(2):
                side = k if half == 0 else 1 - k
                row = pl.multiple_of(c * 256 + side * 128, 128)
                factor = scale[pl.ds(c * 2 + side, 1), :]
                block = raw[pl.ds(row, 128), :].astype(F32) * factor
                deq[half, pl.ds(pl.multiple_of(c * 128, 128), 128), :] = block.astype(BF16)
            return carry

        lax.fori_loop(0, 16, body, 0)

    def scaled_down():
        def body(c, carry):
            for half in range(2):
                side = k if half == 0 else 1 - k
                col = pl.multiple_of(c * 256 + side * 128, 128)
                to = pl.multiple_of(c * 128, 128)
                for b in range(3):
                    factor = ds_ref[b : b + 1, pl.ds(col, 128)]
                    block = raw_d[b * 128 : (b + 1) * 128, pl.ds(col, 128)].astype(F32) * factor
                    deq_d[half, b * 128 : (b + 1) * 128, pl.ds(to, 128)] = block.astype(BF16)
            return carry

        lax.fori_loop(0, 16, body, 0)

    for step in range(1, 4):
        loads[step - 1].wait()
        if step == 1:
            scaled(raw_g, gs_ref, deq_g)
        elif step == 2:
            scaled(raw_u, us_ref, deq_u)
        else:
            scaled_down()
            start(remote(deq_d.at[1], down_in, one_s.at[0], one_r.at[0], partner))
        for q in range(NQ):
            ring_wait(q, step - 1, True)
            start(ring(q, step, True))
            if step < 3:
                ring_wait(q, step - 1, False)
                start(ring(q, step, False))

    for i in range(1, 16):
        remote(
            meta_ref.at[z], meta_in.at[i], meta_s.at[i], meta_r.at[i], partner
        ).wait_recv()
    slots = meta_in[0]
    for i in range(1, 16):
        slots = slots + meta_in[i]
    tokens = lax.broadcasted_iota(jnp.int32, (256, 384), 0).astype(F32) + 1.0
    chosen = tokens == slots[0:1, :]
    select = jnp.where(chosen, 1.0, 0.0).astype(BF16)
    weights = jnp.where(chosen, slots[1:2, :], 0.0)
    weights_hi = weights.astype(BF16)
    weights_lo = (weights - weights_hi.astype(F32)).astype(BF16)

    def to_plane(bufs, bufr, s_sem, r_sem, q, d):
        device, there = me.at_plane(*PLANE[d])
        return remote(
            bufs.at[q, there], bufr.at[q, me.plane], s_sem.at[q, d], r_sem.at[q, d], device
        )

    def from_plane(bufr, s_sem, r_sem, q, d):
        came = me.plane_from(*PLANE[d])
        remote(
            bufr.at[q, came], bufr.at[q, came], s_sem.at[q, d], r_sem.at[q, d], partner
        ).wait_recv()
        return came

    for q in range(NQ):
        ring_wait(q, 3, True)
        ring_wait(q, 2, False)
        picked = contract_first(select, xg[q].reshape(256, ch)).astype(BF16)
        ys[q] = picked.reshape(8, 48, ch)
        for d in range(1, 8):
            start(to_plane(ys, yr, pd_s, pd_r, q, d))
        yr[q, me.plane] = ys[q, me.plane]
        start(
            remote(
                yr.at[q, me.plane], xo.at[q, me.plane], fw_s.at[q, 0], fw_r.at[q, 0], partner
            )
        )

    gate = jnp.zeros((384, 384), F32)
    up = jnp.zeros((384, 384), F32)
    for q in range(NQ):
        for d in range(1, 8):
            came = from_plane(yr, pd_s, pd_r, q, d)
            start(remote(yr.at[q, came], xo.at[q, came], fw_s.at[q, d], fw_r.at[q, d], partner))
        for d in range(8):
            came = me.plane_from(*PLANE[d])
            remote(
                yr.at[q, came], xo.at[q, came], fw_s.at[q, d], fw_r.at[q, d], partner
            ).wait_recv()
        for half, rows in ((0, yr), (1, xo)):
            block = rows[q].reshape(384, ch)
            gate = gate + jnp.dot(
                block, deq_g[half, q * ch : (q + 1) * ch, :], preferred_element_type=F32
            )
            up = up + jnp.dot(
                block, deq_u[half, q * ch : (q + 1) * ch, :], preferred_element_type=F32
            )
    hid[...] = (gate / (1.0 + jnp.exp(-gate)) * up).astype(BF16)
    swap = remote(hid, hid_in, one_s.at[1], one_r.at[1], partner)
    start(swap)
    remote(deq_d.at[1], down_in, one_s.at[0], one_r.at[0], partner).wait_recv()
    swap.wait_recv()

    for q in range(NQ):
        cols = slice(q * ch, (q + 1) * ch)
        result = jnp.dot(hid[...], deq_d[0, :, cols], preferred_element_type=F32)
        result = result + jnp.dot(hid_in[...], down_in[:, cols], preferred_element_type=F32)
        os_[q] = result.astype(BF16).reshape(8, 48, ch)
        for d in range(1, 8):
            start(to_plane(os_, orr, ps_s, ps_r, q, d))
        orr[q, me.plane] = os_[q, me.plane]

    def back(q, step, rightward):
        if rightward:
            return remote(sr.at[q, step], rr.at[q, step], br_s.at[q, step], br_r.at[q, step], right)
        return remote(sl.at[q, step], rl.at[q, step], bl_s.at[q, step], bl_r.at[q, step], left)

    for q in range(NQ):
        for d in range(1, 8):
            from_plane(orr, ps_s, ps_r, q, d)
        rows = orr[q].reshape(384, ch)
        total = jnp.dot(weights_hi, rows, preferred_element_type=F32)
        total = total + jnp.dot(weights_lo, rows, preferred_element_type=F32)
        comb[q] = total.reshape(8, 32, ch)
        sr[q, 0] = comb[q, (z + 4) % 8].astype(BF16)
        start(back(q, 0, True))
        sl[q, 0] = comb[q, (z + 5) % 8].astype(BF16)
        start(back(q, 0, False))
    for step in range(1, 4):
        for q in range(NQ):
            back(q, step - 1, True).wait_recv()
            sr[q, step] = (rr[q, step - 1].astype(F32) + comb[q, (z + 4 - step) % 8]).astype(BF16)
            start(back(q, step, True))
            if step < 3:
                back(q, step - 1, False).wait_recv()
                sl[q, step] = (
                    rl[q, step - 1].astype(F32) + comb[q, (z + 5 + step) % 8]
                ).astype(BF16)
                start(back(q, step, False))
    for q in range(NQ):
        back(q, 3, True).wait_recv()
        back(q, 2, False).wait_recv()
        total = comb[q, z] + rr[q, 3].astype(F32) + rl[q, 2].astype(F32)
        total = total + st_ref[:, q * ch : (q + 1) * ch]
        fin[q] = total.astype(BF16).reshape(2, 16, ch)
        start(remote(fin.at[q, 1 - k], fin_in.at[q], fn_s.at[q], fn_r.at[q], partner))
    for q in range(NQ):
        remote(fin.at[q, 1 - k], fin_in.at[q], fn_s.at[q], fn_r.at[q], partner).wait_recv()
        own, got = fin[q, k], fin_in[q]
        for c in range(ch // 128):
            at = (q * (ch // 128) + c) * 256
            piece = slice(c * 128, (c + 1) * 128)
            out_ref[:, pl.ds(pl.multiple_of(at + k * 128, 128), 128)] = own[:, piece]
            out_ref[:, pl.ds(pl.multiple_of(at + (1 - k) * 128, 128), 128)] = got[:, piece]
    for copy in sends:
        copy.wait_send()


def moe(x, state, meta, gate_w, up_w, down_w, gate_s, up_s, down_s):
    width = x.shape[1]
    ch = width // NQ
    vmem = pl.BlockSpec(memory_space=pltpu.VMEM)
    hbm = pl.BlockSpec(memory_space=pl.ANY)
    dma = pltpu.SemaphoreType.DMA
    return pl.pallas_call(
        moe_kernel,
        out_shape=jax.ShapeDtypeStruct((x.shape[0] // 2, 2 * width), BF16),
        in_specs=[vmem, vmem, vmem, hbm, hbm, hbm, vmem, vmem, vmem],
        out_specs=vmem,
        scratch_shapes=[
            pltpu.VMEM((16, 8, 384), F32),
            pltpu.VMEM((NQ, 8, 32, ch), BF16),
            pltpu.VMEM((NQ, 8, 48, ch), BF16),
            pltpu.VMEM((NQ, 8, 48, ch), BF16),
            pltpu.VMEM((NQ, 8, 48, ch), BF16),
            pltpu.VMEM(gate_w.shape, BF16),
            pltpu.VMEM(up_w.shape, BF16),
            pltpu.VMEM(down_w.shape, BF16),
            pltpu.VMEM((2, width, 384), BF16),
            pltpu.VMEM((2, width, 384), BF16),
            pltpu.VMEM((2, 384, width), BF16),
            pltpu.VMEM((384, width), BF16),
            pltpu.VMEM((384, 384), BF16),
            pltpu.VMEM((384, 384), BF16),
            pltpu.VMEM((NQ, 8, 48, ch), BF16),
            pltpu.VMEM((NQ, 8, 48, ch), BF16),
            pltpu.VMEM((NQ, 8, 32, ch), F32),
            pltpu.VMEM((NQ, 4, 32, ch), BF16),
            pltpu.VMEM((NQ, 4, 32, ch), BF16),
            pltpu.VMEM((NQ, 3, 32, ch), BF16),
            pltpu.VMEM((NQ, 3, 32, ch), BF16),
            pltpu.VMEM((NQ, 2, 16, ch), BF16),
            pltpu.VMEM((NQ, 16, ch), BF16),
            dma((3,)),
            dma((16,)),
            dma((16,)),
            dma((NQ, 4)),
            dma((NQ, 4)),
            dma((NQ, 3)),
            dma((NQ, 3)),
            dma((NQ, 8)),
            dma((NQ, 8)),
            dma((NQ, 8)),
            dma((NQ, 8)),
            dma((2,)),
            dma((2,)),
            dma((NQ, 8)),
            dma((NQ, 8)),
            dma((NQ, 4)),
            dma((NQ, 4)),
            dma((NQ, 3)),
            dma((NQ, 3)),
            dma((NQ,)),
            dma((NQ,)),
        ],
        compiler_params=pltpu.CompilerParams(
            collective_id=1, has_side_effects=True, vmem_limit_bytes=58 * 1024 * 1024
        ),
        name="experts",
    )(x, state, meta, gate_w, up_w, down_w, gate_s, up_s, down_s)


def routing(expert_ids, route_weight, my_ctx, my_exp):
    z, k = my_ctx % 8, my_exp % 2
    rows = expert_ids.shape[0]
    named = expert_ids[:, :, None] == jnp.arange(64, dtype=jnp.int32)[None, None, :]
    member = jnp.sum(named.astype(F32), axis=1)
    weight = jnp.sum(jnp.where(named, route_weight[:, :, None], 0.0), axis=1)
    earlier = jnp.arange(rows)[:, None] > jnp.arange(rows)[None, :]
    slot = jnp.sum(jnp.where(earlier[:, :, None], member[None], 0.0), axis=1)
    number = (z * 32 + k * 16 + 1 + jnp.arange(rows, dtype=jnp.int32)).astype(F32)
    at = (slot[:, :, None] == jnp.arange(3).astype(F32)) & (member[:, :, None] > 0.5)
    token = jnp.sum(jnp.where(at, number[:, None, None], 0.0), axis=0)
    gain = jnp.sum(jnp.where(at, weight[:, :, None], 0.0), axis=0)
    both = jnp.stack([token, gain], axis=0).reshape(2, 2, 8, 4, 3)
    both = both.transpose(2, 0, 1, 3, 4).reshape(8, 2, 8, 1, 1, 3)
    here = (jnp.arange(8) == z)[:, None, None] & (jnp.arange(2) == k)[None, :, None]
    spread = jnp.where(here[None, None, None], both, 0.0).reshape(8, 2, 384)
    return jnp.concatenate([spread, jnp.zeros((8, 6, 384), F32)], axis=1)


def shards(
    residual,
    encoded_query_rows,
    quantized_key_rows,
    quantized_value_rows,
    key_block_exponent,
    value_block_exponent,
    block_order,
    out_weight,
    norm_gain,
    expert_ids,
    route_weight,
    gate_weight,
    gate_scale,
    up_weight,
    up_scale,
    down_weight,
    down_scale,
):
    span_rows = encoded_query_rows.shape[0]
    head_count = encoded_query_rows.shape[1] // HEAD_SIZE
    query_group_width = QUERY_HEADS // KEY_VALUE_HEADS
    ctx_count = lax.axis_size("ctx")
    exp_count = lax.axis_size("exp")
    tok_count = residual.shape[0]
    model_width = residual.shape[1]
    half_width = model_width // 2
    my_ctx = lax.axis_index("ctx")
    my_exp = lax.axis_index("exp")
    kv_head = my_exp * head_count // query_group_width
    ctx_ids = jnp.arange(ctx_count, dtype=jnp.int32)

    def place_of(block_ids):
        return jnp.sum(
            jnp.where(block_ids[:, None] == ctx_ids[None, :], block_order[None, :], 0), axis=1
        )

    own_place = place_of(jnp.reshape(my_ctx, (1,)))[0]
    query_place = own_place * span_rows + jnp.arange(span_rows, dtype=jnp.int32)

    def head_rows(row_vals, scales):
        picked = lax.dynamic_slice_in_dim(row_vals, kv_head * HEAD_SIZE, HEAD_SIZE, 1)
        factor = lax.dynamic_slice_in_dim(scales, kv_head, 1, 1)
        factor = jnp.repeat(pow_two(factor, -2, 1), SCALE_POSITIONS, axis=0)
        return (picked.astype(jnp.float32) * factor).astype(jnp.bfloat16)

    key_head = head_rows(quantized_key_rows, key_block_exponent)
    value_head = head_rows(quantized_value_rows, value_block_exponent)
    queries = encoded_query_rows.reshape(span_rows, head_count, HEAD_SIZE)
    inv_scale = 1.0 / math.sqrt(HEAD_SIZE)
    initial = (
        jnp.full((head_count, span_rows), -1e30, jnp.float32),
        jnp.zeros((head_count, span_rows), jnp.float32),
        jnp.zeros((span_rows, head_count, HEAD_SIZE), jnp.float32),
    )
    key_piece = lax.all_gather(key_head, "ctx", axis=0, tiled=True)
    value_piece = lax.all_gather(value_head, "ctx", axis=0, tiled=True)
    piece_len = key_piece.shape[0]
    row_ids = jnp.arange(piece_len, dtype=jnp.int32)
    key_place = place_of(row_ids // span_rows) * span_rows + row_ids % span_rows
    seen = jnp.min(key_place) <= jnp.max(query_place)

    def update(state_in):
        run_max, run_sum, run_acc = state_in
        scores = (
            jnp.einsum("qhd,kd->hqk", queries, key_piece, preferred_element_type=jnp.float32)
            * inv_scale
        )
        visible_mask = key_place[None, None, :] <= query_place[None, :, None]
        scores = jnp.where(visible_mask, scores, -1e30)
        new_max = jnp.maximum(run_max, jnp.max(scores, axis=-1))
        weights = jnp.where(visible_mask, jnp.exp(scores - new_max[:, :, None]), 0.0)
        factor = jnp.exp(run_max - new_max)
        run_sum = jnp.sum(weights, axis=-1)
        added = jnp.einsum(
            "hqk,kd->qhd",
            weights.astype(jnp.bfloat16),
            value_piece,
            preferred_element_type=jnp.float32,
        )
        run_acc = added
        return (new_max, run_sum, run_acc)

    def unchanged(state_in):
        return state_in

    run_max, run_sum, run_acc = lax.cond(seen, update, unchanged, initial)
    attended = (
        (run_acc / jnp.transpose(run_sum)[:, :, None])
        .astype(jnp.bfloat16)
        .reshape(span_rows, head_count * HEAD_SIZE)
    )
    partial_rows = jnp.dot(
        attended,
        lax.all_gather(out_weight, "ctx", axis=1, tiled=True),
        preferred_element_type=jnp.float32,
    )
    mixed = lax.psum_scatter(
        partial_rows.astype(jnp.bfloat16), "exp", scatter_dimension=0, tiled=True
    ).astype(jnp.float32)
    state_rows = residual.astype(jnp.float32) + mixed
    mean_sq = jnp.mean(state_rows * state_rows, axis=-1, keepdims=True)
    normed = (state_rows * lax.rsqrt(mean_sq + 1e-06) * norm_gain).astype(jnp.bfloat16)
    k = my_exp % 2

    def own_half(rows):
        tiles = rows.reshape(tok_count, 16, 2, 128)
        kept = lax.dynamic_index_in_dim(tiles, k, 2, False).reshape(tok_count, half_width)
        given = lax.dynamic_index_in_dim(tiles, 1 - k, 2, False).reshape(tok_count, half_width)
        came = from_partner(given, "exp", 0)
        return jnp.where(k == 0, jnp.concatenate([kept, came]), jnp.concatenate([came, kept]))

    def expanded(scale):
        return jnp.repeat(pow_two(scale, -1, 1), 128, axis=1)

    return moe(
        own_half(normed),
        own_half(state_rows),
        routing(expert_ids, route_weight, my_ctx, my_exp),
        gate_weight[0],
        up_weight[0],
        down_weight[0],
        expanded(gate_scale[0]),
        expanded(up_scale[0]),
        expanded(down_scale[0]),
    )


def solution(mesh):
    return jax.shard_map(
        shards,
        mesh=mesh,
        in_specs=(
            P(("dp", "ctx", "exp"), None),
            P(("dp", "ctx"), "exp"),
            P(("dp", "ctx"), None),
            P(("dp", "ctx"), None),
            P(("dp", "ctx"), None),
            P(("dp", "ctx"), None),
            P(),
            P("exp", "ctx"),
            P(),
            P(("dp", "ctx", "exp"), None),
            P(("dp", "ctx", "exp"), None),
            P(("ctx", "exp"), None, None),
            P(("ctx", "exp"), None, None),
            P(("ctx", "exp"), None, None),
            P(("ctx", "exp"), None, None),
            P(("ctx", "exp"), None, None),
            P(("ctx", "exp"), None, None),
        ),
        out_specs=P(("dp", "ctx", "exp"), None),
        check_vma=False,
    )
```

```python
import math

import jax
import jax.numpy as jnp
from jax import lax
from jax.experimental import pallas as pl
from jax.experimental.pallas import tpu as pltpu
from jax.sharding import PartitionSpec as P

HEAD_SIZE = 128

MESH = pl.DeviceIdType.MESH
F32 = jnp.float32
BF16 = jnp.bfloat16
NQ = 2
OFFSETS = (0, 1, 7, 2, 6, 3, 5, 4)
GROUPS = ((0, 1), (1, 3), (3, 5), (5, 8))
PLANE = [(dx, dy) for dy in range(2) for dx in range(4)]


def contract_first(lhs, rhs):
    return lax.dot_general(lhs, rhs, (((0,), (0,)), ((), ())), preferred_element_type=F32)


def contract_last(lhs, rhs):
    return lax.dot_general(lhs, rhs, (((1,), (1,)), ((), ())), preferred_element_type=F32)


def mul(lhs, rhs):
    return jnp.dot(lhs, rhs, preferred_element_type=F32)


def remote(src, dst, send_sem, recv_sem, device):
    return pltpu.make_async_remote_copy(
        src_ref=src,
        dst_ref=dst,
        send_sem=send_sem,
        recv_sem=recv_sem,
        device_id=device,
        device_id_type=MESH,
    )


def hops(q):
    return (4, 3) if q % 2 == 0 else (3, 4)


class Place:
    def __init__(self):
        self.ctx = lax.axis_index("ctx")
        self.exp = lax.axis_index("exp")
        self.dp = lax.axis_index("dp")
        self.z = self.ctx % 8
        self.yh = self.ctx // 8
        self.x = self.exp // 2
        self.k = self.exp % 2
        self.plane = self.yh * 4 + self.x

    def at_ctx(self, i):
        return {"ctx": (self.ctx + i) % 16, "exp": self.exp, "dp": self.dp}

    def at_z(self, dz, dk=0):
        z = (self.z + dz) % 8
        k = (self.k + dk) % 2
        return {"ctx": self.yh * 8 + z, "exp": self.x * 2 + k, "dp": self.dp}

    def at_plane(self, dx, dy):
        x = (self.x + dx) % 4
        yh = (self.yh + dy) % 2
        dp = (self.dp + dy) % 2
        return {"ctx": yh * 8 + self.z, "exp": x * 2 + self.k, "dp": dp}, yh * 4 + x

    def plane_from(self, dx, dy):
        return ((self.yh + 2 - dy) % 2) * 4 + (self.x + 4 - dx) % 4

    def other_core(self):
        return {"ctx": self.ctx, "exp": self.x * 2 + (1 - self.k), "dp": self.dp}


def layer_kernel(
    q_ref,
    kq_ref,
    vq_ref,
    ke_ref,
    ve_ref,
    order_ref,
    w_ref,
    res_ref,
    gain_ref,
    meta_ref,
    gw_ref,
    uw_ref,
    dw_ref,
    gs_ref,
    us_ref,
    ds_ref,
    out_ref,
    *scratch_refs,
):
    r = dict(zip(SCRATCH, scratch_refs, strict=True))
    sem = {name[:-2]: (r[name], r[name[:-2] + "_r"]) for name in SCRATCH if name.endswith("_s")}
    me = Place()
    z, k, x, yh = me.z, me.k, me.x, me.yh
    partner = me.other_core()
    right, left = me.at_z(1), me.at_z(7)
    xg, st = r["xg"], r["st"]
    ch = xg.shape[-1]
    sends = []

    def start(copy):
        copy.start()
        sends.append(copy)

    def pair(name, *index):
        return sem[name][0].at[index], sem[name][1].at[index]

    loads = [
        pltpu.make_async_copy(src, r[dst], r["w_sem"].at[i])
        for i, (src, dst) in enumerate(((gw_ref, "raw_g"), (uw_ref, "raw_u"), (dw_ref, "raw_d")))
    ]
    for load in loads:
        load.start()

    barrier = pltpu.get_barrier_semaphore()
    peers = [me.at_ctx(i) for i in range(1, 16)] + [me.at_z(i, 1) for i in range(8)]
    peers = peers + [me.at_plane(dx, dy)[0] for dx, dy in PLANE[1:]]
    for peer in peers:
        pl.semaphore_signal(barrier, inc=1, device_id=peer, device_id_type=MESH)
    pl.semaphore_wait(barrier, len(peers))

    kv = r["kv"]
    row = lax.broadcasted_iota(jnp.int32, (128, 128), 0)
    col = lax.broadcasted_iota(jnp.int32, (128, 128), 1)
    head = pl.ds(pl.multiple_of(x * 128, 128), 128)
    first = jnp.where(k == 0, ke_ref[0, x], ve_ref[0, x])
    second = jnp.where(k == 0, ke_ref[1, x], ve_ref[1, x])
    power = jnp.where(row < 64, first, second)
    factor = jnp.zeros((128, 128), F32)
    for p in range(-2, 2):
        factor = factor + jnp.where(power == p, 2.0**p, 0.0)
    mine = jnp.where(k == 0, kq_ref[:, head].astype(F32), vq_ref[:, head].astype(F32))
    kv[k, me.ctx] = (mine * factor).astype(BF16)

    def kv_copy(i):
        return remote(kv.at[k, me.ctx], kv.at[k, me.ctx], *pair("kv", i), me.at_ctx(i))

    def kv_pass(i):
        src = (me.ctx + 16 - i) % 16
        return remote(kv.at[k, src], kv.at[k, src], *pair("kvp", i), partner)

    for i in range(1, 16):
        start(kv_copy(i))
    start(kv_pass(0))

    wb = r["wb"]
    wb[k, z] = w_ref[:, pl.ds(pl.multiple_of(k * 128, 128), 128)]
    give = w_ref.at[:, pl.ds(pl.multiple_of((1 - k) * 128, 128), 128)]

    def gather(buf, name, q, step, rightward):
        block = (z + 8 - step) % 8 if rightward else (z + step) % 8
        sems = pair(name + "r" if rightward else name + "l", q, step)
        return remote(buf(block), buf(block), *sems, right if rightward else left)

    def gathered(buf, name, q, step, rightward):
        block = (z + 7 - step) % 8 if rightward else (z + 1 + step) % 8
        sems = pair(name + "r" if rightward else name + "l", q, step)
        remote(buf(block), buf(block), *sems, right if rightward else left).wait_recv()

    def ring_start(buf, name, q):
        start(gather(buf, name, q, 0, True))
        start(gather(buf, name, q, 0, False))

    def ring_step(buf, name, q, step):
        rights, lefts = hops(q)
        for rightward, count in ((True, rights), (False, lefts)):
            if step < count:
                gathered(buf, name, q, step - 1, rightward)
                start(gather(buf, name, q, step, rightward))

    def ring_end(buf, name, q):
        rights, lefts = hops(q)
        gathered(buf, name, q, rights - 1, True)
        gathered(buf, name, q, lefts - 1, False)

    def w_block(q):
        core = k if q == 0 else 1 - k
        return lambda block: wb.at[core, block]

    start(remote(give, wb.at[k, z], *pair("one", 2), partner))
    ring_start(w_block(0), "w", 0)

    meta_in = r["meta_in"]
    for i in range(1, 16):
        dz, dk = i // 2, i % 2
        there = (z + dz) % 8
        start(remote(meta_ref.at[there], meta_in.at[i], *pair("meta", i), me.at_z(dz, dk)))
    meta_in[0] = meta_ref[z]

    res, res_give, gain = r["res"], r["res_give"], r["gain"]
    for c in range(16):
        to = slice(c * 128, (c + 1) * 128)
        own = pl.ds(pl.multiple_of(c * 256 + k * 128, 128), 128)
        other = pl.ds(pl.multiple_of(c * 256 + (1 - k) * 128, 128), 128)
        res[k, :, to] = res_ref[:, own]
        res_give[:, to] = res_ref[:, other]
        gain[:, to] = gain_ref[:, own]
    start(remote(res_give, res.at[k], *pair("one", 3), partner))

    def scaled(raw, scale, deq):
        def body(c, carry):
            for half in range(2):
                side = k if half == 0 else 1 - k
                at = pl.multiple_of(c * 256 + side * 128, 128)
                block = raw[pl.ds(at, 128), :].astype(F32) * scale[pl.ds(c * 2 + side, 1), :]
                deq[half, pl.ds(pl.multiple_of(c * 128, 128), 128), :] = block.astype(BF16)
            return carry

        lax.fori_loop(0, 16, body, 0)

    def scaled_down(raw, scale, deq):
        def body(c, carry):
            for half in range(2):
                side = k if half == 0 else 1 - k
                at = pl.ds(pl.multiple_of(c * 256 + side * 128, 128), 128)
                to = pl.ds(pl.multiple_of(c * 128, 128), 128)
                for b in range(3):
                    rows = slice(b * 128, (b + 1) * 128)
                    block = raw[rows, at].astype(F32) * scale[b : b + 1, at]
                    deq[half, rows, to] = block.astype(BF16)
            return carry

        lax.fori_loop(0, 16, body, 0)

    loads[0].wait()
    scaled(r["raw_g"], gs_ref, r["deq_g"])
    remote(give, wb.at[1 - k, z], *pair("one", 2), partner).wait_recv()
    ring_start(w_block(1), "w", 1)
    loads[1].wait()
    scaled(r["raw_u"], us_ref, r["deq_u"])
    loads[2].wait()
    scaled_down(r["raw_d"], ds_ref, r["deq_d"])
    start(remote(r["deq_d"].at[1], r["down_in"], *pair("one", 0), partner))

    bias = r["bias"]
    own_place = order_ref[me.ctx]
    for j in range(16):
        seen = order_ref[j] * 128 + col <= own_place * 128 + row
        bias[:, j * 128 : (j + 1) * 128] = jnp.where(seen, 0.0, -1e30)

    for i in range(1, 16):
        kv_copy(i).wait_recv()
        start(kv_pass(i))
        if i == 8:
            for q in range(2):
                ring_step(w_block(q), "w", q, 1)
    for i in range(16):
        src = (me.ctx + 16 - i) % 16
        remote(kv.at[1 - k, src], kv.at[1 - k, src], *pair("kvp", i), partner).wait_recv()

    ab = r["ab"]
    keys, values = kv[0].reshape(2048, 128), kv[1].reshape(2048, 128)
    for h in range(4):
        to = slice(h * 128, (h + 1) * 128)
        scores = contract_last(q_ref[:, to], keys) * (1.0 / math.sqrt(HEAD_SIZE) * math.log2(math.e))
        scores = scores + bias[...]
        exps = jnp.exp2(scores - jnp.max(scores, axis=1, keepdims=True))
        total = jnp.sum(exps, axis=1, keepdims=True)
        ab[k, yh, :, to] = (mul(exps.astype(BF16), values) / total).astype(BF16)
        if h % 2 == 0:
            for q in range(2):
                ring_step(w_block(q), "w", q, 2 + h // 2)
    start(remote(ab.at[k, yh], ab.at[k, yh], *pair("a", 0), partner))
    over = me.at_plane(0, 1)[0]
    start(remote(ab.at[k, yh], ab.at[k, yh], *pair("a", 1), over))
    came = ab.at[k, 1 - yh]
    remote(came, came, *pair("a", 1), over).wait_recv()
    start(remote(came, came, *pair("a", 2), partner))
    for i, there in ((0, yh), (2, 1 - yh)):
        came = ab.at[1 - k, there]
        remote(came, came, *pair("a", i), partner).wait_recv()

    px, rx, tot, yo, yi = r["px"], r["rx"], r["tot"], r["yo"], r["yi"]
    attended = [ab[core].reshape(256, 512) for core in range(2)]

    def x_copy(g, dx):
        lo, hi = GROUPS[g]
        part = pl.ds(lo, hi - lo)
        return remote(
            px.at[(x + dx) % 4, part], rx.at[dx, part], *pair("x", g, dx), me.at_plane(dx, 0)[0]
        )

    def y_copy(g):
        lo, hi = GROUPS[g]
        part = pl.ds(lo, hi - lo)
        return remote(yo.at[part], yi.at[part], *pair("y", g), over)

    for g, (lo, hi) in enumerate(GROUPS):
        for q in range(2):
            if g == len(GROUPS) - 1:
                ring_end(w_block(q), "w", q)
        if 0 < g < len(GROUPS) - 1:
            pass
        for n in range(lo, hi):
            at = (z + OFFSETS[n]) % 8
            part = mul(attended[0], wb[0, at]) + mul(attended[1], wb[1, at])
            part = part.astype(BF16).reshape(2, 4, 32, 128)
            for to in range(4):
                px[to, n] = part[:, to]
        for dx in range(1, 4):
            start(x_copy(g, dx))

    def place_columns(n, side, values):
        at = pl.ds(pl.multiple_of((side * 8 + (z + OFFSETS[n]) % 8) * 128, 128), 128)
        st[:, at] = values

    for g, (lo, hi) in enumerate(GROUPS):
        for dx in range(1, 4):
            x_copy(g, dx).wait_recv()
        for n in range(lo, hi):
            total = px[x, n].astype(F32)
            for dx in range(1, 4):
                total = total + rx[dx, n].astype(F32)
            tot[n] = total
            yo[n] = tot[n, 1 - yh].astype(BF16)
            place_columns(n, yh, tot[n, yh])
        start(y_copy(g))
    remote(res_give, res.at[1 - k], *pair("one", 3), partner).wait_recv()
    for g, (lo, hi) in enumerate(GROUPS):
        y_copy(g).wait_recv()
        for n in range(lo, hi):
            place_columns(n, 1 - yh, yi[n].astype(F32))
    st[...] = st[...] + res[...].reshape(32, 2048).astype(F32)
    squares = jnp.sum(st[...] * st[...], axis=1, keepdims=True)
    r["sq"][0] = jnp.broadcast_to(squares, (32, 128))
    swap = remote(r["sq"].at[0], r["sq"].at[1], *pair("one", 4), partner)
    start(swap)
    swap.wait_recv()
    mean = (r["sq"][0, :, 0:1] + r["sq"][1, :, 0:1]) / 4096.0
    normed = (st[...] * lax.rsqrt(mean + 1e-6) * gain[...]).astype(BF16)

    def x_block(q):
        return lambda block: xg.at[q, block]

    for q in range(NQ):
        xg[q, z] = normed[:, q * ch : (q + 1) * ch]
        ring_start(x_block(q), "z", q)

    for i in range(1, 16):
        remote(meta_ref.at[z], meta_in.at[i], *pair("meta", i), partner).wait_recv()
    slots = meta_in[0]
    for i in range(1, 16):
        slots = slots + meta_in[i]
    tokens = lax.broadcasted_iota(jnp.int32, (256, 384), 0).astype(F32) + 1.0
    chosen = tokens == slots[0:1, :]
    select = jnp.where(chosen, 1.0, 0.0).astype(BF16)
    weights = jnp.where(chosen, slots[1:2, :], 0.0)
    weights_hi = weights.astype(BF16)
    weights_lo = (weights - weights_hi.astype(F32)).astype(BF16)

    for step in range(1, 4):
        for q in range(NQ):
            ring_step(x_block(q), "z", q, step)

    def to_plane(bufs, bufr, name, q, d):
        device, there = me.at_plane(*PLANE[d])
        return remote(bufs.at[q, there], bufr.at[q, me.plane], *pair(name, q, d), device)

    def from_plane(bufr, name, q, d):
        came = me.plane_from(*PLANE[d])
        remote(bufr.at[q, came], bufr.at[q, came], *pair(name, q, d), partner).wait_recv()
        return came

    ys, yr, xo = r["ys"], r["yr"], r["xo"]
    for q in range(NQ):
        ring_end(x_block(q), "z", q)
        picked = contract_first(select, xg[q].reshape(256, ch)).astype(BF16)
        ys[q] = picked.reshape(8, 48, ch)
        for d in range(1, 8):
            start(to_plane(ys, yr, "pd", q, d))
        yr[q, me.plane] = ys[q, me.plane]
        start(remote(yr.at[q, me.plane], xo.at[q, me.plane], *pair("fw", q, 0), partner))

    gate = jnp.zeros((384, 384), F32)
    up = jnp.zeros((384, 384), F32)
    for q in range(NQ):
        for d in range(1, 8):
            came = from_plane(yr, "pd", q, d)
            start(remote(yr.at[q, came], xo.at[q, came], *pair("fw", q, d), partner))
        for d in range(8):
            came = me.plane_from(*PLANE[d])
            remote(yr.at[q, came], xo.at[q, came], *pair("fw", q, d), partner).wait_recv()
        for half, rows in ((0, yr), (1, xo)):
            block = rows[q].reshape(384, ch)
            gate = gate + mul(block, r["deq_g"][half, q * ch : (q + 1) * ch, :])
            up = up + mul(block, r["deq_u"][half, q * ch : (q + 1) * ch, :])
    hid, hid_in = r["hid"], r["hid_in"]
    hid[...] = (gate / (1.0 + jnp.exp(-gate)) * up).astype(BF16)
    swap = remote(hid, hid_in, *pair("one", 1), partner)
    start(swap)
    remote(r["deq_d"].at[1], r["down_in"], *pair("one", 0), partner).wait_recv()
    swap.wait_recv()

    es, er = r["es"], r["er"]
    for q in range(NQ):
        cols = slice(q * ch, (q + 1) * ch)
        result = mul(hid[...], r["deq_d"][0, :, cols]) + mul(hid_in[...], r["down_in"][:, cols])
        es[q] = result.astype(BF16).reshape(8, 48, ch)
        for d in range(1, 8):
            start(to_plane(es, er, "ps", q, d))
        er[q, me.plane] = es[q, me.plane]

    comb = r["comb"]

    def back(q, step, rightward):
        side, there = ("br", right) if rightward else ("bl", left)
        return remote(
            r[side + "_out"].at[q, step], r[side + "_in"].at[q, step], *pair(side, q, step), there
        )

    def back_start(q, step, rightward):
        rights, lefts = hops(q)
        side = "br" if rightward else "bl"
        block = (z + rights - step) % 8 if rightward else (z + 8 - lefts + step) % 8
        part = comb[q, block]
        if step:
            back(q, step - 1, rightward).wait_recv()
            part = part + r[side + "_in"][q, step - 1].astype(F32)
        r[side + "_out"][q, step] = part.astype(BF16)
        start(back(q, step, rightward))

    for q in range(NQ):
        for d in range(1, 8):
            from_plane(er, "ps", q, d)
        rows = er[q].reshape(384, ch)
        comb[q] = (mul(weights_hi, rows) + mul(weights_lo, rows)).reshape(8, 32, ch)
        back_start(q, 0, True)
        back_start(q, 0, False)
    for step in range(1, 4):
        for q in range(NQ):
            for rightward, count in zip((True, False), hops(q)):
                if step < count:
                    back_start(q, step, rightward)
    fin, fin_in = r["fin"], r["fin_in"]
    for q in range(NQ):
        total = comb[q, z] + st[:, q * ch : (q + 1) * ch]
        for rightward, count in zip((True, False), hops(q)):
            back(q, count - 1, rightward).wait_recv()
            total = total + r["br_in" if rightward else "bl_in"][q, count - 1].astype(F32)
        fin[q] = total.astype(BF16).reshape(2, 16, ch)
        start(remote(fin.at[q, 1 - k], fin_in.at[q], *pair("fn", q), partner))
    for q in range(NQ):
        remote(fin.at[q, 1 - k], fin_in.at[q], *pair("fn", q), partner).wait_recv()
        own, got = fin[q, k], fin_in[q]
        for c in range(ch // 128):
            at = (q * (ch // 128) + c) * 256
            piece = slice(c * 128, (c + 1) * 128)
            out_ref[:, pl.ds(pl.multiple_of(at + k * 128, 128), 128)] = own[:, piece]
            out_ref[:, pl.ds(pl.multiple_of(at + (1 - k) * 128, 128), 128)] = got[:, piece]
    for copy in sends:
        copy.wait_send()


def scratch():
    ch = 2048 // NQ
    shapes = {
        "kv": ((2, 16, 128, 128), BF16),
        "wb": ((2, 8, 512, 128), BF16),
        "res": ((2, 16, 2048), BF16),
        "res_give": ((16, 2048), BF16),
        "gain": ((1, 2048), F32),
        "bias": ((128, 2048), F32),
        "ab": ((2, 2, 128, 512), BF16),
        "px": ((4, 8, 2, 32, 128), BF16),
        "rx": ((4, 8, 2, 32, 128), BF16),
        "tot": ((8, 2, 32, 128), F32),
        "yo": ((8, 32, 128), BF16),
        "yi": ((8, 32, 128), BF16),
        "st": ((32, 2048), F32),
        "sq": ((2, 32, 128), F32),
        "meta_in": ((16, 8, 384), F32),
        "xg": ((NQ, 8, 32, ch), BF16),
        "ys": ((NQ, 8, 48, ch), BF16),
        "yr": ((NQ, 8, 48, ch), BF16),
        "xo": ((NQ, 8, 48, ch), BF16),
        "raw_g": ((4096, 384), BF16),
        "raw_u": ((4096, 384), BF16),
        "raw_d": ((384, 4096), BF16),
        "deq_g": ((2, 2048, 384), BF16),
        "deq_u": ((2, 2048, 384), BF16),
        "deq_d": ((2, 384, 2048), BF16),
        "down_in": ((384, 2048), BF16),
        "hid": ((384, 384), BF16),
        "hid_in": ((384, 384), BF16),
        "es": ((NQ, 8, 48, ch), BF16),
        "er": ((NQ, 8, 48, ch), BF16),
        "comb": ((NQ, 8, 32, ch), F32),
        "br_out": ((NQ, 4, 32, ch), BF16),
        "br_in": ((NQ, 4, 32, ch), BF16),
        "bl_out": ((NQ, 4, 32, ch), BF16),
        "bl_in": ((NQ, 4, 32, ch), BF16),
        "fin": ((NQ, 2, 16, ch), BF16),
        "fin_in": ((NQ, 16, ch), BF16),
    }
    made = {name: pltpu.VMEM(*what) for name, what in shapes.items()}
    made["w_sem"] = pltpu.SemaphoreType.DMA((3,))
    copies = {
        "kv": (16,),
        "kvp": (16,),
        "one": (5,),
        "wr": (2, 4),
        "wl": (2, 4),
        "meta": (16,),
        "a": (3,),
        "x": (len(GROUPS), 4),
        "y": (len(GROUPS),),
        "zr": (NQ, 4),
        "zl": (NQ, 4),
        "pd": (NQ, 8),
        "fw": (NQ, 8),
        "ps": (NQ, 8),
        "br": (NQ, 4),
        "bl": (NQ, 4),
        "fn": (NQ,),
    }
    for name, shape in copies.items():
        made[name + "_s"] = pltpu.SemaphoreType.DMA(shape)
        made[name + "_r"] = pltpu.SemaphoreType.DMA(shape)
    return made


SCRATCH = tuple(scratch())


def layer(*operands):
    vmem = pl.BlockSpec(memory_space=pltpu.VMEM)
    smem = pl.BlockSpec(memory_space=pltpu.SMEM)
    hbm = pl.BlockSpec(memory_space=pl.ANY)
    return pl.pallas_call(
        layer_kernel,
        out_shape=jax.ShapeDtypeStruct((16, 4096), BF16),
        in_specs=[vmem] * 3 + [smem] * 3 + [vmem] * 4 + [hbm] * 3 + [vmem] * 3,
        out_specs=vmem,
        scratch_shapes=list(scratch().values()),
        compiler_params=pltpu.CompilerParams(
            collective_id=1, has_side_effects=True, vmem_limit_bytes=58 * 1024 * 1024
        ),
        name="layer",
    )(*operands)


def pow_two(exponent, lowest, highest):
    result_sum = jnp.zeros(exponent.shape, jnp.float32)
    for power_of in range(lowest, highest + 1):
        result_sum = result_sum + jnp.where(exponent == power_of, 2.0**power_of, 0.0)
    return result_sum


def routing(expert_ids, route_weight, my_ctx, my_exp):
    z, k = my_ctx % 8, my_exp % 2
    rows = expert_ids.shape[0]
    named = expert_ids[:, :, None] == jnp.arange(64, dtype=jnp.int32)[None, None, :]
    member = jnp.sum(named.astype(F32), axis=1)
    weight = jnp.sum(jnp.where(named, route_weight[:, :, None], 0.0), axis=1)
    earlier = jnp.arange(rows)[:, None] > jnp.arange(rows)[None, :]
    slot = jnp.sum(jnp.where(earlier[:, :, None], member[None], 0.0), axis=1)
    number = (z * 32 + k * 16 + 1 + jnp.arange(rows, dtype=jnp.int32)).astype(F32)
    at = (slot[:, :, None] == jnp.arange(3).astype(F32)) & (member[:, :, None] > 0.5)
    token = jnp.sum(jnp.where(at, number[:, None, None], 0.0), axis=0)
    gain = jnp.sum(jnp.where(at, weight[:, :, None], 0.0), axis=0)
    both = jnp.stack([token, gain], axis=0).reshape(2, 2, 8, 4, 3)
    both = both.transpose(2, 0, 1, 3, 4).reshape(8, 2, 8, 1, 1, 3)
    here = (jnp.arange(8) == z)[:, None, None] & (jnp.arange(2) == k)[None, :, None]
    spread = jnp.where(here[None, None, None], both, 0.0).reshape(8, 2, 384)
    return jnp.concatenate([spread, jnp.zeros((8, 6, 384), F32)], axis=1)


def shards(
    residual,
    encoded_query_rows,
    quantized_key_rows,
    quantized_value_rows,
    key_block_exponent,
    value_block_exponent,
    block_order,
    out_weight,
    norm_gain,
    expert_ids,
    route_weight,
    gate_weight,
    gate_scale,
    up_weight,
    up_scale,
    down_weight,
    down_scale,
):
    def expanded(scale):
        return jnp.repeat(pow_two(scale, -1, 1), 128, axis=1)

    return layer(
        encoded_query_rows,
        quantized_key_rows,
        quantized_value_rows,
        key_block_exponent,
        value_block_exponent,
        block_order,
        out_weight,
        residual,
        norm_gain.reshape(1, -1),
        routing(expert_ids, route_weight, lax.axis_index("ctx"), lax.axis_index("exp")),
        gate_weight[0],
        up_weight[0],
        down_weight[0],
        expanded(gate_scale[0]),
        expanded(up_scale[0]),
        expanded(down_scale[0]),
    )


def solution(mesh):
    return jax.shard_map(
        shards,
        mesh=mesh,
        in_specs=(
            P(("dp", "ctx", "exp"), None),
            P(("dp", "ctx"), "exp"),
            P(("dp", "ctx"), None),
            P(("dp", "ctx"), None),
            P(("dp", "ctx"), None),
            P(("dp", "ctx"), None),
            P(),
            P("exp", "ctx"),
            P(),
            P(("dp", "ctx", "exp"), None),
            P(("dp", "ctx", "exp"), None),
            P(("ctx", "exp"), None, None),
            P(("ctx", "exp"), None, None),
            P(("ctx", "exp"), None, None),
            P(("ctx", "exp"), None, None),
            P(("ctx", "exp"), None, None),
            P(("ctx", "exp"), None, None),
        ),
        out_specs=P(("dp", "ctx", "exp"), None),
        check_vma=False,
    )
```

```python
import math

import jax
import jax.numpy as jnp
from jax import lax
from jax.experimental import pallas as pl
from jax.experimental.pallas import tpu as pltpu
from jax.sharding import PartitionSpec as P

HEAD_SIZE = 128

MESH = pl.DeviceIdType.MESH
F32 = jnp.float32
BF16 = jnp.bfloat16
NQ = 4
OFFSETS = (0, 1, 7, 2, 6, 3, 5, 4)
GROUPS = ((0, 1), (1, 3), (3, 5), (5, 8))
PLANE = [(dx, dy) for dy in range(2) for dx in range(4)]


def contract_first(lhs, rhs):
    return lax.dot_general(lhs, rhs, (((0,), (0,)), ((), ())), preferred_element_type=F32)


def contract_last(lhs, rhs):
    return lax.dot_general(lhs, rhs, (((1,), (1,)), ((), ())), preferred_element_type=F32)


def mul(lhs, rhs):
    return jnp.dot(lhs, rhs, preferred_element_type=F32)


def remote(src, dst, send_sem, recv_sem, device):
    return pltpu.make_async_remote_copy(
        src_ref=src,
        dst_ref=dst,
        send_sem=send_sem,
        recv_sem=recv_sem,
        device_id=device,
        device_id_type=MESH,
    )


def hops(q):
    return (4, 3) if q % 2 == 0 else (3, 4)


class Place:
    def __init__(self):
        self.ctx = lax.axis_index("ctx")
        self.exp = lax.axis_index("exp")
        self.dp = lax.axis_index("dp")
        self.z = self.ctx % 8
        self.yh = self.ctx // 8
        self.x = self.exp // 2
        self.k = self.exp % 2
        self.plane = self.yh * 4 + self.x

    def at_ctx(self, i):
        return {"ctx": (self.ctx + i) % 16, "exp": self.exp, "dp": self.dp}

    def at_z(self, dz, dk=0):
        z = (self.z + dz) % 8
        k = (self.k + dk) % 2
        return {"ctx": self.yh * 8 + z, "exp": self.x * 2 + k, "dp": self.dp}

    def at_plane(self, dx, dy):
        x = (self.x + dx) % 4
        yh = (self.yh + dy) % 2
        dp = (self.dp + dy) % 2
        return {"ctx": yh * 8 + self.z, "exp": x * 2 + self.k, "dp": dp}, yh * 4 + x

    def plane_from(self, dx, dy):
        return ((self.yh + 2 - dy) % 2) * 4 + (self.x + 4 - dx) % 4

    def other_core(self):
        return {"ctx": self.ctx, "exp": self.x * 2 + (1 - self.k), "dp": self.dp}


def layer_kernel(
    q_ref,
    kq_ref,
    vq_ref,
    ke_ref,
    ve_ref,
    order_ref,
    w_ref,
    res_ref,
    gain_ref,
    ids_ref,
    rw_ref,
    gw_ref,
    uw_ref,
    dw_ref,
    gs_ref,
    us_ref,
    ds_ref,
    out_ref,
    *scratch_refs,
):
    r = dict(zip(SCRATCH, scratch_refs, strict=True))
    sem = {name[:-2]: (r[name], r[name[:-2] + "_r"]) for name in SCRATCH if name.endswith("_s")}
    me = Place()
    z, k, x, yh = me.z, me.k, me.x, me.yh
    partner = me.other_core()
    right, left = me.at_z(1), me.at_z(7)
    xg, st = r["xg"], r["st"]
    ch = xg.shape[-1]
    sends = []

    def start(copy):
        copy.start()
        sends.append(copy)

    def pair(name, *index):
        return sem[name][0].at[index], sem[name][1].at[index]

    loads = [
        pltpu.make_async_copy(src, r[dst], r["w_sem"].at[i])
        for i, (src, dst) in enumerate(((gw_ref, "raw_g"), (uw_ref, "raw_u"), (dw_ref, "raw_d")))
    ]
    for load in loads:
        load.start()

    barrier = pltpu.get_barrier_semaphore()
    peers = [me.at_plane(dx, dy)[0] for dx, dy in PLANE[1:]]
    peers = peers + [partner, right, left, me.at_ctx(8)]
    for peer in peers:
        pl.semaphore_signal(barrier, inc=1, device_id=peer, device_id_type=MESH)
    pl.semaphore_wait(barrier, len(peers))

    def gather(buf, name, q, step, rightward):
        block = (z + 8 - step) % 8 if rightward else (z + step) % 8
        sems = pair(name + "r" if rightward else name + "l", q, step)
        return remote(buf(block), buf(block), *sems, right if rightward else left)

    def gathered(buf, name, q, step, rightward):
        block = (z + 7 - step) % 8 if rightward else (z + 1 + step) % 8
        sems = pair(name + "r" if rightward else name + "l", q, step)
        remote(buf(block), buf(block), *sems, right if rightward else left).wait_recv()

    def ring_start(buf, name, q):
        start(gather(buf, name, q, 0, True))
        start(gather(buf, name, q, 0, False))

    def ring_step(buf, name, q, step, arrived=None):
        for rightward, count in zip((True, False), hops(q)):
            if step <= count:
                gathered(buf, name, q, step - 1, rightward)
                if step < count:
                    start(gather(buf, name, q, step, rightward))
                if arrived is not None:
                    arrived(q, (8 - step if rightward else step) % 8)

    kv = r["kv"]
    row = lax.broadcasted_iota(jnp.int32, (128, 128), 0)
    col = lax.broadcasted_iota(jnp.int32, (128, 128), 1)
    head = pl.ds(pl.multiple_of(x * 128, 128), 128)
    first = jnp.where(k == 0, ke_ref[0, x], ve_ref[0, x])
    second = jnp.where(k == 0, ke_ref[1, x], ve_ref[1, x])
    power = jnp.where(row < 64, first, second)
    factor = jnp.zeros((128, 128), F32)
    for p in range(-2, 2):
        factor = factor + jnp.where(power == p, 2.0**p, 0.0)
    mine = jnp.where(k == 0, kq_ref[:, head].astype(F32), vq_ref[:, head].astype(F32))
    kv[k, me.ctx] = (mine * factor).astype(BF16)

    def kv_block(q):
        side = yh if q == 0 else 1 - yh
        return lambda block: kv.at[k, side * 8 + block]

    def kv_pass(q, offset, kind=k):
        at = kv.at[kind, (yh if q == 0 else 1 - yh) * 8 + (z + offset) % 8]
        return remote(at, at, *pair("kvp", q, offset), partner)

    def kv_arrived(q, offset):
        start(kv_pass(q, offset))

    own_kv = kv.at[k, me.ctx]
    start(remote(own_kv, own_kv, *pair("one", 5), me.at_ctx(8)))
    ring_start(kv_block(0), "kv", 0)
    kv_arrived(0, 0)

    mt = r["mt"]
    mt[z, k] = jnp.zeros((2, 16, 128), F32)
    mt[z, k, 0, :, 0:8] = ids_ref[...].astype(F32)
    mt[z, k, 1, :, 0:8] = rw_ref[...]

    def mt_block(block):
        return mt.at[block, k]

    def mt_pass(offset, core=k):
        at = mt.at[(z + offset) % 8, core]
        return remote(at, at, *pair("mtp", offset), partner)

    def mt_arrived(q, offset):
        start(mt_pass(offset))

    ring_start(mt_block, "mt", 0)
    mt_arrived(0, 0)

    wb = r["wb"]
    wb[k, z] = w_ref[:, pl.ds(pl.multiple_of(k * 128, 128), 128)]
    give = w_ref.at[:, pl.ds(pl.multiple_of((1 - k) * 128, 128), 128)]

    def w_block(q):
        core = k if q == 0 else 1 - k
        return lambda block: wb.at[core, block]

    start(remote(give, wb.at[k, z], *pair("one", 2), partner))
    ring_start(w_block(0), "w", 0)

    res, res_give, gain = r["res"], r["res_give"], r["gain"]
    for c in range(16):
        to = slice(c * 128, (c + 1) * 128)
        own = pl.ds(pl.multiple_of(c * 256 + k * 128, 128), 128)
        other = pl.ds(pl.multiple_of(c * 256 + (1 - k) * 128, 128), 128)
        res[k, :, to] = res_ref[:, own]
        res_give[:, to] = res_ref[:, other]
        gain[:, to] = gain_ref[:, own]
    start(remote(res_give, res.at[k], *pair("one", 3), partner))

    def power_of(exponent):
        return jnp.where(exponent == 0, 1.0, jnp.where(exponent > 0, 2.0, 0.5))

    def scaled(raw, scale, deq):
        def body(c, carry):
            for half in range(2):
                side = k if half == 0 else 1 - k
                at = pl.ds(pl.multiple_of(c * 256 + side * 128, 128), 128)
                to = pl.ds(pl.multiple_of(c * 128, 128), 128)
                for b in range(3):
                    cols = slice(b * 128, (b + 1) * 128)
                    block = raw[at, cols].astype(F32) * power_of(scale[c * 2 + side, b])
                    deq[half, to, cols] = block.astype(BF16)
            return carry

        lax.fori_loop(0, 16, body, 0)

    def scaled_down(raw, scale, deq):
        def body(c, carry):
            for half in range(2):
                side = k if half == 0 else 1 - k
                at = pl.ds(pl.multiple_of(c * 256 + side * 128, 128), 128)
                to = pl.ds(pl.multiple_of(c * 128, 128), 128)
                for b in range(3):
                    rows = slice(b * 128, (b + 1) * 128)
                    block = raw[rows, at].astype(F32) * power_of(scale[b, c * 2 + side])
                    deq[half, rows, to] = block.astype(BF16)
            return carry

        lax.fori_loop(0, 16, body, 0)

    across = kv.at[k, (1 - yh) * 8 + z]
    remote(across, across, *pair("one", 5), me.at_ctx(8)).wait_recv()
    ring_start(kv_block(1), "kv", 1)
    kv_arrived(1, 0)
    remote(give, wb.at[1 - k, z], *pair("one", 2), partner).wait_recv()
    ring_start(w_block(1), "w", 1)

    bias = r["bias"]
    own_place = order_ref[me.ctx]
    for j in range(16):
        seen = order_ref[j] * 128 + col <= own_place * 128 + row
        bias[:, j * 128 : (j + 1) * 128] = jnp.where(seen, 0.0, -1e30)

    for step in range(1, 5):
        for q in range(2):
            ring_step(kv_block(q), "kv", q, step, kv_arrived)
        ring_step(mt_block, "mt", 0, step, mt_arrived)
        if step == 1:
            loads[0].wait()
            scaled(r["raw_g"], gs_ref, r["deq_g"])
        if step >= 3:
            ring_step(w_block(step - 3), "w", step - 3, 1)
    for q in range(2):
        for offset in range(8):
            kv_pass(q, offset, 1 - k).wait_recv()

    ab = r["ab"]
    keys, values = kv[0].reshape(2048, 128), kv[1].reshape(2048, 128)
    for h in range(4):
        to = slice(h * 128, (h + 1) * 128)
        scores = contract_last(q_ref[:, to], keys) * (1.0 / math.sqrt(HEAD_SIZE) * math.log2(math.e))
        scores = scores + bias[...]
        exps = jnp.exp2(scores - jnp.max(scores, axis=1, keepdims=True))
        total = jnp.sum(exps, axis=1, keepdims=True)
        ab[k, yh, :, to] = (mul(exps.astype(BF16), values) / total).astype(BF16)
        ring_step(w_block(h % 2), "w", h % 2, 2 + h // 2)
    over = me.at_plane(0, 1)[0]
    start(remote(ab.at[k, yh], ab.at[k, yh], *pair("a", 0), partner))
    start(remote(ab.at[k, yh], ab.at[k, yh], *pair("a", 1), over))

    for offset in range(8):
        mt_pass(offset, 1 - k).wait_recv()
    table = mt[...].reshape(16, 2, 16, 128)
    ids, rw = table[:, 0].reshape(256, 128), table[:, 1].reshape(256, 128)
    slot = lax.broadcasted_iota(jnp.int32, (256, 384), 1)
    token = lax.broadcasted_iota(jnp.int32, (256, 384), 0)
    expert = slot // 48
    named = ((expert // 4) * 32 + z * 4 + expert % 4).astype(F32)
    member = jnp.zeros((256, 384), F32)
    weights = jnp.zeros((256, 384), F32)
    for n in range(8):
        hit = ids[:, n : n + 1] == named
        member = jnp.where(hit, 1.0, member)
        weights = jnp.where(hit, rw[:, n : n + 1], weights)
    first = lax.broadcasted_iota(jnp.int32, (256, 256), 0)
    second = lax.broadcasted_iota(jnp.int32, (256, 256), 1)
    earlier = (second < first) & (second // 16 == first // 16)
    number = mul(jnp.where(earlier, 1.0, 0.0).astype(BF16), member.astype(BF16))
    here = (number == (slot % 3).astype(F32)) & ((slot % 48) // 3 == token // 16)
    weights = jnp.where(here, weights, 0.0)
    select, weights_hi, weights_lo = r["sel"], r["whi"], r["wlo"]
    select[...] = jnp.where(here, member, 0.0).astype(BF16)
    weights_hi[...] = weights.astype(BF16)
    weights_lo[...] = (weights - weights.astype(BF16).astype(F32)).astype(BF16)

    came = ab.at[k, 1 - yh]
    remote(came, came, *pair("a", 1), over).wait_recv()
    start(remote(came, came, *pair("a", 2), partner))
    for i, there in ((0, yh), (2, 1 - yh)):
        came = ab.at[1 - k, there]
        remote(came, came, *pair("a", i), partner).wait_recv()

    px, rx, tot, yo, yi = r["px"], r["rx"], r["tot"], r["yo"], r["yi"]
    attended = [ab[core].reshape(256, 512) for core in range(2)]

    def x_copy(g, dx):
        lo, hi = GROUPS[g]
        part = pl.ds(lo, hi - lo)
        return remote(
            px.at[(x + dx) % 4, part], rx.at[dx, part], *pair("x", g, dx), me.at_plane(dx, 0)[0]
        )

    def y_copy(g):
        lo, hi = GROUPS[g]
        part = pl.ds(lo, hi - lo)
        return remote(yo.at[part], yi.at[part], *pair("y", g), over)

    for g, (lo, hi) in enumerate(GROUPS):
        if g == len(GROUPS) - 1:
            loads[1].wait()
            scaled(r["raw_u"], us_ref, r["deq_u"])
            for q in range(2):
                ring_step(w_block(q), "w", q, 4)
        for n in range(lo, hi):
            at = (z + OFFSETS[n]) % 8
            part = mul(attended[0], wb[0, at]) + mul(attended[1], wb[1, at])
            part = part.astype(BF16).reshape(2, 4, 32, 128)
            for to in range(4):
                px[to, n] = part[:, to]
        for dx in range(1, 4):
            start(x_copy(g, dx))

    loads[2].wait()
    scaled_down(r["raw_d"], ds_ref, r["deq_d"])
    start(remote(r["deq_d"].at[1], r["down_in"], *pair("one", 0), partner))

    def place_columns(n, side, values):
        at = pl.ds(pl.multiple_of((side * 8 + (z + OFFSETS[n]) % 8) * 128, 128), 128)
        st[:, at] = values

    for g, (lo, hi) in enumerate(GROUPS):
        for dx in range(1, 4):
            x_copy(g, dx).wait_recv()
        for n in range(lo, hi):
            total = px[x, n].astype(F32)
            for dx in range(1, 4):
                total = total + rx[dx, n].astype(F32)
            tot[n] = total
            yo[n] = tot[n, 1 - yh].astype(BF16)
            place_columns(n, yh, tot[n, yh])
        start(y_copy(g))
    remote(res_give, res.at[1 - k], *pair("one", 3), partner).wait_recv()
    for g, (lo, hi) in enumerate(GROUPS):
        y_copy(g).wait_recv()
        for n in range(lo, hi):
            place_columns(n, 1 - yh, yi[n].astype(F32))
    st[...] = st[...] + res[...].reshape(32, 2048).astype(F32)
    squares = jnp.sum(st[...] * st[...], axis=1, keepdims=True)
    r["sq"][0] = jnp.broadcast_to(squares, (32, 128))
    swap = remote(r["sq"].at[0], r["sq"].at[1], *pair("one", 4), partner)
    start(swap)
    swap.wait_recv()
    mean = (r["sq"][0, :, 0:1] + r["sq"][1, :, 0:1]) / 4096.0
    normed = (st[...] * lax.rsqrt(mean + 1e-6) * gain[...]).astype(BF16)

    def x_block(q):
        return lambda block: xg.at[q, block]

    for q in range(NQ):
        xg[q, z] = normed[:, q * ch : (q + 1) * ch]
        ring_start(x_block(q), "z", q)

    for step in range(1, 4):
        for q in range(NQ):
            ring_step(x_block(q), "z", q, step)

    def to_plane(bufs, bufr, name, q, d):
        device, there = me.at_plane(*PLANE[d])
        return remote(bufs.at[q, there], bufr.at[q, me.plane], *pair(name, q, d), device)

    def from_plane(bufr, name, q, d):
        came = me.plane_from(*PLANE[d])
        remote(bufr.at[q, came], bufr.at[q, came], *pair(name, q, d), partner).wait_recv()
        return came

    ys, yr, xo = r["ys"], r["yr"], r["xo"]
    for q in range(NQ):
        ring_step(x_block(q), "z", q, 4)
        picked = contract_first(select[...], xg[q].reshape(256, ch)).astype(BF16)
        ys[q] = picked.reshape(8, 48, ch)
        for d in range(1, 8):
            start(to_plane(ys, yr, "pd", q, d))
        yr[q, me.plane] = ys[q, me.plane]
        start(remote(yr.at[q, me.plane], xo.at[q, me.plane], *pair("fw", q, 0), partner))

    gate = jnp.zeros((384, 384), F32)
    up = jnp.zeros((384, 384), F32)
    for q in range(NQ):
        for d in range(1, 8):
            came = from_plane(yr, "pd", q, d)
            start(remote(yr.at[q, came], xo.at[q, came], *pair("fw", q, d), partner))
        for d in range(8):
            came = me.plane_from(*PLANE[d])
            remote(yr.at[q, came], xo.at[q, came], *pair("fw", q, d), partner).wait_recv()
        for half, rows in ((0, yr), (1, xo)):
            block = rows[q].reshape(384, ch)
            gate = gate + mul(block, r["deq_g"][half, q * ch : (q + 1) * ch, :])
            up = up + mul(block, r["deq_u"][half, q * ch : (q + 1) * ch, :])
    hid, hid_in = r["hid"], r["hid_in"]
    hid[...] = (gate / (1.0 + jnp.exp(-gate)) * up).astype(BF16)
    swap = remote(hid, hid_in, *pair("one", 1), partner)
    start(swap)
    remote(r["deq_d"].at[1], r["down_in"], *pair("one", 0), partner).wait_recv()
    swap.wait_recv()

    es, er = r["es"], r["er"]
    for q in range(NQ):
        cols = slice(q * ch, (q + 1) * ch)
        result = mul(hid[...], r["deq_d"][0, :, cols]) + mul(hid_in[...], r["down_in"][:, cols])
        es[q] = result.astype(BF16).reshape(8, 48, ch)
        for d in range(1, 8):
            start(to_plane(es, er, "ps", q, d))
        er[q, me.plane] = es[q, me.plane]

    comb = r["comb"]

    def back(q, step, rightward):
        side, there = ("br", right) if rightward else ("bl", left)
        return remote(
            r[side + "_out"].at[q, step], r[side + "_in"].at[q, step], *pair(side, q, step), there
        )

    def back_start(q, step, rightward):
        rights, lefts = hops(q)
        side = "br" if rightward else "bl"
        block = (z + rights - step) % 8 if rightward else (z + 8 - lefts + step) % 8
        part = comb[q, block]
        if step:
            back(q, step - 1, rightward).wait_recv()
            part = part + r[side + "_in"][q, step - 1].astype(F32)
        r[side + "_out"][q, step] = part.astype(BF16)
        start(back(q, step, rightward))

    for q in range(NQ):
        for d in range(1, 8):
            from_plane(er, "ps", q, d)
        rows = er[q].reshape(384, ch)
        comb[q] = (mul(weights_hi[...], rows) + mul(weights_lo[...], rows)).reshape(8, 32, ch)
        back_start(q, 0, True)
        back_start(q, 0, False)
    for step in range(1, 4):
        for q in range(NQ):
            for rightward, count in zip((True, False), hops(q)):
                if step < count:
                    back_start(q, step, rightward)
    fin, fin_in = r["fin"], r["fin_in"]
    for q in range(NQ):
        total = comb[q, z] + st[:, q * ch : (q + 1) * ch]
        for rightward, count in zip((True, False), hops(q)):
            back(q, count - 1, rightward).wait_recv()
            total = total + r["br_in" if rightward else "bl_in"][q, count - 1].astype(F32)
        fin[q] = total.astype(BF16).reshape(2, 16, ch)
        start(remote(fin.at[q, 1 - k], fin_in.at[q], *pair("fn", q), partner))
    for q in range(NQ):
        remote(fin.at[q, 1 - k], fin_in.at[q], *pair("fn", q), partner).wait_recv()
        own, got = fin[q, k], fin_in[q]
        for c in range(ch // 128):
            at = (q * (ch // 128) + c) * 256
            piece = slice(c * 128, (c + 1) * 128)
            out_ref[:, pl.ds(pl.multiple_of(at + k * 128, 128), 128)] = own[:, piece]
            out_ref[:, pl.ds(pl.multiple_of(at + (1 - k) * 128, 128), 128)] = got[:, piece]
    for copy in sends:
        copy.wait_send()


def scratch():
    ch = 2048 // NQ
    shapes = {
        "kv": ((2, 16, 128, 128), BF16),
        "wb": ((2, 8, 512, 128), BF16),
        "res": ((2, 16, 2048), BF16),
        "res_give": ((16, 2048), BF16),
        "gain": ((1, 2048), F32),
        "bias": ((128, 2048), F32),
        "ab": ((2, 2, 128, 512), BF16),
        "px": ((4, 8, 2, 32, 128), BF16),
        "rx": ((4, 8, 2, 32, 128), BF16),
        "tot": ((8, 2, 32, 128), F32),
        "yo": ((8, 32, 128), BF16),
        "yi": ((8, 32, 128), BF16),
        "st": ((32, 2048), F32),
        "sq": ((2, 32, 128), F32),
        "mt": ((8, 2, 2, 16, 128), F32),
        "sel": ((256, 384), BF16),
        "whi": ((256, 384), BF16),
        "wlo": ((256, 384), BF16),
        "xg": ((NQ, 8, 32, ch), BF16),
        "ys": ((NQ, 8, 48, ch), BF16),
        "yr": ((NQ, 8, 48, ch), BF16),
        "xo": ((NQ, 8, 48, ch), BF16),
        "raw_g": ((4096, 384), BF16),
        "raw_u": ((4096, 384), BF16),
        "raw_d": ((384, 4096), BF16),
        "deq_g": ((2, 2048, 384), BF16),
        "deq_u": ((2, 2048, 384), BF16),
        "deq_d": ((2, 384, 2048), BF16),
        "down_in": ((384, 2048), BF16),
        "hid": ((384, 384), BF16),
        "hid_in": ((384, 384), BF16),
        "es": ((NQ, 8, 48, ch), BF16),
        "er": ((NQ, 8, 48, ch), BF16),
        "comb": ((NQ, 8, 32, ch), F32),
        "br_out": ((NQ, 4, 32, ch), BF16),
        "br_in": ((NQ, 4, 32, ch), BF16),
        "bl_out": ((NQ, 4, 32, ch), BF16),
        "bl_in": ((NQ, 4, 32, ch), BF16),
        "fin": ((NQ, 2, 16, ch), BF16),
        "fin_in": ((NQ, 16, ch), BF16),
    }
    made = {name: pltpu.VMEM(*what) for name, what in shapes.items()}
    made["w_sem"] = pltpu.SemaphoreType.DMA((3,))
    copies = {
        "kvr": (2, 4),
        "kvl": (2, 4),
        "kvp": (2, 8),
        "mtr": (1, 4),
        "mtl": (1, 4),
        "mtp": (8,),
        "one": (6,),
        "wr": (2, 4),
        "wl": (2, 4),
        "a": (3,),
        "x": (len(GROUPS), 4),
        "y": (len(GROUPS),),
        "zr": (NQ, 4),
        "zl": (NQ, 4),
        "pd": (NQ, 8),
        "fw": (NQ, 8),
        "ps": (NQ, 8),
        "br": (NQ, 4),
        "bl": (NQ, 4),
        "fn": (NQ,),
    }
    for name, shape in copies.items():
        made[name + "_s"] = pltpu.SemaphoreType.DMA(shape)
        made[name + "_r"] = pltpu.SemaphoreType.DMA(shape)
    return made


SCRATCH = tuple(scratch())


def layer(*operands):
    vmem = pl.BlockSpec(memory_space=pltpu.VMEM)
    smem = pl.BlockSpec(memory_space=pltpu.SMEM)
    hbm = pl.BlockSpec(memory_space=pl.ANY)
    return pl.pallas_call(
        layer_kernel,
        out_shape=jax.ShapeDtypeStruct((16, 4096), BF16),
        in_specs=[vmem] * 3 + [smem] * 3 + [vmem] * 5 + [hbm] * 3 + [smem] * 3,
        out_specs=vmem,
        scratch_shapes=list(scratch().values()),
        compiler_params=pltpu.CompilerParams(
            collective_id=1, has_side_effects=True, vmem_limit_bytes=58 * 1024 * 1024
        ),
        name="layer",
    )(*operands)


def shards(
    residual,
    encoded_query_rows,
    quantized_key_rows,
    quantized_value_rows,
    key_block_exponent,
    value_block_exponent,
    block_order,
    out_weight,
    norm_gain,
    expert_ids,
    route_weight,
    gate_weight,
    gate_scale,
    up_weight,
    up_scale,
    down_weight,
    down_scale,
):
    return layer(
        encoded_query_rows,
        quantized_key_rows,
        quantized_value_rows,
        key_block_exponent,
        value_block_exponent,
        block_order,
        out_weight,
        residual,
        norm_gain.reshape(1, -1),
        expert_ids,
        route_weight,
        gate_weight[0],
        up_weight[0],
        down_weight[0],
        gate_scale[0],
        up_scale[0],
        down_scale[0],
    )


def solution(mesh):
    return jax.shard_map(
        shards,
        mesh=mesh,
        in_specs=(
            P(("dp", "ctx", "exp"), None),
            P(("dp", "ctx"), "exp"),
            P(("dp", "ctx"), None),
            P(("dp", "ctx"), None),
            P(("dp", "ctx"), None),
            P(("dp", "ctx"), None),
            P(),
            P("exp", "ctx"),
            P(),
            P(("dp", "ctx", "exp"), None),
            P(("dp", "ctx", "exp"), None),
            P(("ctx", "exp"), None, None),
            P(("ctx", "exp"), None, None),
            P(("ctx", "exp"), None, None),
            P(("ctx", "exp"), None, None),
            P(("ctx", "exp"), None, None),
            P(("ctx", "exp"), None, None),
        ),
        out_specs=P(("dp", "ctx", "exp"), None),
        check_vma=False,
    )
```

```python
import math

import jax
import jax.numpy as jnp
from jax import lax
from jax.experimental import pallas as pl
from jax.experimental.pallas import tpu as pltpu
from jax.sharding import PartitionSpec as P

HEAD_SIZE = 128

MESH = pl.DeviceIdType.MESH
F32 = jnp.float32
BF16 = jnp.bfloat16
NQ = 4
OFFSETS = (0, 1, 7, 2, 6, 3, 5, 4)
GROUPS = ((0, 1), (1, 3), (3, 5), (5, 8))
PLANE = [(dx, dy) for dy in range(2) for dx in range(4)]


def contract_first(lhs, rhs):
    return lax.dot_general(lhs, rhs, (((0,), (0,)), ((), ())), preferred_element_type=F32)


def contract_last(lhs, rhs):
    return lax.dot_general(lhs, rhs, (((1,), (1,)), ((), ())), preferred_element_type=F32)


def mul(lhs, rhs):
    return jnp.dot(lhs, rhs, preferred_element_type=F32)


def remote(src, dst, send_sem, recv_sem, device):
    return pltpu.make_async_remote_copy(
        src_ref=src,
        dst_ref=dst,
        send_sem=send_sem,
        recv_sem=recv_sem,
        device_id=device,
        device_id_type=MESH,
    )


def hops(q):
    return (4, 3) if q % 2 == 0 else (3, 4)


class Place:
    def __init__(self):
        self.ctx = lax.axis_index("ctx")
        self.exp = lax.axis_index("exp")
        self.dp = lax.axis_index("dp")
        self.z = self.ctx % 8
        self.yh = self.ctx // 8
        self.x = self.exp // 2
        self.k = self.exp % 2
        self.plane = self.yh * 4 + self.x

    def at_ctx(self, i):
        return {"ctx": (self.ctx + i) % 16, "exp": self.exp, "dp": self.dp}

    def at_z(self, dz, dk=0):
        z = (self.z + dz) % 8
        k = (self.k + dk) % 2
        return {"ctx": self.yh * 8 + z, "exp": self.x * 2 + k, "dp": self.dp}

    def at_plane(self, dx, dy):
        x = (self.x + dx) % 4
        yh = (self.yh + dy) % 2
        dp = (self.dp + dy) % 2
        return {"ctx": yh * 8 + self.z, "exp": x * 2 + self.k, "dp": dp}, yh * 4 + x

    def plane_from(self, dx, dy):
        return ((self.yh + 2 - dy) % 2) * 4 + (self.x + 4 - dx) % 4

    def other_core(self):
        return {"ctx": self.ctx, "exp": self.x * 2 + (1 - self.k), "dp": self.dp}


def layer_kernel(
    q_ref,
    kq_ref,
    vq_ref,
    ke_ref,
    ve_ref,
    order_ref,
    w_ref,
    res_ref,
    gain_ref,
    ids_ref,
    rw_ref,
    gw_ref,
    uw_ref,
    dw_ref,
    gs_ref,
    us_ref,
    ds_ref,
    out_ref,
    *scratch_refs,
):
    r = dict(zip(SCRATCH, scratch_refs, strict=True))
    sem = {name[:-2]: (r[name], r[name[:-2] + "_r"]) for name in SCRATCH if name.endswith("_s")}
    me = Place()
    z, k, x, yh = me.z, me.k, me.x, me.yh
    partner = me.other_core()
    right, left = me.at_z(1), me.at_z(7)
    xg, st = r["xg"], r["st"]
    ch = xg.shape[-1]
    sends = []

    def start(copy):
        copy.start()
        sends.append(copy)

    def pair(name, *index):
        return sem[name][0].at[index], sem[name][1].at[index]

    loads = [
        pltpu.make_async_copy(src, r[dst], r["w_sem"].at[i])
        for i, (src, dst) in enumerate(((gw_ref, "raw_g"), (uw_ref, "raw_u"), (dw_ref, "raw_d")))
    ]
    for load in loads:
        load.start()

    barrier = pltpu.get_barrier_semaphore()
    peers = [me.at_plane(dx, dy)[0] for dx, dy in PLANE[1:]]
    peers = peers + [partner, me.at_ctx(8)] + [me.at_z(i) for i in range(1, 8)]
    for peer in peers:
        pl.semaphore_signal(barrier, inc=1, device_id=peer, device_id_type=MESH)
    pl.semaphore_wait(barrier, len(peers))

    def gather(buf, name, q, step, rightward):
        block = (z + 8 - step) % 8 if rightward else (z + step) % 8
        sems = pair(name + "r" if rightward else name + "l", q, step)
        return remote(buf(block), buf(block), *sems, right if rightward else left)

    def gathered(buf, name, q, step, rightward):
        block = (z + 7 - step) % 8 if rightward else (z + 1 + step) % 8
        sems = pair(name + "r" if rightward else name + "l", q, step)
        remote(buf(block), buf(block), *sems, right if rightward else left).wait_recv()

    def ring_start(buf, name, q):
        start(gather(buf, name, q, 0, True))
        start(gather(buf, name, q, 0, False))

    def ring_step(buf, name, q, step, arrived=None):
        for rightward, count in zip((True, False), hops(q)):
            if step <= count:
                gathered(buf, name, q, step - 1, rightward)
                if step < count:
                    start(gather(buf, name, q, step, rightward))
                if arrived is not None:
                    arrived(q, (8 - step if rightward else step) % 8)

    kv = r["kv"]
    row = lax.broadcasted_iota(jnp.int32, (128, 128), 0)
    col = lax.broadcasted_iota(jnp.int32, (128, 128), 1)
    head = pl.ds(pl.multiple_of(x * 128, 128), 128)
    first = jnp.where(k == 0, ke_ref[0, x], ve_ref[0, x])
    second = jnp.where(k == 0, ke_ref[1, x], ve_ref[1, x])
    power = jnp.where(row < 64, first, second)
    factor = jnp.zeros((128, 128), F32)
    for p in range(-2, 2):
        factor = factor + jnp.where(power == p, 2.0**p, 0.0)
    mine = jnp.where(k == 0, kq_ref[:, head].astype(F32), vq_ref[:, head].astype(F32))
    kv[k, me.ctx] = (mine * factor).astype(BF16)

    def kv_at(offset, side, kind=k):
        return kv.at[kind, (yh if side == 0 else 1 - yh) * 8 + (z + offset) % 8]

    def kv_copy(offset):
        own = kv_at(0, 0)
        return remote(own, own, *pair("kv", offset), me.at_z(offset))

    def kv_across(offset):
        at = kv_at(offset, 0)
        return remote(at, at, *pair("kva", offset), me.at_ctx(8))

    def kv_pass(offset, side):
        at = kv_at(offset, side)
        return remote(at, at, *pair("kvp", side, offset), partner)

    for offset in (4, 3, 5, 2, 6, 1, 7):
        start(kv_copy(offset))
    start(kv_across(0))
    start(kv_pass(0, 0))

    mt = r["mt"]
    mt[z, k] = jnp.zeros((2, 8, 128), F32)
    mt[z, k, 0, :, 0:16] = ids_ref[...].astype(F32)
    mt[z, k, 1, :, 0:16] = rw_ref[...]

    def mt_copy(offset):
        return remote(mt.at[z, k], mt.at[z, k], *pair("mt", offset), me.at_z(offset))

    def mt_pass(offset, core=k):
        at = mt.at[(z + offset) % 8, core]
        return remote(at, at, *pair("mtp", offset), partner)

    for offset in range(1, 8):
        start(mt_copy(offset))
    start(mt_pass(0))

    wb = r["wb"]
    wb[k, z] = w_ref[:, pl.ds(pl.multiple_of(k * 128, 128), 128)]
    give = w_ref.at[:, pl.ds(pl.multiple_of((1 - k) * 128, 128), 128)]

    def w_block(q):
        core = k if q < 2 else 1 - k
        rows = pl.ds((q % 2) * 256, 256)
        return lambda block: wb.at[core, block, rows]

    def w_step(step, parts=range(4)):
        for q in parts:
            ring_step(w_block(q), "w", q, step)

    start(remote(give, wb.at[k, z], *pair("one", 2), partner))
    for q in range(2):
        ring_start(w_block(q), "w", q)

    res, res_give, gain = r["res"], r["res_give"], r["gain"]
    for c in range(16):
        to = slice(c * 128, (c + 1) * 128)
        own = pl.ds(pl.multiple_of(c * 256 + k * 128, 128), 128)
        other = pl.ds(pl.multiple_of(c * 256 + (1 - k) * 128, 128), 128)
        res[k, :, to] = res_ref[:, own]
        res_give[:, to] = res_ref[:, other]
        gain[:, to] = gain_ref[:, own]
    start(remote(res_give, res.at[k], *pair("one", 3), partner))

    def power_of(exponent):
        return jnp.where(exponent == 0, 1.0, jnp.where(exponent > 0, 2.0, 0.5))

    def scaled(raw, scale, deq, lo=0, hi=16):
        def body(c, carry):
            for half in range(2):
                side = k if half == 0 else 1 - k
                at = pl.ds(pl.multiple_of(c * 256 + side * 128, 128), 128)
                to = pl.ds(pl.multiple_of(c * 128, 128), 128)
                for b in range(3):
                    cols = slice(b * 128, (b + 1) * 128)
                    block = raw[at, cols].astype(F32) * power_of(scale[b, 0, c * 2 + side])
                    deq[half, to, cols] = block.astype(BF16)
            return carry

        lax.fori_loop(lo, hi, body, 0)

    def scaled_down(raw, scale, deq, lo=0, hi=16):
        def body(c, carry):
            for half in range(2):
                side = k if half == 0 else 1 - k
                at = pl.ds(pl.multiple_of(c * 256 + side * 128, 128), 128)
                to = pl.ds(pl.multiple_of(c * 128, 128), 128)
                for b in range(3):
                    rows = slice(b * 128, (b + 1) * 128)
                    block = raw[rows, at].astype(F32) * power_of(scale[b, 0, c * 2 + side])
                    deq[half, rows, to] = block.astype(BF16)
            return carry

        lax.fori_loop(lo, hi, body, 0)

    remote(give, wb.at[1 - k, z], *pair("one", 2), partner).wait_recv()
    for q in range(2, 4):
        ring_start(w_block(q), "w", q)

    bias = r["bias"]
    own_place = order_ref[me.ctx]
    for j in range(16):
        seen = order_ref[j] * 128 + col <= own_place * 128 + row
        bias[:, j * 128 : (j + 1) * 128] = jnp.where(seen, 0.0, -1e30)

    loads[0].wait()
    scaled(r["raw_g"], gs_ref, r["deq_g"])
    for offset in (1, 7, 2, 6, 3, 5, 4):
        came = kv_at(8 - offset, 0)
        remote(came, came, *pair("kv", offset), partner).wait_recv()
        start(kv_across(8 - offset))
        start(kv_pass(8 - offset, 0))
    w_step(1)
    for offset in range(1, 8):
        came = mt.at[(z + 8 - offset) % 8, k]
        remote(came, came, *pair("mt", offset), partner).wait_recv()
        start(mt_pass(8 - offset))
    for offset in (0, 7, 1, 6, 2, 5, 3, 4):
        came = kv_at(offset, 1)
        remote(came, came, *pair("kva", offset), partner).wait_recv()
        start(kv_pass(offset, 1))
    for side in range(2):
        for offset in range(8):
            came = kv_at(offset, side, 1 - k)
            remote(came, came, *pair("kvp", side, offset), partner).wait_recv()

    ab = r["ab"]
    keys, values = kv[0].reshape(2048, 128), kv[1].reshape(2048, 128)
    for h in range(4):
        to = slice(h * 128, (h + 1) * 128)
        scores = contract_last(q_ref[:, to], keys) * (1.0 / math.sqrt(HEAD_SIZE) * math.log2(math.e))
        scores = scores + bias[...]
        exps = jnp.exp2(scores - jnp.max(scores, axis=1, keepdims=True))
        total = jnp.sum(exps, axis=1, keepdims=True)
        ab[k, yh, :, to] = (mul(exps.astype(BF16), values) / total).astype(BF16)
        if h == 1:
            w_step(2, range(2))
    w_step(2, range(2, 4))
    over = me.at_plane(0, 1)[0]
    start(remote(ab.at[k, yh], ab.at[k, yh], *pair("a", 0), partner))
    start(remote(ab.at[k, yh], ab.at[k, yh], *pair("a", 1), over))

    for offset in range(8):
        mt_pass(offset, 1 - k).wait_recv()
    tables = r["tables"]
    for n in range(16):
        for kind in range(2):
            block = jnp.transpose(mt[n // 2, n % 2, kind])
            tables[kind, n * 16 : (n + 1) * 16, 0:8] = block[0:16, :]
    ids, rw = tables[0], tables[1]
    slot = lax.broadcasted_iota(jnp.int32, (256, 384), 1)
    token = lax.broadcasted_iota(jnp.int32, (256, 384), 0)
    expert = slot // 48
    named = ((expert // 4) * 32 + z * 4 + expert % 4).astype(F32)
    member = jnp.zeros((256, 384), F32)
    weights = jnp.zeros((256, 384), F32)
    for n in range(8):
        hit = ids[:, n : n + 1] == named
        member = jnp.where(hit, 1.0, member)
        weights = jnp.where(hit, rw[:, n : n + 1], weights)
    first = lax.broadcasted_iota(jnp.int32, (256, 256), 0)
    second = lax.broadcasted_iota(jnp.int32, (256, 256), 1)
    earlier = (second < first) & (second // 16 == first // 16)
    number = mul(jnp.where(earlier, 1.0, 0.0).astype(BF16), member.astype(BF16))
    here = (number == (slot % 3).astype(F32)) & ((slot % 48) // 3 == token // 16)
    weights = jnp.where(here, weights, 0.0)
    select, weights_hi, weights_lo = r["sel"], r["whi"], r["wlo"]
    select[...] = jnp.where(here, member, 0.0).astype(BF16)
    weights_hi[...] = weights.astype(BF16)
    weights_lo[...] = (weights - weights.astype(BF16).astype(F32)).astype(BF16)

    w_step(3)
    came = ab.at[k, 1 - yh]
    remote(came, came, *pair("a", 1), over).wait_recv()
    start(remote(came, came, *pair("a", 2), partner))
    for i, there in ((0, yh), (2, 1 - yh)):
        came = ab.at[1 - k, there]
        remote(came, came, *pair("a", i), partner).wait_recv()

    px, rx, tot, yo, yi = r["px"], r["rx"], r["tot"], r["yo"], r["yi"]
    attended = [ab[core].reshape(256, 512) for core in range(2)]

    def x_copy(g, dx):
        lo, hi = GROUPS[g]
        part = pl.ds(lo, hi - lo)
        return remote(
            px.at[(x + dx) % 4, part], rx.at[dx, part], *pair("x", g, dx), me.at_plane(dx, 0)[0]
        )

    def y_copy(g):
        lo, hi = GROUPS[g]
        part = pl.ds(lo, hi - lo)
        return remote(yo.at[part], yi.at[part], *pair("y", g), over)

    for g, (lo, hi) in enumerate(GROUPS):
        if g == len(GROUPS) - 1:
            loads[1].wait()
            scaled(r["raw_u"], us_ref, r["deq_u"])
            w_step(4)
        for n in range(lo, hi):
            at = (z + OFFSETS[n]) % 8
            part = mul(attended[0], wb[0, at]) + mul(attended[1], wb[1, at])
            part = part.astype(BF16).reshape(2, 4, 32, 128)
            for to in range(4):
                px[to, n] = part[:, to]
        for dx in range(1, 4):
            start(x_copy(g, dx))

    def place_columns(n, side, values):
        at = pl.ds(pl.multiple_of((side * 8 + (z + OFFSETS[n]) % 8) * 128, 128), 128)
        st[:, at] = values

    for g, (lo, hi) in enumerate(GROUPS):
        for dx in range(1, 4):
            x_copy(g, dx).wait_recv()
        for n in range(lo, hi):
            total = px[x, n].astype(F32)
            for dx in range(1, 4):
                total = total + rx[dx, n].astype(F32)
            tot[n] = total
            yo[n] = tot[n, 1 - yh].astype(BF16)
            place_columns(n, yh, tot[n, yh])
        start(y_copy(g))
    remote(res_give, res.at[1 - k], *pair("one", 3), partner).wait_recv()
    for g, (lo, hi) in enumerate(GROUPS):
        y_copy(g).wait_recv()
        for n in range(lo, hi):
            place_columns(n, 1 - yh, yi[n].astype(F32))
    st[...] = st[...] + res[...].reshape(32, 2048).astype(F32)
    squares = jnp.sum(st[...] * st[...], axis=1, keepdims=True)
    r["sq"][0] = jnp.broadcast_to(squares, (32, 128))
    swap = remote(r["sq"].at[0], r["sq"].at[1], *pair("one", 4), partner)
    start(swap)
    swap.wait_recv()
    mean = (r["sq"][0, :, 0:1] + r["sq"][1, :, 0:1]) / 4096.0
    normed = (st[...] * lax.rsqrt(mean + 1e-6) * gain[...]).astype(BF16)

    for q in range(NQ):
        xg[q, z] = normed[:, q * ch : (q + 1) * ch]

    def z_copy(q, source, to):
        block = xg.at[q, (z + source) % 8]
        return remote(block, block, *pair("z", q, (source - to) % 8), me.at_z(to % 8))

    def z_wait(q, source):
        block = xg.at[q, (z + source) % 8]
        remote(block, block, *pair("z", q, source), partner).wait_recv()

    def z_first(q):
        for to in (2, -2, 1, -1):
            start(z_copy(q, 0, to))

    def z_second(q):
        for side in (1, -1):
            z_wait(q, (-2 * side) % 8)
            start(z_copy(q, -2 * side, side))
            if (side == 1) == (q % 2 == 0):
                start(z_copy(q, -2 * side, 2 * side))

    def to_plane(bufs, bufr, name, q, d):
        device, there = me.at_plane(*PLANE[d])
        return remote(bufs.at[q, there], bufr.at[q, me.plane], *pair(name, q, d), device)

    def from_plane(bufr, name, q, d):
        came = me.plane_from(*PLANE[d])
        remote(bufr.at[q, came], bufr.at[q, came], *pair(name, q, d), partner).wait_recv()
        return came

    ys, yr, xo = r["ys"], r["yr"], r["xo"]
    def pick(q):
        picked = contract_first(select[...], xg[q].reshape(256, ch)).astype(BF16)
        ys[q] = picked.reshape(8, 48, ch)
        for d in range(1, 8):
            start(to_plane(ys, yr, "pd", q, d))
        yr[q, me.plane] = ys[q, me.plane]
        start(remote(yr.at[q, me.plane], xo.at[q, me.plane], *pair("fw", q, 0), partner))

    ahead = 2
    for q in range(min(ahead, NQ)):
        z_first(q)
    loads[2].wait()
    for turn in range(NQ + 1):
        if turn < NQ:
            if turn < 2:
                scaled_down(r["raw_d"], ds_ref, r["deq_d"], turn * 8, turn * 8 + 8)
            z_second(turn)
            if turn + ahead < NQ:
                z_first(turn + ahead)
        if turn:
            for source in (1, 7, 3, 5, 4):
                z_wait(turn - 1, source)
            pick(turn - 1)
    start(remote(r["deq_d"].at[1], r["down_in"], *pair("one", 0), partner))

    gate = jnp.zeros((384, 384), F32)
    up = jnp.zeros((384, 384), F32)
    for q in range(NQ):
        for d in range(1, 8):
            came = from_plane(yr, "pd", q, d)
            start(remote(yr.at[q, came], xo.at[q, came], *pair("fw", q, d), partner))
        for d in range(8):
            came = me.plane_from(*PLANE[d])
            remote(yr.at[q, came], xo.at[q, came], *pair("fw", q, d), partner).wait_recv()
        for half, rows in ((0, yr), (1, xo)):
            block = rows[q].reshape(384, ch)
            gate = gate + mul(block, r["deq_g"][half, q * ch : (q + 1) * ch, :])
            up = up + mul(block, r["deq_u"][half, q * ch : (q + 1) * ch, :])
    hid, hid_in = r["hid"], r["hid_in"]
    hid[...] = (gate / (1.0 + jnp.exp(-gate)) * up).astype(BF16)
    swap = remote(hid, hid_in, *pair("one", 1), partner)
    start(swap)
    remote(r["deq_d"].at[1], r["down_in"], *pair("one", 0), partner).wait_recv()
    swap.wait_recv()

    es, er = r["es"], r["er"]
    for q in range(NQ):
        cols = slice(q * ch, (q + 1) * ch)
        result = mul(hid[...], r["deq_d"][0, :, cols]) + mul(hid_in[...], r["down_in"][:, cols])
        es[q] = result.astype(BF16).reshape(8, 48, ch)
        for d in range(1, 8):
            start(to_plane(es, er, "ps", q, d))
        er[q, me.plane] = es[q, me.plane]

    comb = r["comb"]

    towards = {1: 1, 7: -1, 3: 1, 5: -1, 2: 2, 6: -2}
    back_out, back_in = r["back_out"], r["back_in"]

    def back(q, offset):
        to = towards.get(offset, 2 if q % 2 == 0 else -2)
        return remote(
            back_out.at[q, offset], back_in.at[q, offset], *pair("b", q, offset), me.at_z(to % 8)
        )

    def back_start(q, offset, came=()):
        part = comb[q, (z + offset) % 8]
        for other in came:
            back(q, other).wait_recv()
            part = part + back_in[q, other].astype(F32)
        back_out[q, offset] = part.astype(BF16)
        start(back(q, offset))

    def back_second(q):
        back_start(q, 2, (3, 4) if q % 2 == 0 else (3,))
        back_start(q, 6, (5,) if q % 2 == 0 else (5, 4))

    fin, fin_in = r["fin"], r["fin_in"]
    for turn in range(NQ + 1):
        if turn < NQ:
            for d in range(1, 8):
                from_plane(er, "ps", turn, d)
            rows = er[turn].reshape(384, ch)
            total = mul(weights_hi[...], rows) + mul(weights_lo[...], rows)
            comb[turn] = total.reshape(8, 32, ch)
            for offset in (4, 3, 5, 1, 7):
                back_start(turn, offset)
        if turn:
            back_second(turn - 1)
    for q in range(NQ):
        total = comb[q, z] + st[:, q * ch : (q + 1) * ch]
        for offset in (1, 7, 2, 6):
            back(q, offset).wait_recv()
            total = total + back_in[q, offset].astype(F32)
        fin[q] = total.astype(BF16).reshape(2, 16, ch)
        start(remote(fin.at[q, 1 - k], fin_in.at[q], *pair("fn", q), partner))
    for q in range(NQ):
        remote(fin.at[q, 1 - k], fin_in.at[q], *pair("fn", q), partner).wait_recv()
        own, got = fin[q, k], fin_in[q]
        for c in range(ch // 128):
            at = (q * (ch // 128) + c) * 256
            piece = slice(c * 128, (c + 1) * 128)
            out_ref[:, pl.ds(pl.multiple_of(at + k * 128, 128), 128)] = own[:, piece]
            out_ref[:, pl.ds(pl.multiple_of(at + (1 - k) * 128, 128), 128)] = got[:, piece]
    for copy in sends:
        copy.wait_send()


def scratch():
    ch = 2048 // NQ
    shapes = {
        "kv": ((2, 16, 128, 128), BF16),
        "wb": ((2, 8, 512, 128), BF16),
        "res": ((2, 16, 2048), BF16),
        "res_give": ((16, 2048), BF16),
        "gain": ((1, 2048), F32),
        "bias": ((128, 2048), F32),
        "ab": ((2, 2, 128, 512), BF16),
        "px": ((4, 8, 2, 32, 128), BF16),
        "rx": ((4, 8, 2, 32, 128), BF16),
        "tot": ((8, 2, 32, 128), F32),
        "yo": ((8, 32, 128), BF16),
        "yi": ((8, 32, 128), BF16),
        "st": ((32, 2048), F32),
        "sq": ((2, 32, 128), F32),
        "mt": ((8, 2, 2, 8, 128), F32),
        "tables": ((2, 256, 128), F32),
        "sel": ((256, 384), BF16),
        "whi": ((256, 384), BF16),
        "wlo": ((256, 384), BF16),
        "xg": ((NQ, 8, 32, ch), BF16),
        "ys": ((NQ, 8, 48, ch), BF16),
        "yr": ((NQ, 8, 48, ch), BF16),
        "xo": ((NQ, 8, 48, ch), BF16),
        "raw_g": ((4096, 384), BF16),
        "raw_u": ((4096, 384), BF16),
        "raw_d": ((384, 4096), BF16),
        "deq_g": ((2, 2048, 384), BF16),
        "deq_u": ((2, 2048, 384), BF16),
        "deq_d": ((2, 384, 2048), BF16),
        "down_in": ((384, 2048), BF16),
        "hid": ((384, 384), BF16),
        "hid_in": ((384, 384), BF16),
        "es": ((NQ, 8, 48, ch), BF16),
        "er": ((NQ, 8, 48, ch), BF16),
        "comb": ((NQ, 8, 32, ch), F32),
        "back_out": ((NQ, 8, 32, ch), BF16),
        "back_in": ((NQ, 8, 32, ch), BF16),
        "fin": ((NQ, 2, 16, ch), BF16),
        "fin_in": ((NQ, 16, ch), BF16),
    }
    made = {name: pltpu.VMEM(*what) for name, what in shapes.items()}
    made["w_sem"] = pltpu.SemaphoreType.DMA((3,))
    copies = {
        "kv": (8,),
        "kva": (8,),
        "kvp": (2, 8),
        "mt": (8,),
        "mtp": (8,),
        "one": (6,),
        "wr": (4, 4),
        "wl": (4, 4),
        "a": (3,),
        "x": (len(GROUPS), 4),
        "y": (len(GROUPS),),
        "z": (NQ, 8),
        "pd": (NQ, 8),
        "fw": (NQ, 8),
        "ps": (NQ, 8),
        "b": (NQ, 8),
        "fn": (NQ,),
    }
    for name, shape in copies.items():
        made[name + "_s"] = pltpu.SemaphoreType.DMA(shape)
        made[name + "_r"] = pltpu.SemaphoreType.DMA(shape)
    return made


SCRATCH = tuple(scratch())


def layer(*operands):
    vmem = pl.BlockSpec(memory_space=pltpu.VMEM)
    smem = pl.BlockSpec(memory_space=pltpu.SMEM)
    hbm = pl.BlockSpec(memory_space=pl.ANY)
    return pl.pallas_call(
        layer_kernel,
        out_shape=jax.ShapeDtypeStruct((16, 4096), BF16),
        in_specs=[vmem] * 3 + [smem] * 3 + [vmem] * 5 + [hbm] * 3 + [smem] * 3,
        out_specs=vmem,
        scratch_shapes=list(scratch().values()),
        compiler_params=pltpu.CompilerParams(
            collective_id=1, has_side_effects=True, vmem_limit_bytes=58 * 1024 * 1024
        ),
        name="layer",
    )(*operands)


def shards(
    residual,
    encoded_query_rows,
    quantized_key_rows,
    quantized_value_rows,
    key_block_exponent,
    value_block_exponent,
    block_order,
    out_weight,
    norm_gain,
    expert_ids,
    route_weight,
    gate_weight,
    gate_scale,
    up_weight,
    up_scale,
    down_weight,
    down_scale,
):
    return layer(
        encoded_query_rows,
        quantized_key_rows,
        quantized_value_rows,
        key_block_exponent,
        value_block_exponent,
        block_order,
        out_weight,
        residual,
        norm_gain.reshape(1, -1),
        expert_ids.T,
        route_weight.T,
        gate_weight[0],
        up_weight[0],
        down_weight[0],
        gate_scale.transpose(2, 0, 1),
        up_scale.transpose(2, 0, 1),
        down_scale.transpose(1, 0, 2),
    )


def solution(mesh):
    return jax.shard_map(
        shards,
        mesh=mesh,
        in_specs=(
            P(("dp", "ctx", "exp"), None),
            P(("dp", "ctx"), "exp"),
            P(("dp", "ctx"), None),
            P(("dp", "ctx"), None),
            P(("dp", "ctx"), None),
            P(("dp", "ctx"), None),
            P(),
            P("exp", "ctx"),
            P(),
            P(("dp", "ctx", "exp"), None),
            P(("dp", "ctx", "exp"), None),
            P(("ctx", "exp"), None, None),
            P(("ctx", "exp"), None, None),
            P(("ctx", "exp"), None, None),
            P(("ctx", "exp"), None, None),
            P(("ctx", "exp"), None, None),
            P(("ctx", "exp"), None, None),
        ),
        out_specs=P(("dp", "ctx", "exp"), None),
        check_vma=False,
    )
```

```python
import math

import jax
import jax.numpy as jnp
from jax import lax
from jax.experimental import pallas as pl
from jax.experimental.pallas import tpu as pltpu
from jax.sharding import PartitionSpec as P

HEAD_SIZE = 128

MESH = pl.DeviceIdType.MESH
F32 = jnp.float32
BF16 = jnp.bfloat16
NQ = 4
OFFSETS = (0, 1, 7, 2, 6, 3, 5, 4)
GROUPS = ((0, 3), (3, 5), (5, 8))
PLANE = [(dx, dy) for dy in range(2) for dx in range(4)]


def contract_first(lhs, rhs):
    return lax.dot_general(lhs, rhs, (((0,), (0,)), ((), ())), preferred_element_type=F32)


def contract_last(lhs, rhs):
    return lax.dot_general(lhs, rhs, (((1,), (1,)), ((), ())), preferred_element_type=F32)


def mul(lhs, rhs):
    return jnp.dot(lhs, rhs, preferred_element_type=F32)


def remote(src, dst, send_sem, recv_sem, device):
    return pltpu.make_async_remote_copy(
        src_ref=src,
        dst_ref=dst,
        send_sem=send_sem,
        recv_sem=recv_sem,
        device_id=device,
        device_id_type=MESH,
    )


def hops(q):
    return (4, 3) if q % 2 == 0 else (3, 4)


class Place:
    def __init__(self):
        self.ctx = lax.axis_index("ctx")
        self.exp = lax.axis_index("exp")
        self.dp = lax.axis_index("dp")
        self.z = self.ctx % 8
        self.yh = self.ctx // 8
        self.x = self.exp // 2
        self.k = self.exp % 2
        self.plane = self.yh * 4 + self.x

    def at_ctx(self, i):
        return {"ctx": (self.ctx + i) % 16, "exp": self.exp, "dp": self.dp}

    def at_z(self, dz, dk=0):
        z = (self.z + dz) % 8
        k = (self.k + dk) % 2
        return {"ctx": self.yh * 8 + z, "exp": self.x * 2 + k, "dp": self.dp}

    def at_plane(self, dx, dy):
        x = (self.x + dx) % 4
        yh = (self.yh + dy) % 2
        dp = (self.dp + dy) % 2
        return {"ctx": yh * 8 + self.z, "exp": x * 2 + self.k, "dp": dp}, yh * 4 + x

    def plane_from(self, dx, dy):
        return ((self.yh + 2 - dy) % 2) * 4 + (self.x + 4 - dx) % 4

    def other_core(self):
        return {"ctx": self.ctx, "exp": self.x * 2 + (1 - self.k), "dp": self.dp}


def layer_kernel(
    q_ref,
    kq_ref,
    vq_ref,
    ke_ref,
    ve_ref,
    order_ref,
    w_ref,
    res_ref,
    gain_ref,
    ids_ref,
    rw_ref,
    gw_ref,
    uw_ref,
    dw_ref,
    gs_ref,
    us_ref,
    ds_ref,
    out_ref,
    *scratch_refs,
):
    r = dict(zip(SCRATCH, scratch_refs, strict=True))
    sem = {name[:-2]: (r[name], r[name[:-2] + "_r"]) for name in SCRATCH if name.endswith("_s")}
    me = Place()
    z, k, x, yh = me.z, me.k, me.x, me.yh
    partner = me.other_core()
    right, left = me.at_z(1), me.at_z(7)
    xg, st = r["xg"], r["st"]
    ch = xg.shape[-1]
    sends = []

    def start(copy):
        copy.start()
        sends.append(copy)

    def pair(name, *index):
        return sem[name][0].at[index], sem[name][1].at[index]

    shared = []

    def post(copy, *sent):
        copy.start()
        if sent:
            shared.append(sent)

    def shares(name, send, recv):
        return sem[name][0].at[send], sem[name][1].at[recv]

    def arrived(buf, name, recv):
        remote(buf, buf, *shares(name, 0, recv), partner).wait_recv()

    loads = [
        pltpu.make_async_copy(src, r[dst], r["w_sem"].at[i])
        for i, (src, dst) in enumerate(((gw_ref, "raw_g"), (uw_ref, "raw_u"), (dw_ref, "raw_d")))
    ]
    for load in loads:
        load.start()

    barrier = pltpu.get_barrier_semaphore()
    peers = [me.at_plane(dx, dy)[0] for dx, dy in PLANE[1:]]
    peers = peers + [partner, me.at_ctx(8)] + [me.at_z(i) for i in range(1, 8)]
    for peer in peers:
        pl.semaphore_signal(barrier, inc=1, device_id=peer, device_id_type=MESH)
    pl.semaphore_wait(barrier, len(peers))

    def gather(buf, name, q, step, rightward):
        block = (z + 8 - step) % 8 if rightward else (z + step) % 8
        sems = shares(name, 0, q * 8 + step * 2 + (0 if rightward else 1))
        return remote(buf(block), buf(block), *sems, right if rightward else left)

    def gathered(buf, name, q, step, rightward):
        block = (z + 7 - step) % 8 if rightward else (z + 1 + step) % 8
        arrived(buf(block), name, q * 8 + step * 2 + (0 if rightward else 1))

    def ring_start(buf, name, q):
        post(gather(buf, name, q, 0, True))
        post(gather(buf, name, q, 0, False))

    def ring_step(buf, name, q, step):
        for rightward, count in zip((True, False), hops(q)):
            if step <= count:
                gathered(buf, name, q, step - 1, rightward)
                if step < count:
                    post(gather(buf, name, q, step, rightward))

    kv = r["kv"]
    row = lax.broadcasted_iota(jnp.int32, (128, 128), 0)
    col = lax.broadcasted_iota(jnp.int32, (128, 128), 1)
    head = pl.ds(pl.multiple_of(x * 128, 128), 128)
    first = jnp.where(k == 0, ke_ref[0, x], ve_ref[0, x])
    second = jnp.where(k == 0, ke_ref[1, x], ve_ref[1, x])
    power = jnp.where(row < 64, first, second)
    factor = jnp.zeros((128, 128), F32)
    for p in range(-2, 2):
        factor = factor + jnp.where(power == p, 2.0**p, 0.0)
    mine = jnp.where(k == 0, kq_ref[:, head].astype(F32), vq_ref[:, head].astype(F32))
    kv[k, me.ctx] = (mine * factor).astype(BF16)

    def kv_at(offset, side, kind=k):
        return kv.at[kind, (yh if side == 0 else 1 - yh) * 8 + (z + offset) % 8]

    def kv_copy(offset):
        own = kv_at(0, 0)
        return remote(own, own, *shares("kv", 0, offset), me.at_z(offset))

    def kv_across(offset):
        at = kv_at(offset, 0)
        return remote(at, at, *shares("kva", 0, 0), me.at_ctx(8))

    def kv_side(side, kind):
        return kv.at[kind, pl.ds(pl.multiple_of((yh if side == 0 else 1 - yh) * 8, 8), 8)]

    def kv_pass(side):
        return remote(kv_side(side, k), kv_side(side, k), *pair("kvp", side), partner)

    for offset in (4, 3, 5, 2, 6, 1, 7):
        post(kv_copy(offset))
    post(kv_across(0))
    shared.append((kv.at[0, pl.ds(0, 7)], "kv", 0))
    shared.append((kv.at[0, pl.ds(0, 8)], "kva", 0))

    mt = r["mt"]
    mt[z, k] = jnp.zeros((2, 8, 128), F32)
    mt[z, k, 0, :, 0:16] = ids_ref[...].astype(F32)
    mt[z, k, 1, :, 0:16] = rw_ref[...]

    for offset in range(1, 8):
        post(remote(mt.at[z, k], mt.at[z, k], *shares("mt", 0, 0), me.at_z(offset)))
    shared.append((mt.at[pl.ds(0, 7), 0], "mt", 0))

    def mt_pass(core):
        return remote(mt.at[:, core], mt.at[:, core], *pair("one", 4), partner)

    wb = r["wb"]
    wb[k, z] = w_ref[:, pl.ds(pl.multiple_of(k * 128, 128), 128)]
    give = w_ref.at[:, pl.ds(pl.multiple_of((1 - k) * 128, 128), 128)]

    def w_block(q):
        core = k if q < 2 else 1 - k
        rows = pl.ds((q % 2) * 256, 256)
        return lambda block: wb.at[core, block, rows]

    def w_step(step, parts=range(4)):
        for q in parts:
            ring_step(w_block(q), "w", q, step)

    start(remote(give, wb.at[k, z], *pair("one", 2), partner))
    for q in range(2):
        ring_start(w_block(q), "w", q)

    res, res_give, gain = r["res"], r["res_give"], r["gain"]
    for c in range(16):
        to = slice(c * 128, (c + 1) * 128)
        own = pl.ds(pl.multiple_of(c * 256 + k * 128, 128), 128)
        other = pl.ds(pl.multiple_of(c * 256 + (1 - k) * 128, 128), 128)
        res[k, :, to] = res_ref[:, own]
        res_give[:, to] = res_ref[:, other]
        gain[:, to] = gain_ref[:, own]
    start(remote(res_give, res.at[k], *pair("one", 3), partner))

    def power_of(exponent):
        return jnp.where(exponent == 0, 1.0, jnp.where(exponent > 0, 2.0, 0.5))

    def scaled(raw, scale, deq, lo=0, hi=16):
        def body(c, carry):
            for half in range(2):
                side = k if half == 0 else 1 - k
                at = pl.ds(pl.multiple_of(c * 256 + side * 128, 128), 128)
                to = pl.ds(pl.multiple_of(c * 128, 128), 128)
                for b in range(3):
                    cols = slice(b * 128, (b + 1) * 128)
                    block = raw[at, cols].astype(F32) * power_of(scale[b, 0, c * 2 + side])
                    deq[half, to, cols] = block.astype(BF16)
            return carry

        lax.fori_loop(lo, hi, body, 0)

    def scaled_down(raw, scale, deq, lo=0, hi=16):
        def body(c, carry):
            for half in range(2):
                side = k if half == 0 else 1 - k
                at = pl.ds(pl.multiple_of(c * 256 + side * 128, 128), 128)
                to = pl.ds(pl.multiple_of(c * 128, 128), 128)
                for b in range(3):
                    rows = slice(b * 128, (b + 1) * 128)
                    block = raw[rows, at].astype(F32) * power_of(scale[b, 0, c * 2 + side])
                    deq[half, rows, to] = block.astype(BF16)
            return carry

        lax.fori_loop(lo, hi, body, 0)

    remote(give, wb.at[1 - k, z], *pair("one", 2), partner).wait_recv()
    for q in range(2, 4):
        ring_start(w_block(q), "w", q)
    shared.append((wb.at[:, pl.ds(0, 7)], "w", 0))

    bias = r["bias"]
    own_place = order_ref[me.ctx]
    for j in range(16):
        seen = order_ref[j] * 128 + col <= own_place * 128 + row
        bias[:, j * 128 : (j + 1) * 128] = jnp.where(seen, 0.0, -1e30)

    loads[0].wait()
    scaled(r["raw_g"], gs_ref, r["deq_g"])
    for offset in (1, 7, 2, 6, 3, 5, 4):
        arrived(kv_at(8 - offset, 0), "kv", offset)
        post(kv_across(8 - offset))
    start(kv_pass(0))
    w_step(1)
    arrived(mt.at[pl.ds(0, 7), k], "mt", 0)
    start(mt_pass(k))
    arrived(kv_side(1, k), "kva", 0)
    start(kv_pass(1))
    w_step(2, range(2))
    for side in range(2):
        remote(kv_side(side, 1 - k), kv_side(side, 1 - k), *pair("kvp", side), partner).wait_recv()

    ab = r["ab"]
    keys, values = kv[0].reshape(2048, 128), kv[1].reshape(2048, 128)
    over = me.at_plane(0, 1)[0]

    def a_part(core, side, n):
        return ab.at[core, yh if side == 0 else 1 - yh, :, pl.ds(n * 256, 256)]

    def a_start(n):
        own = a_part(k, 0, n)
        start(remote(own, own, *pair("a", n * 3 + 1), over))
        start(remote(own, own, *pair("a", n * 3), partner))

    for h in range(4):
        to = slice(h * 128, (h + 1) * 128)
        scores = contract_last(q_ref[:, to], keys) * (1.0 / math.sqrt(HEAD_SIZE) * math.log2(math.e))
        scores = scores + bias[...]
        exps = jnp.exp2(scores - jnp.max(scores, axis=1, keepdims=True))
        total = jnp.sum(exps, axis=1, keepdims=True)
        ab[k, yh, :, to] = (mul(exps.astype(BF16), values) / total).astype(BF16)
        if h == 0:
            w_step(2, range(2, 4))
        if h == 2:
            w_step(3, range(2))
        if h % 2 == 1:
            a_start(h // 2)
    w_step(3, range(2, 4))
    mt_pass(1 - k).wait_recv()
    tables = r["tables"]
    for n in range(16):
        for kind in range(2):
            block = jnp.transpose(mt[n // 2, n % 2, kind])
            tables[kind, n * 16 : (n + 1) * 16, 0:8] = block[0:16, :]
    ids, rw = tables[0], tables[1]
    slot = lax.broadcasted_iota(jnp.int32, (256, 384), 1)
    token = lax.broadcasted_iota(jnp.int32, (256, 384), 0)
    expert = slot // 48
    named = ((expert // 4) * 32 + z * 4 + expert % 4).astype(F32)
    member = jnp.zeros((256, 384), F32)
    weights = jnp.zeros((256, 384), F32)
    for n in range(8):
        hit = ids[:, n : n + 1] == named
        member = jnp.where(hit, 1.0, member)
        weights = jnp.where(hit, rw[:, n : n + 1], weights)
    first = lax.broadcasted_iota(jnp.int32, (256, 256), 0)
    second = lax.broadcasted_iota(jnp.int32, (256, 256), 1)
    earlier = (second < first) & (second // 16 == first // 16)
    number = mul(jnp.where(earlier, 1.0, 0.0).astype(BF16), member.astype(BF16))
    here = (number == (slot % 3).astype(F32)) & ((slot % 48) // 3 == token // 16)
    weights = jnp.where(here, weights, 0.0)
    select, weights_hi, weights_lo = r["sel"], r["whi"], r["wlo"]
    select[...] = jnp.where(here, member, 0.0).astype(BF16)
    weights_hi[...] = weights.astype(BF16)
    weights_lo[...] = (weights - weights.astype(BF16).astype(F32)).astype(BF16)

    for n in range(2):
        came = a_part(k, 1, n)
        remote(came, came, *pair("a", n * 3 + 1), over).wait_recv()
        start(remote(came, came, *pair("a", n * 3 + 2), partner))
    for n in range(2):
        for i in (0, 2):
            came = a_part(1 - k, i // 2, n)
            remote(came, came, *pair("a", n * 3 + i), partner).wait_recv()

    px, rx = r["px"], r["rx"]
    attended = [ab[core].reshape(256, 512) for core in range(2)]
    for g, (lo, hi) in enumerate(GROUPS):
        if g == len(GROUPS) - 1:
            loads[1].wait()
            scaled(r["raw_u"], us_ref, r["deq_u"])
            w_step(4)
        for n in range(lo, hi):
            at = (z + OFFSETS[n]) % 8
            part = mul(attended[0], wb[0, at]) + mul(attended[1], wb[1, at])
            part = part.astype(BF16).reshape(2, 4, 32, 128)
            for side in range(2):
                for to in range(4):
                    px[side * 4 + to, n] = part[side, to]
        cut = pl.ds(lo, hi - lo)
        for d in range(1, 8):
            device, there = me.at_plane(*PLANE[d])
            post(remote(px.at[there, cut], rx.at[d, cut], *pair("x", g), device))
        shared.append((rx.at[pl.ds(1, 7), cut], "x", g))

    remote(res_give, res.at[1 - k], *pair("one", 3), partner).wait_recv()
    for g, (lo, hi) in enumerate(GROUPS):
        arrived(rx.at[pl.ds(1, 7), pl.ds(lo, hi - lo)], "x", g)
        for n in range(lo, hi):
            for side in range(2):
                total = (px[me.plane, n] if side == 0 else rx[4, n]).astype(F32)
                for dx in range(1, 4):
                    total = total + rx[side * 4 + dx, n].astype(F32)
                at = ((yh if side == 0 else 1 - yh) * 8 + (z + OFFSETS[n]) % 8) * 128
                st[:, pl.ds(pl.multiple_of(at, 128), 128)] = total
    st[...] = st[...] + res[...].reshape(32, 2048).astype(F32)
    squares = jnp.sum(st[...] * st[...], axis=1, keepdims=True)
    r["sq"][0] = jnp.broadcast_to(squares, (32, 128))
    swap = remote(r["sq"].at[0], r["sq"].at[1], *pair("one", 5), partner)
    start(swap)
    swap.wait_recv()
    mean = (r["sq"][0, :, 0:1] + r["sq"][1, :, 0:1]) / 4096.0
    normed = (st[...] * lax.rsqrt(mean + 1e-6) * gain[...]).astype(BF16)

    for q in range(NQ):
        xg[q, z] = normed[:, q * ch : (q + 1) * ch]

    def z_copy(q, source, to):
        block = xg.at[q, (z + source) % 8]
        offset = (source - to) % 8
        sems = shares("z", q, q * 3 + {2: 1, 6: 2}.get(offset, 0))
        return remote(block, block, *sems, me.at_z(to % 8))

    def z_first(q):
        for to in (2, -2, 1, -1):
            post(z_copy(q, 0, to))
        shared.append((xg.at[q, pl.ds(0, 7)], "z", q))

    def z_second(q):
        for side in (1, -1):
            arrived(xg.at[q, (z + 8 - 2 * side) % 8], "z", q * 3 + (2 if side == 1 else 1))
            post(z_copy(q, -2 * side, side))
            if (side == 1) == (q % 2 == 0):
                post(z_copy(q, -2 * side, 2 * side))

    def to_plane(bufs, bufr, name, q, d):
        device, there = me.at_plane(*PLANE[d])
        return remote(bufs.at[q, there], bufr.at[q, me.plane], *pair(name, q), device)

    def plane_start(bufs, bufr, name, q):
        for d in range(1, 8):
            post(to_plane(bufs, bufr, name, q, d))
        shared.append((bufs.at[q, pl.ds(0, 7)], name, q))
        bufr[q, me.plane] = bufs[q, me.plane]

    def plane_end(bufr, name, q):
        arrived(bufr.at[q, pl.ds(0, 7)], name, q)

    ys, yr, xo = r["ys"], r["yr"], r["xo"]
    def pick(q):
        picked = contract_first(select[...], xg[q].reshape(256, ch)).astype(BF16)
        ys[q] = picked.reshape(8, 48, ch)
        plane_start(ys, yr, "pd", q)

    ahead = 2
    for q in range(min(ahead, NQ)):
        z_first(q)
    loads[2].wait()
    for turn in range(NQ + 1):
        if turn < NQ:
            if turn < 2:
                scaled_down(r["raw_d"], ds_ref, r["deq_d"], turn * 8, turn * 8 + 8)
            z_second(turn)
            if turn + ahead < NQ:
                z_first(turn + ahead)
        if turn:
            arrived(xg.at[turn - 1, pl.ds(0, 5)], "z", (turn - 1) * 3)
            pick(turn - 1)
    start(remote(r["deq_d"].at[1], r["down_in"], *pair("one", 0), partner))

    gate = jnp.zeros((384, 384), F32)
    up = jnp.zeros((384, 384), F32)
    for q in range(NQ):
        plane_end(yr, "pd", q)
        swap = remote(yr.at[q], xo.at[q], *pair("fw", q), partner)
        start(swap)
        swap.wait_recv()
        for half, rows in ((0, yr), (1, xo)):
            block = rows[q].reshape(384, ch)
            gate = gate + mul(block, r["deq_g"][half, q * ch : (q + 1) * ch, :])
            up = up + mul(block, r["deq_u"][half, q * ch : (q + 1) * ch, :])
    hid, hid_in = r["hid"], r["hid_in"]
    hid[...] = (gate / (1.0 + jnp.exp(-gate)) * up).astype(BF16)
    swap = remote(hid, hid_in, *pair("one", 1), partner)
    start(swap)
    remote(r["deq_d"].at[1], r["down_in"], *pair("one", 0), partner).wait_recv()
    swap.wait_recv()

    es, er = r["es"], r["er"]
    for q in range(NQ):
        cols = slice(q * ch, (q + 1) * ch)
        result = mul(hid[...], r["deq_d"][0, :, cols]) + mul(hid_in[...], r["down_in"][:, cols])
        es[q] = result.astype(BF16).reshape(8, 48, ch)
        plane_start(es, er, "ps", q)

    comb = r["comb"]

    towards = {1: 1, 7: -1, 3: 1, 5: -1, 2: 2, 6: -2}
    back_out, back_in = r["back_out"], r["back_in"]

    def back_kind(q, offset):
        if offset in (3, 5):
            return q * 3 + (1 if offset == 3 else 2)
        if offset == 4:
            return q * 3 + (1 if q % 2 == 0 else 2)
        return q * 3

    def back_slot(q, offset):
        return {3: 0, 5: 2, 4: 1, 1: 3, 7: 4, 2: 5, 6: 6}[offset]

    def back_start(q, offset, came=None):
        part = comb[q, (z + offset) % 8]
        if came is not None:
            lo, count = came
            arrived(back_in.at[q, pl.ds(lo, count)], "b", back_kind(q, 3 if offset == 2 else 5))
            for n in range(lo, lo + count):
                part = part + back_in[q, n].astype(F32)
        slot = back_slot(q, offset)
        back_out[q, slot] = part.astype(BF16)
        to = towards.get(offset, 2 if q % 2 == 0 else -2)
        sems = shares("b", q, back_kind(q, offset))
        post(remote(back_out.at[q, slot], back_in.at[q, slot], *sems, me.at_z(to % 8)))

    def back_second(q):
        back_start(q, 2, (0, 2) if q % 2 == 0 else (0, 1))
        back_start(q, 6, (2, 1) if q % 2 == 0 else (1, 2))
        shared.append((back_out.at[q, pl.ds(0, 7)], "b", q))

    fin, fin_in = r["fin"], r["fin_in"]
    for turn in range(NQ + 1):
        if turn < NQ:
            plane_end(er, "ps", turn)
            rows = er[turn].reshape(384, ch)
            total = mul(weights_hi[...], rows) + mul(weights_lo[...], rows)
            comb[turn] = total.reshape(8, 32, ch)
            for offset in (4, 3, 5, 1, 7):
                back_start(turn, offset)
        if turn:
            back_second(turn - 1)
    for q in range(NQ):
        total = comb[q, z] + st[:, q * ch : (q + 1) * ch]
        arrived(back_in.at[q, pl.ds(3, 4)], "b", q * 3)
        for n in range(3, 7):
            total = total + back_in[q, n].astype(F32)
        fin[q] = total.astype(BF16).reshape(2, 16, ch)
        start(remote(fin.at[q, 1 - k], fin_in.at[q], *pair("fn", q), partner))
    for q in range(NQ):
        remote(fin.at[q, 1 - k], fin_in.at[q], *pair("fn", q), partner).wait_recv()
        own, got = fin[q, k], fin_in[q]
        for c in range(ch // 128):
            at = (q * (ch // 128) + c) * 256
            piece = slice(c * 128, (c + 1) * 128)
            out_ref[:, pl.ds(pl.multiple_of(at + k * 128, 128), 128)] = own[:, piece]
            out_ref[:, pl.ds(pl.multiple_of(at + (1 - k) * 128, 128), 128)] = got[:, piece]
    for copy in sends:
        copy.wait_send()
    for buf, name, send in shared:
        remote(buf, buf, *shares(name, send, 0), partner).wait_send()


def scratch():
    ch = 2048 // NQ
    shapes = {
        "kv": ((2, 16, 128, 128), BF16),
        "wb": ((2, 8, 512, 128), BF16),
        "res": ((2, 16, 2048), BF16),
        "res_give": ((16, 2048), BF16),
        "gain": ((1, 2048), F32),
        "bias": ((128, 2048), F32),
        "ab": ((2, 2, 128, 512), BF16),
        "px": ((8, 8, 32, 128), BF16),
        "rx": ((8, 8, 32, 128), BF16),
        "st": ((32, 2048), F32),
        "sq": ((2, 32, 128), F32),
        "mt": ((8, 2, 2, 8, 128), F32),
        "tables": ((2, 256, 128), F32),
        "sel": ((256, 384), BF16),
        "whi": ((256, 384), BF16),
        "wlo": ((256, 384), BF16),
        "xg": ((NQ, 8, 32, ch), BF16),
        "ys": ((NQ, 8, 48, ch), BF16),
        "yr": ((NQ, 8, 48, ch), BF16),
        "xo": ((NQ, 8, 48, ch), BF16),
        "raw_g": ((4096, 384), BF16),
        "raw_u": ((4096, 384), BF16),
        "raw_d": ((384, 4096), BF16),
        "deq_g": ((2, 2048, 384), BF16),
        "deq_u": ((2, 2048, 384), BF16),
        "deq_d": ((2, 384, 2048), BF16),
        "down_in": ((384, 2048), BF16),
        "hid": ((384, 384), BF16),
        "hid_in": ((384, 384), BF16),
        "es": ((NQ, 8, 48, ch), BF16),
        "er": ((NQ, 8, 48, ch), BF16),
        "comb": ((NQ, 8, 32, ch), F32),
        "back_out": ((NQ, 8, 32, ch), BF16),
        "back_in": ((NQ, 8, 32, ch), BF16),
        "fin": ((NQ, 2, 16, ch), BF16),
        "fin_in": ((NQ, 16, ch), BF16),
    }
    made = {name: pltpu.VMEM(*what) for name, what in shapes.items()}
    made["w_sem"] = pltpu.SemaphoreType.DMA((3,))
    copies = {
        "kv": (1, 8),
        "kva": (1, 1),
        "kvp": (2, 2),
        "mt": (1, 1),
        "one": (7, 7),
        "w": (1, 32),
        "a": (6, 6),
        "x": (len(GROUPS), len(GROUPS)),
        "z": (NQ, 3 * NQ),
        "pd": (NQ, NQ),
        "fw": (NQ, NQ),
        "ps": (NQ, NQ),
        "b": (NQ, 3 * NQ),
        "fn": (NQ, NQ),
    }
    for name, (sent, received) in copies.items():
        made[name + "_s"] = pltpu.SemaphoreType.DMA((sent,))
        made[name + "_r"] = pltpu.SemaphoreType.DMA((received,))
    return made


SCRATCH = tuple(scratch())


def layer(*operands):
    vmem = pl.BlockSpec(memory_space=pltpu.VMEM)
    smem = pl.BlockSpec(memory_space=pltpu.SMEM)
    hbm = pl.BlockSpec(memory_space=pl.ANY)
    return pl.pallas_call(
        layer_kernel,
        out_shape=jax.ShapeDtypeStruct((16, 4096), BF16),
        in_specs=[vmem] * 3 + [smem] * 3 + [vmem] * 5 + [hbm] * 3 + [smem] * 3,
        out_specs=vmem,
        scratch_shapes=list(scratch().values()),
        compiler_params=pltpu.CompilerParams(
            collective_id=1, has_side_effects=True, vmem_limit_bytes=58 * 1024 * 1024
        ),
        name="layer",
    )(*operands)


def shards(
    residual,
    encoded_query_rows,
    quantized_key_rows,
    quantized_value_rows,
    key_block_exponent,
    value_block_exponent,
    block_order,
    out_weight,
    norm_gain,
    expert_ids,
    route_weight,
    gate_weight,
    gate_scale,
    up_weight,
    up_scale,
    down_weight,
    down_scale,
):
    return layer(
        encoded_query_rows,
        quantized_key_rows,
        quantized_value_rows,
        key_block_exponent,
        value_block_exponent,
        block_order,
        out_weight,
        residual,
        norm_gain.reshape(1, -1),
        expert_ids.T,
        route_weight.T,
        gate_weight[0],
        up_weight[0],
        down_weight[0],
        gate_scale.transpose(2, 0, 1),
        up_scale.transpose(2, 0, 1),
        down_scale.transpose(1, 0, 2),
    )


def solution(mesh):
    return jax.shard_map(
        shards,
        mesh=mesh,
        in_specs=(
            P(("dp", "ctx", "exp"), None),
            P(("dp", "ctx"), "exp"),
            P(("dp", "ctx"), None),
            P(("dp", "ctx"), None),
            P(("dp", "ctx"), None),
            P(("dp", "ctx"), None),
            P(),
            P("exp", "ctx"),
            P(),
            P(("dp", "ctx", "exp"), None),
            P(("dp", "ctx", "exp"), None),
            P(("ctx", "exp"), None, None),
            P(("ctx", "exp"), None, None),
            P(("ctx", "exp"), None, None),
            P(("ctx", "exp"), None, None),
            P(("ctx", "exp"), None, None),
            P(("ctx", "exp"), None, None),
        ),
        out_specs=P(("dp", "ctx", "exp"), None),
        check_vma=False,
    )
```

```python
import math

import jax
import jax.numpy as jnp
from jax import lax
from jax.experimental import pallas as pl
from jax.experimental.pallas import tpu as pltpu
from jax.sharding import PartitionSpec as P

HEAD_SIZE = 128

MESH = pl.DeviceIdType.MESH
F32 = jnp.float32
BF16 = jnp.bfloat16
NQ = 4
OFFSETS = (0, 1, 7, 2, 6, 3, 5, 4)
GROUPS = ((0, 3), (3, 5), (5, 8))
SLOTS = ((0, 1), (1, 2))
PLANE = [(dx, dy) for dy in range(2) for dx in range(4)]


def contract_last(lhs, rhs):
    return lax.dot_general(lhs, rhs, (((1,), (1,)), ((), ())), preferred_element_type=F32)


def mul(lhs, rhs):
    return jnp.dot(lhs, rhs, preferred_element_type=F32)


def remote(src, dst, send_sem, recv_sem, device):
    return pltpu.make_async_remote_copy(
        src_ref=src,
        dst_ref=dst,
        send_sem=send_sem,
        recv_sem=recv_sem,
        device_id=device,
        device_id_type=MESH,
    )


def hops(q):
    return (4, 3) if q % 2 == 0 else (3, 4)


class Place:
    def __init__(self):
        self.ctx = lax.axis_index("ctx")
        self.exp = lax.axis_index("exp")
        self.dp = lax.axis_index("dp")
        self.z = self.ctx % 8
        self.yh = self.ctx // 8
        self.x = self.exp // 2
        self.k = self.exp % 2
        self.plane = self.yh * 4 + self.x

    def at_ctx(self, i):
        return {"ctx": (self.ctx + i) % 16, "exp": self.exp, "dp": self.dp}

    def at_z(self, dz, dk=0):
        z = (self.z + dz) % 8
        k = (self.k + dk) % 2
        return {"ctx": self.yh * 8 + z, "exp": self.x * 2 + k, "dp": self.dp}

    def at_plane(self, dx, dy):
        x = (self.x + dx) % 4
        yh = (self.yh + dy) % 2
        dp = (self.dp + dy) % 2
        return {"ctx": yh * 8 + self.z, "exp": x * 2 + self.k, "dp": dp}, yh * 4 + x

    def plane_from(self, dx, dy):
        return ((self.yh + 2 - dy) % 2) * 4 + (self.x + 4 - dx) % 4

    def other_part(self):
        return {"ctx": self.ctx, "exp": self.exp, "dp": 1 - self.dp}

    def other_core(self):
        return {"ctx": self.ctx, "exp": self.x * 2 + (1 - self.k), "dp": self.dp}


def layer_kernel(
    q_ref,
    kq_ref,
    vq_ref,
    ke_ref,
    ve_ref,
    order_ref,
    w_ref,
    res_ref,
    gain_ref,
    ids_ref,
    rw_ref,
    gw_ref,
    uw_ref,
    dw_ref,
    gs_ref,
    us_ref,
    ds_ref,
    out_ref,
    *scratch_refs,
):
    r = dict(zip(SCRATCH, scratch_refs, strict=True))
    sem = {name[:-2]: (r[name], r[name[:-2] + "_r"]) for name in SCRATCH if name.endswith("_s")}
    me = Place()
    z, k, x, yh = me.z, me.k, me.x, me.yh
    partner = me.other_core()
    right, left = me.at_z(1), me.at_z(7)
    xg, st = r["xg"], r["st"]
    ch = xg.shape[-1]
    sends = []

    def start(copy):
        copy.start()
        sends.append(copy)

    def pair(name, *index):
        return sem[name][0].at[index], sem[name][1].at[index]

    shared = []

    def post(copy, *sent):
        copy.start()
        if sent:
            shared.append(sent)

    def shares(name, send, recv):
        return sem[name][0].at[send], sem[name][1].at[recv]

    def arrived(buf, name, recv):
        remote(buf, buf, *shares(name, 0, recv), partner).wait_recv()

    loads = [
        pltpu.make_async_copy(src, r[dst], r["w_sem"].at[i])
        for i, (src, dst) in enumerate(((gw_ref, "raw_g"), (uw_ref, "raw_u"), (dw_ref, "raw_d")))
    ]
    for load in loads:
        load.start()

    barrier = pltpu.get_barrier_semaphore()
    peers = [me.at_plane(dx, dy)[0] for dx, dy in PLANE[1:]]
    peers = peers + [partner, me.at_ctx(8), me.other_part()] + [me.at_z(i) for i in range(1, 8)]
    for peer in peers:
        pl.semaphore_signal(barrier, inc=1, device_id=peer, device_id_type=MESH)
    pl.semaphore_wait(barrier, len(peers))

    def gather(buf, name, q, step, rightward):
        block = (z + 8 - step) % 8 if rightward else (z + step) % 8
        sems = shares(name, q, q * 8 + step * 2 + (0 if rightward else 1))
        return remote(buf(block), buf(block), *sems, right if rightward else left)

    def gathered(buf, name, q, step, rightward):
        block = (z + 7 - step) % 8 if rightward else (z + 1 + step) % 8
        arrived(buf(block), name, q * 8 + step * 2 + (0 if rightward else 1))

    def ring_start(buf, name, q):
        post(gather(buf, name, q, 0, True))
        post(gather(buf, name, q, 0, False))

    def ring_step(buf, name, q, step):
        for rightward, count in zip((True, False), hops(q)):
            if step <= count:
                gathered(buf, name, q, step - 1, rightward)
                if step < count:
                    post(gather(buf, name, q, step, rightward))

    kv = r["kv"]
    row = lax.broadcasted_iota(jnp.int32, (128, 128), 0)
    col = lax.broadcasted_iota(jnp.int32, (128, 128), 1)
    head = pl.ds(pl.multiple_of(x * 128, 128), 128)
    first = jnp.where(k == 0, ke_ref[0, x], ve_ref[0, x])
    second = jnp.where(k == 0, ke_ref[1, x], ve_ref[1, x])
    power = jnp.where(row < 64, first, second)
    factor = jnp.zeros((128, 128), F32)
    for p in range(-2, 2):
        factor = factor + jnp.where(power == p, 2.0**p, 0.0)
    mine = jnp.where(k == 0, kq_ref[:, head].astype(F32), vq_ref[:, head].astype(F32))
    kv[k, me.ctx] = (mine * factor).astype(BF16)

    def kv_at(offset, side, kind=k):
        return kv.at[kind, (yh if side == 0 else 1 - yh) * 8 + (z + offset) % 8]

    def kv_copy(offset):
        own = kv_at(0, 0)
        return remote(own, own, *shares("kv", 0, offset), me.at_z(offset))

    def kv_across(offset):
        at = kv_at(offset, 0)
        return remote(at, at, *shares("kva", 0, 0), me.at_ctx(8))

    def kv_side(side, kind):
        return kv.at[kind, pl.ds(pl.multiple_of((yh if side == 0 else 1 - yh) * 8, 8), 8)]

    def kv_pass(side):
        return remote(kv_side(side, k), kv_side(side, k), *pair("kvp", side), partner)

    for offset in (4, 3, 5, 2, 6, 1, 7):
        post(kv_copy(offset))
    post(kv_across(0))
    shared.append((kv.at[0, pl.ds(0, 7)], "kv", 0))
    shared.append((kv.at[0, pl.ds(0, 8)], "kva", 0))

    mt = r["mt"]
    mt[z, k] = jnp.zeros((2, 8, 128), F32)
    mt[z, k, 0, :, 0:16] = ids_ref[...].astype(F32)
    mt[z, k, 1, :, 0:16] = rw_ref[...]

    for offset in range(1, 8):
        post(remote(mt.at[z, k], mt.at[z, k], *shares("mt", 0, 0), me.at_z(offset)))
    shared.append((mt.at[pl.ds(0, 7), 0], "mt", 0))

    def mt_pass(core):
        return remote(mt.at[:, core], mt.at[:, core], *pair("one", 4), partner)

    wb = r["wb"]
    wb[k, z] = w_ref[:, pl.ds(pl.multiple_of(k * 128, 128), 128)]
    give = w_ref.at[:, pl.ds(pl.multiple_of((1 - k) * 128, 128), 128)]

    def w_block(q):
        core = k if q < 2 else 1 - k
        rows = pl.ds(q * 256 if q < 2 else pl.multiple_of(me.dp * 256, 256), 256)
        return lambda block: wb.at[core, block, rows]

    def w_step(step, parts=range(3)):
        for q in parts:
            ring_step(w_block(q), "w", q, step)
            if q == 2:
                for offset in (8 - step, step) if step < 4 else (4,):
                    block = w_block(2)((z + offset) % 8)
                    post(remote(block, block, *shares("ws", 0, step), me.other_part()))

    def w_shared(step):
        arrived(wb.at[0, pl.ds(0, 2 if step < 4 else 1), pl.ds(0, 256)], "ws", step)

    start(remote(give, wb.at[k, z], *pair("one", 2), partner))
    for q in range(2):
        ring_start(w_block(q), "w", q)

    res, res_give, gain = r["res"], r["res_give"], r["gain"]
    for c in range(16):
        to = slice(c * 128, (c + 1) * 128)
        own = pl.ds(pl.multiple_of(c * 256 + k * 128, 128), 128)
        other = pl.ds(pl.multiple_of(c * 256 + (1 - k) * 128, 128), 128)
        res[k, :, to] = res_ref[:, own]
        res_give[:, to] = res_ref[:, other]
        gain[:, to] = gain_ref[:, own]
    start(remote(res_give, res.at[k], *pair("one", 3), partner))

    def power_of(exponent):
        return jnp.where(exponent == 0, 1.0, jnp.where(exponent > 0, 2.0, 0.5))

    def scaled(raw, scale, deq, lo=0, hi=16):
        def body(c, carry):
            for half in range(2):
                side = k if half == 0 else 1 - k
                at = pl.ds(pl.multiple_of(c * 256 + side * 128, 128), 128)
                to = pl.ds(pl.multiple_of(c * 128, 128), 128)
                for b in range(3):
                    cols = slice(b * 128, (b + 1) * 128)
                    block = raw[at, cols].astype(F32) * power_of(scale[b, 0, c * 2 + side])
                    deq[half, to, cols] = block.astype(BF16)
            return carry

        lax.fori_loop(lo, hi, body, 0)

    def scaled_down(raw, scale, deq, lo=0, hi=16):
        def body(c, carry):
            for half in range(2):
                side = k if half == 0 else 1 - k
                at = pl.ds(pl.multiple_of(c * 256 + side * 128, 128), 128)
                to = pl.ds(pl.multiple_of(c * 128, 128), 128)
                for b in range(3):
                    rows = slice(b * 128, (b + 1) * 128)
                    block = raw[rows, at].astype(F32) * power_of(scale[b, 0, c * 2 + side])
                    deq[half, rows, to] = block.astype(BF16)
            return carry

        lax.fori_loop(lo, hi, body, 0)

    remote(give, wb.at[1 - k, z], *pair("one", 2), partner).wait_recv()
    ring_start(w_block(2), "w", 2)
    for q in range(3):
        shared.append((wb.at[0, pl.ds(0, 7), pl.ds(0, 256)], "w", q))
    shared.append((wb.at[0, pl.ds(0, 7), pl.ds(0, 256)], "ws", 0))

    bias = r["bias"]
    own_place = order_ref[me.ctx]
    for j in range(16):
        seen = order_ref[j] * 128 + col <= own_place * 128 + row
        bias[:, j * 128 : (j + 1) * 128] = jnp.where(seen, 0.0, -1e30)

    loads[0].wait()
    scaled(r["raw_g"], gs_ref, r["deq_g"])
    for offset in (1, 7, 2, 6, 3, 5, 4):
        arrived(kv_at(8 - offset, 0), "kv", offset)
        post(kv_across(8 - offset))
    start(kv_pass(0))
    w_step(1)
    arrived(mt.at[pl.ds(0, 7), k], "mt", 0)
    start(mt_pass(k))
    arrived(kv_side(1, k), "kva", 0)
    start(kv_pass(1))
    w_step(2, range(2))
    for side in range(2):
        remote(kv_side(side, 1 - k), kv_side(side, 1 - k), *pair("kvp", side), partner).wait_recv()

    ab = r["ab"]
    keys, values = kv[0].reshape(2048, 128), kv[1].reshape(2048, 128)
    over = me.at_plane(0, 1)[0]

    def a_part(core, side, n):
        return ab.at[core, yh if side == 0 else 1 - yh, :, pl.ds(n * 256, 256)]

    def a_start(n):
        own = a_part(k, 0, n)
        start(remote(own, own, *pair("a", n * 3 + 1), over))
        start(remote(own, own, *pair("a", n * 3), partner))

    for h in range(4):
        to = slice(h * 128, (h + 1) * 128)
        scores = contract_last(q_ref[:, to], keys) * (1.0 / math.sqrt(HEAD_SIZE) * math.log2(math.e))
        scores = scores + bias[...]
        exps = jnp.exp2(scores - jnp.max(scores, axis=1, keepdims=True))
        total = jnp.sum(exps, axis=1, keepdims=True)
        ab[k, yh, :, to] = (mul(exps.astype(BF16), values) / total).astype(BF16)
        if h == 0:
            w_step(2, range(2, 3))
        if h == 2:
            w_step(3, range(2))
        if h % 2 == 1:
            a_start(h // 2)
    w_step(3, range(2, 3))
    mt_pass(1 - k).wait_recv()
    tables = r["tables"]
    for n in range(16):
        for kind in range(2):
            block = jnp.transpose(mt[n // 2, n % 2, kind])
            tables[kind, n * 16 : (n + 1) * 16, 0:8] = block[0:16, :]
    ids, rw = tables[0], tables[1]
    slot = lax.broadcasted_iota(jnp.int32, (256, 384), 1)
    token = lax.broadcasted_iota(jnp.int32, (256, 384), 0)
    expert = slot // 48
    named = ((expert // 4) * 32 + z * 4 + expert % 4).astype(F32)
    member = jnp.zeros((256, 384), F32)
    weights = jnp.zeros((256, 384), F32)
    for n in range(8):
        hit = ids[:, n : n + 1] == named
        member = jnp.where(hit, 1.0, member)
        weights = jnp.where(hit, rw[:, n : n + 1], weights)
    first = lax.broadcasted_iota(jnp.int32, (256, 256), 0)
    second = lax.broadcasted_iota(jnp.int32, (256, 256), 1)
    earlier = (second < first) & (second // 16 == first // 16)
    number = mul(jnp.where(earlier, 1.0, 0.0).astype(BF16), member.astype(BF16))
    here = (number == (slot % 48 // 16).astype(F32)) & (slot % 16 == token // 16)
    weights = jnp.where(here, weights, 0.0)
    select, weights_hi, weights_lo = r["sel"], r["whi"], r["wlo"]
    select[...] = jnp.transpose(jnp.where(here, member, 0.0)).astype(BF16)
    weights_hi[...] = weights.astype(BF16)
    weights_lo[...] = (weights - weights.astype(BF16).astype(F32)).astype(BF16)

    for n in range(2):
        came = a_part(k, 1, n)
        remote(came, came, *pair("a", n * 3 + 1), over).wait_recv()
        start(remote(came, came, *pair("a", n * 3 + 2), partner))
    for n in range(2):
        for i in (0, 2):
            came = a_part(1 - k, i // 2, n)
            remote(came, came, *pair("a", n * 3 + i), partner).wait_recv()

    px, rx = r["px"], r["rx"]
    attended = [ab[core].reshape(256, 512) for core in range(2)]
    for g, (lo, hi) in enumerate(GROUPS):
        if g == len(GROUPS) - 1:
            loads[1].wait()
            scaled(r["raw_u"], us_ref, r["deq_u"])
            w_step(4)
        for step in ((1,), (2,), (3, 4))[g]:
            w_shared(step)
        for n in range(lo, hi):
            at = (z + OFFSETS[n]) % 8
            part = mul(attended[0], wb[0, at]) + mul(attended[1], wb[1, at])
            part = part.astype(BF16).reshape(2, 4, 32, 128)
            for side in range(2):
                for to in range(4):
                    px[side * 4 + to, n] = part[side, to]
        cut = pl.ds(lo, hi - lo)
        for d in range(1, 8):
            device, there = me.at_plane(*PLANE[d])
            post(remote(px.at[there, cut], rx.at[d, cut], *pair("x", g), device))
        shared.append((rx.at[pl.ds(1, 7), cut], "x", g))

    remote(res_give, res.at[1 - k], *pair("one", 3), partner).wait_recv()
    for g, (lo, hi) in enumerate(GROUPS):
        arrived(rx.at[pl.ds(1, 7), pl.ds(lo, hi - lo)], "x", g)
        for n in range(lo, hi):
            for side in range(2):
                total = (px[me.plane, n] if side == 0 else rx[4, n]).astype(F32)
                for dx in range(1, 4):
                    total = total + rx[side * 4 + dx, n].astype(F32)
                at = ((yh if side == 0 else 1 - yh) * 8 + (z + OFFSETS[n]) % 8) * 128
                st[:, pl.ds(pl.multiple_of(at, 128), 128)] = total
    st[...] = st[...] + res[...].reshape(32, 2048).astype(F32)
    squares = jnp.sum(st[...] * st[...], axis=1, keepdims=True)
    r["sq"][0] = jnp.broadcast_to(squares, (32, 128))
    swap = remote(r["sq"].at[0], r["sq"].at[1], *pair("one", 5), partner)
    start(swap)
    swap.wait_recv()
    mean = (r["sq"][0, :, 0:1] + r["sq"][1, :, 0:1]) / 4096.0
    normed = (st[...] * lax.rsqrt(mean + 1e-6) * gain[...]).astype(BF16)

    for q in range(NQ):
        xg[q, z] = normed[:, q * ch : (q + 1) * ch]

    def z_copy(q, source, to):
        block = xg.at[q, (z + source) % 8]
        offset = (source - to) % 8
        sems = shares("z", q, q * 3 + {2: 1, 6: 2}.get(offset, 0))
        return remote(block, block, *sems, me.at_z(to % 8))

    def z_first(q):
        for to in (2, -2, 1, -1):
            post(z_copy(q, 0, to))
        shared.append((xg.at[q, pl.ds(0, 7)], "z", q))

    def z_second(q):
        for side in (1, -1):
            arrived(xg.at[q, (z + 8 - 2 * side) % 8], "z", q * 3 + (2 if side == 1 else 1))
            post(z_copy(q, -2 * side, side))
            if (side == 1) == (q % 2 == 0):
                post(z_copy(q, -2 * side, 2 * side))

    def plane_start(bufs, bufr, name, q, g):
        slots = pl.ds(*SLOTS[g])
        for d in range(1, 8):
            device, there = me.at_plane(*PLANE[d])
            src, dst = bufs.at[q, there, slots], bufr.at[q, me.plane, slots]
            post(remote(src, dst, *pair(name, q * 2 + g), device))
        shared.append((bufs.at[q, pl.ds(0, 7), slots], name, q * 2 + g))

    def plane_end(bufr, name, q, g):
        arrived(bufr.at[q, pl.ds(0, 7), pl.ds(*SLOTS[g])], name, q * 2 + g)

    ys, yr, xo = r["ys"], r["yr"], r["xo"]

    def pick(q):
        picked = mul(select[...], xg[q].reshape(256, ch)).astype(BF16)
        ys[q] = picked.reshape(8, 3, 16, ch)
        plane_start(ys, yr, "pd", q, 0)
        if q < NQ // 2:
            plane_start(ys, yr, "pd", q, 1)
        if q == NQ - 1:
            for late in range(NQ // 2, NQ):
                plane_start(ys, yr, "pd", late, 1)
        yr[q, me.plane] = ys[q, me.plane]

    ahead = 2
    for q in range(min(ahead, NQ)):
        z_first(q)
    loads[2].wait()
    for turn in range(NQ + 1):
        if turn < NQ:
            if turn < 2:
                scaled_down(r["raw_d"], ds_ref, r["deq_d"], turn * 8, turn * 8 + 8)
            z_second(turn)
            if turn + ahead < NQ:
                z_first(turn + ahead)
        if turn:
            arrived(xg.at[turn - 1, pl.ds(0, 5)], "z", (turn - 1) * 3)
            pick(turn - 1)
    start(remote(r["deq_d"].at[1], r["down_in"], *pair("one", 0), partner))

    es, er = r["es"], r["er"]

    def swap_rows(q, g):
        slots = pl.ds(*SLOTS[g])
        return remote(yr.at[q, :, slots], xo.at[q, :, slots], *pair("fw", q * 2 + g), partner)

    def swap_start(q, g):
        plane_end(yr, "pd", q, g)
        start(swap_rows(q, g))

    def hidden(g):
        lo, count = SLOTS[g]
        rows = 128 * count
        gate = jnp.zeros((rows, 384), F32)
        up = jnp.zeros((rows, 384), F32)
        for q in range(0 if g == 0 else NQ // 2, NQ - 1):
            swap_start(q, g)
        for q in range(NQ):
            if q == NQ - 1:
                swap_start(q, g)
                for early in range(NQ // 2 if g == 0 else 0):
                    swap_start(early, 1)
            swap_rows(q, g).wait_recv()
            cols = slice(q * ch, (q + 1) * ch)
            for half, buf in ((0, yr), (1, xo)):
                block = buf[q, :, lo : lo + count].reshape(rows, ch)
                gate = gate + mul(block, r["deq_g"][half, cols, :])
                up = up + mul(block, r["deq_u"][half, cols, :])
        r["hid%d" % g][...] = (gate / (1.0 + jnp.exp(-gate)) * up).astype(BF16)

    def results(g):
        lo, count = SLOTS[g]
        mine, came = r["hid%d" % g], r["hid_in%d" % g]
        swap = remote(mine, came, *pair("one", 1 + 5 * g), partner)
        start(swap)
        if g == 0:
            remote(r["deq_d"].at[1], r["down_in"], *pair("one", 0), partner).wait_recv()
        ahead = mul(mine[...], r["deq_d"][0, :, 0:ch])
        swap.wait_recv()
        for q in range(NQ):
            cols = slice(q * ch, (q + 1) * ch)
            result = ahead if q == 0 else mul(mine[...], r["deq_d"][0, :, cols])
            result = result + mul(came[...], r["down_in"][:, cols])
            es[q, :, lo : lo + count] = result.astype(BF16).reshape(8, count, 16, ch)
            plane_start(es, er, "ps", q, g)
            er[q, me.plane, lo : lo + count] = es[q, me.plane, lo : lo + count]

    for g in range(2):
        hidden(g)
        results(g)

    comb = r["comb"]

    towards = {1: 1, 7: -1, 3: 1, 5: -1, 2: 2, 6: -2}
    back_out, back_in = r["back_out"], r["back_in"]

    def back_kind(q, offset):
        if offset in (3, 5):
            return q * 3 + (1 if offset == 3 else 2)
        if offset == 4:
            return q * 3 + (1 if q % 2 == 0 else 2)
        return q * 3

    def back_slot(q, offset):
        return {3: 0, 5: 2, 4: 1, 1: 3, 7: 4, 2: 5, 6: 6}[offset]

    def back_start(q, offset, came=None):
        part = comb[q, (z + offset) % 8]
        if came is not None:
            lo, count = came
            arrived(back_in.at[q, pl.ds(lo, count)], "b", back_kind(q, 3 if offset == 2 else 5))
            for n in range(lo, lo + count):
                part = part + back_in[q, n].astype(F32)
        slot = back_slot(q, offset)
        back_out[q, slot] = part.astype(BF16)
        to = towards.get(offset, 2 if q % 2 == 0 else -2)
        sems = shares("b", q, back_kind(q, offset))
        post(remote(back_out.at[q, slot], back_in.at[q, slot], *sems, me.at_z(to % 8)))

    def back_second(q):
        back_start(q, 2, (0, 2) if q % 2 == 0 else (0, 1))
        back_start(q, 6, (2, 1) if q % 2 == 0 else (1, 2))
        shared.append((back_out.at[q, pl.ds(0, 7)], "b", q))

    fin, fin_in = r["fin"], r["fin_in"]
    for turn in range(NQ + 1):
        if turn < NQ:
            for g in range(2):
                plane_end(er, "ps", turn, g)
            rows = er[turn].reshape(384, ch)
            total = mul(weights_hi[...], rows) + mul(weights_lo[...], rows)
            comb[turn] = total.reshape(8, 32, ch)
            for offset in (4, 3, 5, 1, 7):
                back_start(turn, offset)
        if turn:
            back_second(turn - 1)
    for q in range(NQ):
        total = comb[q, z] + st[:, q * ch : (q + 1) * ch]
        arrived(back_in.at[q, pl.ds(3, 4)], "b", q * 3)
        for n in range(3, 7):
            total = total + back_in[q, n].astype(F32)
        fin[q] = total.astype(BF16).reshape(2, 16, ch)
        start(remote(fin.at[q, 1 - k], fin_in.at[q], *pair("fn", q), partner))
    for q in range(NQ):
        remote(fin.at[q, 1 - k], fin_in.at[q], *pair("fn", q), partner).wait_recv()
        own, got = fin[q, k], fin_in[q]
        for c in range(ch // 128):
            at = (q * (ch // 128) + c) * 256
            piece = slice(c * 128, (c + 1) * 128)
            out_ref[:, pl.ds(pl.multiple_of(at + k * 128, 128), 128)] = own[:, piece]
            out_ref[:, pl.ds(pl.multiple_of(at + (1 - k) * 128, 128), 128)] = got[:, piece]
    for copy in sends:
        copy.wait_send()
    for buf, name, send in shared:
        remote(buf, buf, *shares(name, send, 0), partner).wait_send()


def scratch():
    ch = 2048 // NQ
    shapes = {
        "kv": ((2, 16, 128, 128), BF16),
        "wb": ((2, 8, 512, 128), BF16),
        "res": ((2, 16, 2048), BF16),
        "res_give": ((16, 2048), BF16),
        "gain": ((1, 2048), F32),
        "bias": ((128, 2048), F32),
        "ab": ((2, 2, 128, 512), BF16),
        "px": ((8, 8, 32, 128), BF16),
        "rx": ((8, 8, 32, 128), BF16),
        "st": ((32, 2048), F32),
        "sq": ((2, 32, 128), F32),
        "mt": ((8, 2, 2, 8, 128), F32),
        "tables": ((2, 256, 128), F32),
        "sel": ((384, 256), BF16),
        "whi": ((256, 384), BF16),
        "wlo": ((256, 384), BF16),
        "xg": ((NQ, 8, 32, ch), BF16),
        "ys": ((NQ, 8, 3, 16, ch), BF16),
        "yr": ((NQ, 8, 3, 16, ch), BF16),
        "xo": ((NQ, 8, 3, 16, ch), BF16),
        "raw_g": ((4096, 384), BF16),
        "raw_u": ((4096, 384), BF16),
        "raw_d": ((384, 4096), BF16),
        "deq_g": ((2, 2048, 384), BF16),
        "deq_u": ((2, 2048, 384), BF16),
        "deq_d": ((2, 384, 2048), BF16),
        "down_in": ((384, 2048), BF16),
        "hid0": ((128, 384), BF16),
        "hid_in0": ((128, 384), BF16),
        "hid1": ((256, 384), BF16),
        "hid_in1": ((256, 384), BF16),
        "es": ((NQ, 8, 3, 16, ch), BF16),
        "er": ((NQ, 8, 3, 16, ch), BF16),
        "comb": ((NQ, 8, 32, ch), F32),
        "back_out": ((NQ, 8, 32, ch), BF16),
        "back_in": ((NQ, 8, 32, ch), BF16),
        "fin": ((NQ, 2, 16, ch), BF16),
        "fin_in": ((NQ, 16, ch), BF16),
    }
    made = {name: pltpu.VMEM(*what) for name, what in shapes.items()}
    made["w_sem"] = pltpu.SemaphoreType.DMA((3,))
    copies = {
        "kv": (1, 8),
        "kva": (1, 1),
        "kvp": (2, 2),
        "mt": (1, 1),
        "one": (7, 7),
        "w": (3, 24),
        "ws": (1, 5),
        "a": (6, 6),
        "x": (len(GROUPS), len(GROUPS)),
        "z": (NQ, 3 * NQ),
        "pd": (2 * NQ, 2 * NQ),
        "fw": (2 * NQ, 2 * NQ),
        "ps": (2 * NQ, 2 * NQ),
        "b": (NQ, 3 * NQ),
        "fn": (NQ, NQ),
    }
    for name, (sent, received) in copies.items():
        made[name + "_s"] = pltpu.SemaphoreType.DMA((sent,))
        made[name + "_r"] = pltpu.SemaphoreType.DMA((received,))
    return made


SCRATCH = tuple(scratch())


def layer(*operands):
    vmem = pl.BlockSpec(memory_space=pltpu.VMEM)
    smem = pl.BlockSpec(memory_space=pltpu.SMEM)
    hbm = pl.BlockSpec(memory_space=pl.ANY)
    return pl.pallas_call(
        layer_kernel,
        out_shape=jax.ShapeDtypeStruct((16, 4096), BF16),
        in_specs=[vmem] * 3 + [smem] * 3 + [vmem] * 5 + [hbm] * 3 + [smem] * 3,
        out_specs=vmem,
        scratch_shapes=list(scratch().values()),
        compiler_params=pltpu.CompilerParams(
            collective_id=1, has_side_effects=True, vmem_limit_bytes=58 * 1024 * 1024
        ),
        name="layer",
    )(*operands)


def shards(
    residual,
    encoded_query_rows,
    quantized_key_rows,
    quantized_value_rows,
    key_block_exponent,
    value_block_exponent,
    block_order,
    out_weight,
    norm_gain,
    expert_ids,
    route_weight,
    gate_weight,
    gate_scale,
    up_weight,
    up_scale,
    down_weight,
    down_scale,
):
    return layer(
        encoded_query_rows,
        quantized_key_rows,
        quantized_value_rows,
        key_block_exponent,
        value_block_exponent,
        block_order,
        out_weight,
        residual,
        norm_gain.reshape(1, -1),
        expert_ids.T,
        route_weight.T,
        gate_weight[0],
        up_weight[0],
        down_weight[0],
        gate_scale.transpose(2, 0, 1),
        up_scale.transpose(2, 0, 1),
        down_scale.transpose(1, 0, 2),
    )


def solution(mesh):
    return jax.shard_map(
        shards,
        mesh=mesh,
        in_specs=(
            P(("dp", "ctx", "exp"), None),
            P(("dp", "ctx"), "exp"),
            P(("dp", "ctx"), None),
            P(("dp", "ctx"), None),
            P(("dp", "ctx"), None),
            P(("dp", "ctx"), None),
            P(),
            P("exp", "ctx"),
            P(),
            P(("dp", "ctx", "exp"), None),
            P(("dp", "ctx", "exp"), None),
            P(("ctx", "exp"), None, None),
            P(("ctx", "exp"), None, None),
            P(("ctx", "exp"), None, None),
            P(("ctx", "exp"), None, None),
            P(("ctx", "exp"), None, None),
            P(("ctx", "exp"), None, None),
        ),
        out_specs=P(("dp", "ctx", "exp"), None),
        check_vma=False,
    )
```

```python
import math

import jax
import jax.numpy as jnp
from jax import lax
from jax.experimental import pallas as pl
from jax.experimental.pallas import tpu as pltpu
from jax.sharding import PartitionSpec as P

HEAD_SIZE = 128

MESH = pl.DeviceIdType.MESH
F32 = jnp.float32
BF16 = jnp.bfloat16
NQ = 4
OFFSETS = (0, 1, 7, 2, 6, 3, 5, 4)
GROUPS = ((0, 3), (3, 5), (5, 8))
SLOTS = ((0, 1), (1, 2))
PLANE = [(dx, dy) for dy in range(2) for dx in range(4)]


def contract_last(lhs, rhs):
    return lax.dot_general(lhs, rhs, (((1,), (1,)), ((), ())), preferred_element_type=F32)


def mul(lhs, rhs):
    return jnp.dot(lhs, rhs, preferred_element_type=F32)


def remote(src, dst, send_sem, recv_sem, device):
    return pltpu.make_async_remote_copy(
        src_ref=src,
        dst_ref=dst,
        send_sem=send_sem,
        recv_sem=recv_sem,
        device_id=device,
        device_id_type=MESH,
    )


def hops(q):
    return (4, 3) if q % 2 == 0 else (3, 4)


class Place:
    def __init__(self):
        self.ctx = lax.axis_index("ctx")
        self.exp = lax.axis_index("exp")
        self.dp = lax.axis_index("dp")
        self.z = self.ctx % 8
        self.yh = self.ctx // 8
        self.x = self.exp // 2
        self.k = self.exp % 2
        self.plane = self.yh * 4 + self.x

    def at_ctx(self, i):
        return {"ctx": (self.ctx + i) % 16, "exp": self.exp, "dp": self.dp}

    def at_z(self, dz, dk=0):
        z = (self.z + dz) % 8
        k = (self.k + dk) % 2
        return {"ctx": self.yh * 8 + z, "exp": self.x * 2 + k, "dp": self.dp}

    def at_plane(self, dx, dy):
        x = (self.x + dx) % 4
        yh = (self.yh + dy) % 2
        dp = (self.dp + dy) % 2
        return {"ctx": yh * 8 + self.z, "exp": x * 2 + self.k, "dp": dp}, yh * 4 + x

    def plane_from(self, dx, dy):
        return ((self.yh + 2 - dy) % 2) * 4 + (self.x + 4 - dx) % 4

    def other_part(self):
        return {"ctx": self.ctx, "exp": self.exp, "dp": 1 - self.dp}

    def other_core(self):
        return {"ctx": self.ctx, "exp": self.x * 2 + (1 - self.k), "dp": self.dp}


def layer_kernel(
    q_ref,
    kq_ref,
    vq_ref,
    ke_ref,
    ve_ref,
    order_ref,
    w_ref,
    res_ref,
    gain_ref,
    ids_ref,
    rw_ref,
    gw_ref,
    uw_ref,
    dw_ref,
    gs_ref,
    us_ref,
    ds_ref,
    out_ref,
    *scratch_refs,
):
    r = dict(zip(SCRATCH, scratch_refs, strict=True))
    sem = {name[:-2]: (r[name], r[name[:-2] + "_r"]) for name in SCRATCH if name.endswith("_s")}
    me = Place()
    z, k, x, yh = me.z, me.k, me.x, me.yh
    partner = me.other_core()
    right, left = me.at_z(1), me.at_z(7)
    xg, st = r["xg"], r["st"]
    ch = xg.shape[-1]
    sends = []

    def start(copy):
        copy.start()
        sends.append(copy)

    def pair(name, *index):
        return sem[name][0].at[index], sem[name][1].at[index]

    shared = []

    def post(copy, *sent):
        copy.start()
        if sent:
            shared.append(sent)

    def shares(name, send, recv):
        return sem[name][0].at[send], sem[name][1].at[recv]

    def arrived(buf, name, recv):
        remote(buf, buf, *shares(name, 0, recv), partner).wait_recv()

    loads = [
        pltpu.make_async_copy(src, r[dst], r["w_sem"].at[i])
        for i, (src, dst) in enumerate(((gw_ref, "raw_g"), (uw_ref, "raw_u"), (dw_ref, "raw_d")))
    ]
    for load in loads:
        load.start()

    barrier = pltpu.get_barrier_semaphore()
    peers = [me.at_plane(dx, dy)[0] for dx, dy in PLANE[1:]]
    peers = peers + [partner, me.at_ctx(8), me.other_part()] + [me.at_z(i) for i in range(1, 8)]
    for peer in peers:
        pl.semaphore_signal(barrier, inc=1, device_id=peer, device_id_type=MESH)
    pl.semaphore_wait(barrier, len(peers))

    def gather(buf, name, q, step, rightward):
        block = (z + 8 - step) % 8 if rightward else (z + step) % 8
        sems = shares(name, q, q * 8 + step * 2 + (0 if rightward else 1))
        return remote(buf(block), buf(block), *sems, right if rightward else left)

    def gathered(buf, name, q, step, rightward):
        block = (z + 7 - step) % 8 if rightward else (z + 1 + step) % 8
        arrived(buf(block), name, q * 8 + step * 2 + (0 if rightward else 1))

    def ring_start(buf, name, q):
        post(gather(buf, name, q, 0, True))
        post(gather(buf, name, q, 0, False))

    def ring_step(buf, name, q, step):
        for rightward, count in zip((True, False), hops(q)):
            if step <= count:
                gathered(buf, name, q, step - 1, rightward)
                if step < count:
                    post(gather(buf, name, q, step, rightward))

    kv = r["kv"]
    row = lax.broadcasted_iota(jnp.int32, (128, 128), 0)
    col = lax.broadcasted_iota(jnp.int32, (128, 128), 1)
    head = pl.ds(pl.multiple_of(x * 128, 128), 128)
    first = jnp.where(k == 0, ke_ref[0, x], ve_ref[0, x])
    second = jnp.where(k == 0, ke_ref[1, x], ve_ref[1, x])
    power = jnp.where(row < 64, first, second)
    factor = jnp.zeros((128, 128), F32)
    for p in range(-2, 2):
        factor = factor + jnp.where(power == p, 2.0**p, 0.0)
    mine = jnp.where(k == 0, kq_ref[:, head].astype(F32), vq_ref[:, head].astype(F32))
    kv[k, me.ctx] = (mine * factor).astype(BF16)

    def kv_at(offset, side, kind=k):
        return kv.at[kind, (yh if side == 0 else 1 - yh) * 8 + (z + offset) % 8]

    def kv_copy(offset):
        own = kv_at(0, 0)
        return remote(own, own, *shares("kv", 0, offset), me.at_z(offset))

    def kv_across(offset):
        at = kv_at(offset, 0)
        return remote(at, at, *shares("kva", 0, 0), me.at_ctx(8))

    def kv_side(side, kind):
        return kv.at[kind, pl.ds(pl.multiple_of((yh if side == 0 else 1 - yh) * 8, 8), 8)]

    def kv_pass(side):
        return remote(kv_side(side, k), kv_side(side, k), *pair("kvp", side), partner)

    for offset in (4, 3, 5, 2, 6, 1, 7):
        post(kv_copy(offset))
    post(kv_across(0))
    shared.append((kv.at[0, pl.ds(0, 7)], "kv", 0))
    shared.append((kv.at[0, pl.ds(0, 8)], "kva", 0))

    mt = r["mt"]
    mt[z, k] = jnp.zeros((2, 8, 128), F32)
    mt[z, k, 0, :, 0:16] = ids_ref[...].astype(F32)
    mt[z, k, 1, :, 0:16] = rw_ref[...]

    for offset in range(1, 8):
        post(remote(mt.at[z, k], mt.at[z, k], *shares("mt", 0, 0), me.at_z(offset)))
    shared.append((mt.at[pl.ds(0, 7), 0], "mt", 0))

    def mt_pass(core):
        return remote(mt.at[:, core], mt.at[:, core], *pair("one", 4), partner)

    wb = r["wb"]
    wb[k, z] = w_ref[:, pl.ds(pl.multiple_of(k * 128, 128), 128)]
    give = w_ref.at[:, pl.ds(pl.multiple_of((1 - k) * 128, 128), 128)]

    def w_block(q):
        core = k if q < 2 else 1 - k
        rows = pl.ds(q * 256 if q < 2 else pl.multiple_of(me.dp * 256, 256), 256)
        return lambda block: wb.at[core, block, rows]

    def w_step(step, parts=range(3)):
        for q in parts:
            ring_step(w_block(q), "w", q, step)
            if q == 2:
                for offset in (8 - step, step) if step < 4 else (4,):
                    block = w_block(2)((z + offset) % 8)
                    post(remote(block, block, *shares("ws", 0, step), me.other_part()))

    def w_shared(step):
        arrived(wb.at[0, pl.ds(0, 2 if step < 4 else 1), pl.ds(0, 256)], "ws", step)

    start(remote(give, wb.at[k, z], *pair("one", 2), partner))
    for q in range(2):
        ring_start(w_block(q), "w", q)

    res, res_give, gain = r["res"], r["res_give"], r["gain"]
    for c in range(16):
        to = slice(c * 128, (c + 1) * 128)
        own = pl.ds(pl.multiple_of(c * 256 + k * 128, 128), 128)
        other = pl.ds(pl.multiple_of(c * 256 + (1 - k) * 128, 128), 128)
        res[k, :, to] = res_ref[:, own]
        res_give[:, to] = res_ref[:, other]
        gain[:, to] = gain_ref[:, own]
    start(remote(res_give, res.at[k], *pair("one", 3), partner))

    def power_of(exponent):
        return jnp.where(exponent == 0, 1.0, jnp.where(exponent > 0, 2.0, 0.5))

    def scaled(raw, scale, deq, lo=0, hi=16):
        def body(c, carry):
            for half in range(2):
                side = k if half == 0 else 1 - k
                at = pl.ds(pl.multiple_of(c * 256 + side * 128, 128), 128)
                to = pl.ds(pl.multiple_of(c * 128, 128), 128)
                for b in range(3):
                    cols = slice(b * 128, (b + 1) * 128)
                    block = raw[at, cols].astype(F32) * power_of(scale[b, 0, c * 2 + side])
                    deq[half, to, cols] = block.astype(BF16)
            return carry

        lax.fori_loop(lo, hi, body, 0)

    def scaled_down(raw, scale, deq, lo=0, hi=16):
        def body(c, carry):
            for half in range(2):
                side = k if half == 0 else 1 - k
                at = pl.ds(pl.multiple_of(c * 256 + side * 128, 128), 128)
                to = pl.ds(pl.multiple_of(c * 128, 128), 128)
                for b in range(3):
                    rows = slice(b * 128, (b + 1) * 128)
                    block = raw[rows, at].astype(F32) * power_of(scale[b, 0, c * 2 + side])
                    deq[half, rows, to] = block.astype(BF16)
            return carry

        lax.fori_loop(lo, hi, body, 0)

    remote(give, wb.at[1 - k, z], *pair("one", 2), partner).wait_recv()
    ring_start(w_block(2), "w", 2)
    for q in range(3):
        shared.append((wb.at[0, pl.ds(0, 7), pl.ds(0, 256)], "w", q))
    shared.append((wb.at[0, pl.ds(0, 7), pl.ds(0, 256)], "ws", 0))

    bias = r["bias"]
    own_place = order_ref[me.ctx]
    for j in range(16):
        seen = order_ref[j] * 128 + col <= own_place * 128 + row
        bias[:, j * 128 : (j + 1) * 128] = jnp.where(seen, 0.0, -1e30)

    loads[0].wait()
    scaled(r["raw_g"], gs_ref, r["deq_g"])
    for offset in (1, 7, 2, 6, 3, 5, 4):
        arrived(kv_at(8 - offset, 0), "kv", offset)
        post(kv_across(8 - offset))
    start(kv_pass(0))
    w_step(1)
    arrived(mt.at[pl.ds(0, 7), k], "mt", 0)
    start(mt_pass(k))
    acc, top, norm = r["acc"], r["top"], r["norm"]

    def kv_passed(side):
        came = kv_side(side, 1 - k)
        remote(came, came, *pair("kvp", side), partner).wait_recv()

    def attend(h, side):
        block = yh if side == 0 else 1 - yh
        at = pl.ds(pl.multiple_of(block * 8, 8), 8)
        keys, values = kv[0, at].reshape(1024, 128), kv[1, at].reshape(1024, 128)
        scale = 1.0 / math.sqrt(HEAD_SIZE) * math.log2(math.e)
        scores = contract_last(q_ref[:, h * 128 : (h + 1) * 128], keys) * scale
        scores = scores + bias[:, pl.ds(pl.multiple_of(block * 1024, 1024), 1024)]
        high = jnp.max(scores, axis=1, keepdims=True)
        exps = jnp.exp2(scores - high)
        return high, jnp.sum(exps, axis=1, keepdims=True), mul(exps.astype(BF16), values)

    kv_passed(0)
    for h in range(4):
        high, total, mixed = attend(h, 0)
        top[h] = jnp.broadcast_to(high, (128, 128))
        norm[h] = jnp.broadcast_to(total, (128, 128))
        acc[h] = mixed
    arrived(kv_side(1, k), "kva", 0)
    start(kv_pass(1))
    w_step(2, range(2))
    kv_passed(1)

    ab = r["ab"]
    over = me.at_plane(0, 1)[0]

    def a_part(core, side, n):
        return ab.at[core, yh if side == 0 else 1 - yh, :, pl.ds(n * 256, 256)]

    def a_start(n):
        own = a_part(k, 0, n)
        start(remote(own, own, *pair("a", n * 3 + 1), over))
        start(remote(own, own, *pair("a", n * 3), partner))

    for h in range(4):
        to = slice(h * 128, (h + 1) * 128)
        high, total, mixed = attend(h, 1)
        both = jnp.maximum(top[h], high)
        old, new = jnp.exp2(top[h] - both), jnp.exp2(high - both)
        total = norm[h] * old + total * new
        ab[k, yh, :, to] = ((acc[h] * old + mixed * new) / total).astype(BF16)
        if h == 0:
            w_step(2, range(2, 3))
        if h == 2:
            w_step(3, range(2))
        if h % 2 == 1:
            a_start(h // 2)
    w_step(3, range(2, 3))
    mt_pass(1 - k).wait_recv()
    tables = r["tables"]
    for n in range(16):
        for kind in range(2):
            block = jnp.transpose(mt[n // 2, n % 2, kind])
            tables[kind, n * 16 : (n + 1) * 16, 0:8] = block[0:16, :]
    ids, rw = tables[0], tables[1]
    slot = lax.broadcasted_iota(jnp.int32, (256, 384), 1)
    token = lax.broadcasted_iota(jnp.int32, (256, 384), 0)
    expert = slot // 48
    named = ((expert // 4) * 32 + z * 4 + expert % 4).astype(F32)
    member = jnp.zeros((256, 384), F32)
    weights = jnp.zeros((256, 384), F32)
    for n in range(8):
        hit = ids[:, n : n + 1] == named
        member = jnp.where(hit, 1.0, member)
        weights = jnp.where(hit, rw[:, n : n + 1], weights)
    first = lax.broadcasted_iota(jnp.int32, (256, 256), 0)
    second = lax.broadcasted_iota(jnp.int32, (256, 256), 1)
    earlier = (second < first) & (second // 16 == first // 16)
    number = mul(jnp.where(earlier, 1.0, 0.0).astype(BF16), member.astype(BF16))
    here = (number == (slot % 48 // 16).astype(F32)) & (slot % 16 == token // 16)
    weights = jnp.where(here, weights, 0.0)
    select, weights_hi, weights_lo = r["sel"], r["whi"], r["wlo"]
    select[...] = jnp.transpose(jnp.where(here, member, 0.0)).astype(BF16)
    weights_hi[...] = weights.astype(BF16)
    weights_lo[...] = (weights - weights.astype(BF16).astype(F32)).astype(BF16)

    for n in range(2):
        came = a_part(k, 1, n)
        remote(came, came, *pair("a", n * 3 + 1), over).wait_recv()
        start(remote(came, came, *pair("a", n * 3 + 2), partner))
    for n in range(2):
        for i in (0, 2):
            came = a_part(1 - k, i // 2, n)
            remote(came, came, *pair("a", n * 3 + i), partner).wait_recv()

    px, rx = r["px"], r["rx"]
    attended = [ab[core].reshape(256, 512) for core in range(2)]
    for g, (lo, hi) in enumerate(GROUPS):
        if g == len(GROUPS) - 1:
            loads[1].wait()
            scaled(r["raw_u"], us_ref, r["deq_u"])
            w_step(4)
        for step in ((1,), (2,), (3, 4))[g]:
            w_shared(step)
        for n in range(lo, hi):
            at = (z + OFFSETS[n]) % 8
            part = mul(attended[0], wb[0, at]) + mul(attended[1], wb[1, at])
            part = part.astype(BF16).reshape(2, 4, 32, 128)
            for side in range(2):
                for to in range(4):
                    px[side * 4 + to, n] = part[side, to]
        cut = pl.ds(lo, hi - lo)
        for d in range(1, 8):
            device, there = me.at_plane(*PLANE[d])
            post(remote(px.at[there, cut], rx.at[d, cut], *pair("x", g), device))
        shared.append((rx.at[pl.ds(1, 7), cut], "x", g))

    remote(res_give, res.at[1 - k], *pair("one", 3), partner).wait_recv()
    for g, (lo, hi) in enumerate(GROUPS):
        arrived(rx.at[pl.ds(1, 7), pl.ds(lo, hi - lo)], "x", g)
        for n in range(lo, hi):
            for side in range(2):
                total = (px[me.plane, n] if side == 0 else rx[4, n]).astype(F32)
                for dx in range(1, 4):
                    total = total + rx[side * 4 + dx, n].astype(F32)
                at = ((yh if side == 0 else 1 - yh) * 8 + (z + OFFSETS[n]) % 8) * 128
                st[:, pl.ds(pl.multiple_of(at, 128), 128)] = total
    st[...] = st[...] + res[...].reshape(32, 2048).astype(F32)
    squares = jnp.sum(st[...] * st[...], axis=1, keepdims=True)
    r["sq"][0] = jnp.broadcast_to(squares, (32, 128))
    swap = remote(r["sq"].at[0], r["sq"].at[1], *pair("one", 5), partner)
    start(swap)
    swap.wait_recv()
    mean = (r["sq"][0, :, 0:1] + r["sq"][1, :, 0:1]) / 4096.0
    normed = (st[...] * lax.rsqrt(mean + 1e-6) * gain[...]).astype(BF16)

    for q in range(NQ):
        xg[q, z] = normed[:, q * ch : (q + 1) * ch]

    def z_copy(q, source, to):
        block = xg.at[q, (z + source) % 8]
        offset = (source - to) % 8
        sems = shares("z", q, q * 3 + {2: 1, 6: 2}.get(offset, 0))
        return remote(block, block, *sems, me.at_z(to % 8))

    def z_first(q):
        for to in (2, -2, 1, -1):
            post(z_copy(q, 0, to))
        shared.append((xg.at[q, pl.ds(0, 7)], "z", q))

    def z_second(q):
        for side in (1, -1):
            arrived(xg.at[q, (z + 8 - 2 * side) % 8], "z", q * 3 + (2 if side == 1 else 1))
            post(z_copy(q, -2 * side, side))
            if (side == 1) == (q % 2 == 0):
                post(z_copy(q, -2 * side, 2 * side))

    def plane_start(bufs, bufr, name, q, g):
        slots = pl.ds(*SLOTS[g])
        for d in range(1, 8):
            device, there = me.at_plane(*PLANE[d])
            src, dst = bufs.at[q, there, slots], bufr.at[q, me.plane, slots]
            post(remote(src, dst, *pair(name, q * 2 + g), device))
        shared.append((bufs.at[q, pl.ds(0, 7), slots], name, q * 2 + g))

    def plane_end(bufr, name, q, g):
        arrived(bufr.at[q, pl.ds(0, 7), pl.ds(*SLOTS[g])], name, q * 2 + g)

    ys, yr, xo = r["ys"], r["yr"], r["xo"]

    def pick(q):
        picked = mul(select[...], xg[q].reshape(256, ch)).astype(BF16)
        ys[q] = picked.reshape(8, 3, 16, ch)
        plane_start(ys, yr, "pd", q, 0)
        if q < NQ // 2:
            plane_start(ys, yr, "pd", q, 1)
        if q == NQ - 1:
            for late in range(NQ // 2, NQ):
                plane_start(ys, yr, "pd", late, 1)
        yr[q, me.plane] = ys[q, me.plane]

    ahead = 2
    for q in range(min(ahead, NQ)):
        z_first(q)
    loads[2].wait()
    for turn in range(NQ + 1):
        if turn < NQ:
            if turn < 2:
                scaled_down(r["raw_d"], ds_ref, r["deq_d"], turn * 8, turn * 8 + 8)
            z_second(turn)
            if turn + ahead < NQ:
                z_first(turn + ahead)
        if turn:
            arrived(xg.at[turn - 1, pl.ds(0, 5)], "z", (turn - 1) * 3)
            pick(turn - 1)
    start(remote(r["deq_d"].at[1], r["down_in"], *pair("one", 0), partner))

    es, er = r["es"], r["er"]

    def swap_rows(q, g):
        slots = pl.ds(*SLOTS[g])
        return remote(yr.at[q, :, slots], xo.at[q, :, slots], *pair("fw", q * 2 + g), partner)

    def swap_start(q, g):
        plane_end(yr, "pd", q, g)
        start(swap_rows(q, g))

    def hidden(g):
        lo, count = SLOTS[g]
        rows = 128 * count
        gate = jnp.zeros((rows, 384), F32)
        up = jnp.zeros((rows, 384), F32)
        for q in range(0 if g == 0 else NQ // 2, NQ - 1):
            swap_start(q, g)
        for q in range(NQ):
            if q == NQ - 1:
                swap_start(q, g)
                for early in range(NQ // 2 if g == 0 else 0):
                    swap_start(early, 1)
            swap_rows(q, g).wait_recv()
            cols = slice(q * ch, (q + 1) * ch)
            for half, buf in ((0, yr), (1, xo)):
                block = buf[q, :, lo : lo + count].reshape(rows, ch)
                gate = gate + mul(block, r["deq_g"][half, cols, :])
                up = up + mul(block, r["deq_u"][half, cols, :])
        r["hid%d" % g][...] = (gate / (1.0 + jnp.exp(-gate)) * up).astype(BF16)

    def results(g):
        lo, count = SLOTS[g]
        mine, came = r["hid%d" % g], r["hid_in%d" % g]
        swap = remote(mine, came, *pair("one", 1 + 5 * g), partner)
        start(swap)
        if g == 0:
            remote(r["deq_d"].at[1], r["down_in"], *pair("one", 0), partner).wait_recv()
        ahead = mul(mine[...], r["deq_d"][0, :, 0:ch])
        swap.wait_recv()
        for q in range(NQ):
            cols = slice(q * ch, (q + 1) * ch)
            result = ahead if q == 0 else mul(mine[...], r["deq_d"][0, :, cols])
            result = result + mul(came[...], r["down_in"][:, cols])
            es[q, :, lo : lo + count] = result.astype(BF16).reshape(8, count, 16, ch)
            plane_start(es, er, "ps", q, g)
            er[q, me.plane, lo : lo + count] = es[q, me.plane, lo : lo + count]

    for g in range(2):
        hidden(g)
        results(g)

    comb = r["comb"]

    towards = {1: 1, 7: -1, 3: 1, 5: -1, 2: 2, 6: -2}
    back_out, back_in = r["back_out"], r["back_in"]

    def back_kind(q, offset):
        if offset in (3, 5):
            return q * 3 + (1 if offset == 3 else 2)
        if offset == 4:
            return q * 3 + (1 if q % 2 == 0 else 2)
        return q * 3

    def back_slot(q, offset):
        return {3: 0, 5: 2, 4: 1, 1: 3, 7: 4, 2: 5, 6: 6}[offset]

    def back_start(q, offset, came=None):
        part = comb[q, (z + offset) % 8]
        if came is not None:
            lo, count = came
            arrived(back_in.at[q, pl.ds(lo, count)], "b", back_kind(q, 3 if offset == 2 else 5))
            for n in range(lo, lo + count):
                part = part + back_in[q, n].astype(F32)
        slot = back_slot(q, offset)
        back_out[q, slot] = part.astype(BF16)
        to = towards.get(offset, 2 if q % 2 == 0 else -2)
        sems = shares("b", q, back_kind(q, offset))
        post(remote(back_out.at[q, slot], back_in.at[q, slot], *sems, me.at_z(to % 8)))

    def back_second(q):
        back_start(q, 2, (0, 2) if q % 2 == 0 else (0, 1))
        back_start(q, 6, (2, 1) if q % 2 == 0 else (1, 2))
        shared.append((back_out.at[q, pl.ds(0, 7)], "b", q))

    fin, fin_in = r["fin"], r["fin_in"]
    for turn in range(NQ + 1):
        if turn < NQ:
            for g in range(2):
                plane_end(er, "ps", turn, g)
            rows = er[turn].reshape(384, ch)
            total = mul(weights_hi[...], rows) + mul(weights_lo[...], rows)
            comb[turn] = total.reshape(8, 32, ch)
            for offset in (4, 3, 5, 1, 7):
                back_start(turn, offset)
        if turn:
            back_second(turn - 1)
    for q in range(NQ):
        total = comb[q, z] + st[:, q * ch : (q + 1) * ch]
        arrived(back_in.at[q, pl.ds(3, 4)], "b", q * 3)
        for n in range(3, 7):
            total = total + back_in[q, n].astype(F32)
        fin[q] = total.astype(BF16).reshape(2, 16, ch)
        start(remote(fin.at[q, 1 - k], fin_in.at[q], *pair("fn", q), partner))
    for q in range(NQ):
        remote(fin.at[q, 1 - k], fin_in.at[q], *pair("fn", q), partner).wait_recv()
        own, got = fin[q, k], fin_in[q]
        for c in range(ch // 128):
            at = (q * (ch // 128) + c) * 256
            piece = slice(c * 128, (c + 1) * 128)
            out_ref[:, pl.ds(pl.multiple_of(at + k * 128, 128), 128)] = own[:, piece]
            out_ref[:, pl.ds(pl.multiple_of(at + (1 - k) * 128, 128), 128)] = got[:, piece]
    for copy in sends:
        copy.wait_send()
    for buf, name, send in shared:
        remote(buf, buf, *shares(name, send, 0), partner).wait_send()


def scratch():
    ch = 2048 // NQ
    shapes = {
        "kv": ((2, 16, 128, 128), BF16),
        "wb": ((2, 8, 512, 128), BF16),
        "res": ((2, 16, 2048), BF16),
        "res_give": ((16, 2048), BF16),
        "gain": ((1, 2048), F32),
        "bias": ((128, 2048), F32),
        "acc": ((4, 128, 128), F32),
        "top": ((4, 128, 128), F32),
        "norm": ((4, 128, 128), F32),
        "ab": ((2, 2, 128, 512), BF16),
        "px": ((8, 8, 32, 128), BF16),
        "rx": ((8, 8, 32, 128), BF16),
        "st": ((32, 2048), F32),
        "sq": ((2, 32, 128), F32),
        "mt": ((8, 2, 2, 8, 128), F32),
        "tables": ((2, 256, 128), F32),
        "sel": ((384, 256), BF16),
        "whi": ((256, 384), BF16),
        "wlo": ((256, 384), BF16),
        "xg": ((NQ, 8, 32, ch), BF16),
        "ys": ((NQ, 8, 3, 16, ch), BF16),
        "yr": ((NQ, 8, 3, 16, ch), BF16),
        "xo": ((NQ, 8, 3, 16, ch), BF16),
        "raw_g": ((4096, 384), BF16),
        "raw_u": ((4096, 384), BF16),
        "raw_d": ((384, 4096), BF16),
        "deq_g": ((2, 2048, 384), BF16),
        "deq_u": ((2, 2048, 384), BF16),
        "deq_d": ((2, 384, 2048), BF16),
        "down_in": ((384, 2048), BF16),
        "hid0": ((128, 384), BF16),
        "hid_in0": ((128, 384), BF16),
        "hid1": ((256, 384), BF16),
        "hid_in1": ((256, 384), BF16),
        "es": ((NQ, 8, 3, 16, ch), BF16),
        "er": ((NQ, 8, 3, 16, ch), BF16),
        "comb": ((NQ, 8, 32, ch), F32),
        "back_out": ((NQ, 8, 32, ch), BF16),
        "back_in": ((NQ, 8, 32, ch), BF16),
        "fin": ((NQ, 2, 16, ch), BF16),
        "fin_in": ((NQ, 16, ch), BF16),
    }
    made = {name: pltpu.VMEM(*what) for name, what in shapes.items()}
    made["w_sem"] = pltpu.SemaphoreType.DMA((3,))
    copies = {
        "kv": (1, 8),
        "kva": (1, 1),
        "kvp": (2, 2),
        "mt": (1, 1),
        "one": (7, 7),
        "w": (3, 24),
        "ws": (1, 5),
        "a": (6, 6),
        "x": (len(GROUPS), len(GROUPS)),
        "z": (NQ, 3 * NQ),
        "pd": (2 * NQ, 2 * NQ),
        "fw": (2 * NQ, 2 * NQ),
        "ps": (2 * NQ, 2 * NQ),
        "b": (NQ, 3 * NQ),
        "fn": (NQ, NQ),
    }
    for name, (sent, received) in copies.items():
        made[name + "_s"] = pltpu.SemaphoreType.DMA((sent,))
        made[name + "_r"] = pltpu.SemaphoreType.DMA((received,))
    return made


SCRATCH = tuple(scratch())


def layer(*operands):
    vmem = pl.BlockSpec(memory_space=pltpu.VMEM)
    smem = pl.BlockSpec(memory_space=pltpu.SMEM)
    hbm = pl.BlockSpec(memory_space=pl.ANY)
    return pl.pallas_call(
        layer_kernel,
        out_shape=jax.ShapeDtypeStruct((16, 4096), BF16),
        in_specs=[vmem] * 3 + [smem] * 3 + [vmem] * 5 + [hbm] * 3 + [smem] * 3,
        out_specs=vmem,
        scratch_shapes=list(scratch().values()),
        compiler_params=pltpu.CompilerParams(
            collective_id=1, has_side_effects=True, vmem_limit_bytes=58 * 1024 * 1024
        ),
        name="layer",
    )(*operands)


def shards(
    residual,
    encoded_query_rows,
    quantized_key_rows,
    quantized_value_rows,
    key_block_exponent,
    value_block_exponent,
    block_order,
    out_weight,
    norm_gain,
    expert_ids,
    route_weight,
    gate_weight,
    gate_scale,
    up_weight,
    up_scale,
    down_weight,
    down_scale,
):
    return layer(
        encoded_query_rows,
        quantized_key_rows,
        quantized_value_rows,
        key_block_exponent,
        value_block_exponent,
        block_order,
        out_weight,
        residual,
        norm_gain.reshape(1, -1),
        expert_ids.T,
        route_weight.T,
        gate_weight[0],
        up_weight[0],
        down_weight[0],
        gate_scale.transpose(2, 0, 1),
        up_scale.transpose(2, 0, 1),
        down_scale.transpose(1, 0, 2),
    )


def solution(mesh):
    return jax.shard_map(
        shards,
        mesh=mesh,
        in_specs=(
            P(("dp", "ctx", "exp"), None),
            P(("dp", "ctx"), "exp"),
            P(("dp", "ctx"), None),
            P(("dp", "ctx"), None),
            P(("dp", "ctx"), None),
            P(("dp", "ctx"), None),
            P(),
            P("exp", "ctx"),
            P(),
            P(("dp", "ctx", "exp"), None),
            P(("dp", "ctx", "exp"), None),
            P(("ctx", "exp"), None, None),
            P(("ctx", "exp"), None, None),
            P(("ctx", "exp"), None, None),
            P(("ctx", "exp"), None, None),
            P(("ctx", "exp"), None, None),
            P(("ctx", "exp"), None, None),
        ),
        out_specs=P(("dp", "ctx", "exp"), None),
        check_vma=False,
    )
```

```python
import math

import jax
import jax.numpy as jnp
from jax import lax
from jax.experimental import pallas as pl
from jax.experimental.pallas import tpu as pltpu
from jax.sharding import PartitionSpec as P

HEAD_SIZE = 128

MESH = pl.DeviceIdType.MESH
F32 = jnp.float32
BF16 = jnp.bfloat16
NQ = 4
OFFSETS = (0, 1, 7, 2, 6, 3, 5, 4)
GROUPS = ((0, 3), (3, 5), (5, 8))
SLOTS = ((0, 1), (1, 2))
PLANE = [(dx, dy) for dy in range(2) for dx in range(4)]


def contract_last(lhs, rhs):
    return lax.dot_general(lhs, rhs, (((1,), (1,)), ((), ())), preferred_element_type=F32)


def mul(lhs, rhs):
    return jnp.dot(lhs, rhs, preferred_element_type=F32)


def remote(src, dst, send_sem, recv_sem, device):
    return pltpu.make_async_remote_copy(
        src_ref=src,
        dst_ref=dst,
        send_sem=send_sem,
        recv_sem=recv_sem,
        device_id=device,
        device_id_type=MESH,
    )


def hops(q):
    return (4, 3) if q % 2 == 0 else (3, 4)


class Place:
    def __init__(self):
        self.ctx = lax.axis_index("ctx")
        self.exp = lax.axis_index("exp")
        self.dp = lax.axis_index("dp")
        self.z = self.ctx % 8
        self.yh = self.ctx // 8
        self.x = self.exp // 2
        self.k = self.exp % 2
        self.plane = self.yh * 4 + self.x

    def at_ctx(self, i):
        return {"ctx": (self.ctx + i) % 16, "exp": self.exp, "dp": self.dp}

    def at_z(self, dz, dk=0):
        z = (self.z + dz) % 8
        k = (self.k + dk) % 2
        return {"ctx": self.yh * 8 + z, "exp": self.x * 2 + k, "dp": self.dp}

    def at_plane(self, dx, dy):
        x = (self.x + dx) % 4
        yh = (self.yh + dy) % 2
        dp = (self.dp + dy) % 2
        return {"ctx": yh * 8 + self.z, "exp": x * 2 + self.k, "dp": dp}, yh * 4 + x

    def plane_from(self, dx, dy):
        return ((self.yh + 2 - dy) % 2) * 4 + (self.x + 4 - dx) % 4

    def other_part(self):
        return {"ctx": self.ctx, "exp": self.exp, "dp": 1 - self.dp}

    def other_core(self):
        return {"ctx": self.ctx, "exp": self.x * 2 + (1 - self.k), "dp": self.dp}


def layer_kernel(
    q_ref,
    kq_ref,
    vq_ref,
    ke_ref,
    ve_ref,
    order_ref,
    w_ref,
    res_ref,
    gain_ref,
    ids_ref,
    rw_ref,
    gw_ref,
    uw_ref,
    dw_ref,
    gs_ref,
    us_ref,
    ds_ref,
    out_ref,
    *scratch_refs,
):
    r = dict(zip(SCRATCH, scratch_refs, strict=True))
    sem = {name[:-2]: (r[name], r[name[:-2] + "_r"]) for name in SCRATCH if name.endswith("_s")}
    me = Place()
    z, k, x, yh = me.z, me.k, me.x, me.yh
    partner = me.other_core()
    right, left = me.at_z(1), me.at_z(7)
    xg, st = r["xg"], r["st"]
    ch = xg.shape[-1]
    sends = []

    def start(copy):
        copy.start()
        sends.append(copy)

    def pair(name, *index):
        return sem[name][0].at[index], sem[name][1].at[index]

    shared = []

    def post(copy, *sent):
        copy.start()
        if sent:
            shared.append(sent)

    def shares(name, send, recv):
        return sem[name][0].at[send], sem[name][1].at[recv]

    def arrived(buf, name, recv):
        remote(buf, buf, *shares(name, 0, recv), partner).wait_recv()

    loads = [
        pltpu.make_async_copy(src, r[dst], r["w_sem"].at[i])
        for i, (src, dst) in enumerate(((gw_ref, "raw_g"), (uw_ref, "raw_u"), (dw_ref, "raw_d")))
    ]
    for load in loads:
        load.start()

    barrier = pltpu.get_barrier_semaphore()
    peers = [me.at_plane(dx, dy)[0] for dx, dy in PLANE[1:]]
    peers = peers + [partner, me.at_ctx(8), me.other_part()] + [me.at_z(i) for i in range(1, 8)]
    for peer in peers:
        pl.semaphore_signal(barrier, inc=1, device_id=peer, device_id_type=MESH)
    pl.semaphore_wait(barrier, len(peers))

    def gather(buf, name, q, step, rightward):
        block = (z + 8 - step) % 8 if rightward else (z + step) % 8
        sems = shares(name, q, q * 8 + step * 2 + (0 if rightward else 1))
        return remote(buf(block), buf(block), *sems, right if rightward else left)

    def gathered(buf, name, q, step, rightward):
        block = (z + 7 - step) % 8 if rightward else (z + 1 + step) % 8
        arrived(buf(block), name, q * 8 + step * 2 + (0 if rightward else 1))

    def ring_start(buf, name, q):
        post(gather(buf, name, q, 0, True))
        post(gather(buf, name, q, 0, False))

    def ring_step(buf, name, q, step):
        for rightward, count in zip((True, False), hops(q)):
            if step <= count:
                gathered(buf, name, q, step - 1, rightward)
                if step < count:
                    post(gather(buf, name, q, step, rightward))

    kv = r["kv"]
    row = lax.broadcasted_iota(jnp.int32, (128, 128), 0)
    col = lax.broadcasted_iota(jnp.int32, (128, 128), 1)
    head = pl.ds(pl.multiple_of(x * 128, 128), 128)
    first = jnp.where(k == 0, ke_ref[0, x], ve_ref[0, x])
    second = jnp.where(k == 0, ke_ref[1, x], ve_ref[1, x])
    power = jnp.where(row < 64, first, second)
    factor = jnp.zeros((128, 128), F32)
    for p in range(-2, 2):
        factor = factor + jnp.where(power == p, 2.0**p, 0.0)
    mine = jnp.where(k == 0, kq_ref[:, head].astype(F32), vq_ref[:, head].astype(F32))
    kv[k, me.ctx] = (mine * factor).astype(BF16)

    def kv_at(offset, side, kind=k):
        return kv.at[kind, (yh if side == 0 else 1 - yh) * 8 + (z + offset) % 8]

    def kv_copy(offset):
        own = kv_at(0, 0)
        return remote(own, own, *shares("kv", 0, offset), me.at_z(offset))

    def kv_across(offset):
        at = kv_at(offset, 0)
        return remote(at, at, *shares("kva", 0, 0), me.at_ctx(8))

    def kv_side(side, kind):
        return kv.at[kind, pl.ds(pl.multiple_of((yh if side == 0 else 1 - yh) * 8, 8), 8)]

    def kv_pass(side):
        return remote(kv_side(side, k), kv_side(side, k), *pair("kvp", side), partner)

    for offset in (4, 3, 5, 2, 6, 1, 7):
        post(kv_copy(offset))
    post(kv_across(0))
    shared.append((kv.at[0, pl.ds(0, 7)], "kv", 0))
    shared.append((kv.at[0, pl.ds(0, 8)], "kva", 0))

    wb = r["wb"]
    give = w_ref.at[:, pl.ds(pl.multiple_of((1 - k) * 128, 128), 128)]
    start(remote(give, wb.at[k, z], *pair("one", 2), partner))
    wb[k, z] = w_ref[:, pl.ds(pl.multiple_of(k * 128, 128), 128)]

    def w_block(q):
        core = k if q < 2 else 1 - k
        rows = pl.ds(q * 256 if q < 2 else pl.multiple_of(me.dp * 256, 256), 256)
        return lambda block: wb.at[core, block, rows]

    def w_step(step, parts=range(3)):
        for q in parts:
            ring_step(w_block(q), "w", q, step)
            if q == 2:
                for offset in (8 - step, step) if step < 4 else (4,):
                    block = w_block(2)((z + offset) % 8)
                    post(remote(block, block, *shares("ws", 0, step), me.other_part()))

    def w_shared(step):
        arrived(wb.at[0, pl.ds(0, 2 if step < 4 else 1), pl.ds(0, 256)], "ws", step)

    for q in range(2):
        ring_start(w_block(q), "w", q)

    mt = r["mt"]
    mt[z, k] = jnp.zeros((2, 8, 128), F32)
    mt[z, k, 0, :, 0:16] = ids_ref[...].astype(F32)
    mt[z, k, 1, :, 0:16] = rw_ref[...]

    for offset in range(1, 8):
        post(remote(mt.at[z, k], mt.at[z, k], *shares("mt", 0, 0), me.at_z(offset)))
    shared.append((mt.at[pl.ds(0, 7), 0], "mt", 0))

    def mt_pass(core):
        return remote(mt.at[:, core], mt.at[:, core], *pair("one", 4), partner)

    res, res_give, gain = r["res"], r["res_give"], r["gain"]
    for c in range(16):
        to = slice(c * 128, (c + 1) * 128)
        own = pl.ds(pl.multiple_of(c * 256 + k * 128, 128), 128)
        other = pl.ds(pl.multiple_of(c * 256 + (1 - k) * 128, 128), 128)
        res[k, :, to] = res_ref[:, own]
        res_give[:, to] = res_ref[:, other]
        gain[:, to] = gain_ref[:, own]
    start(remote(res_give, res.at[k], *pair("one", 3), partner))

    def power_of(exponent):
        return jnp.where(exponent == 0, 1.0, jnp.where(exponent > 0, 2.0, 0.5))

    def scaled(raw, scale, deq, lo=0, hi=16):
        def body(c, carry):
            for half in range(2):
                side = k if half == 0 else 1 - k
                at = pl.ds(pl.multiple_of(c * 256 + side * 128, 128), 128)
                to = pl.ds(pl.multiple_of(c * 128, 128), 128)
                for b in range(3):
                    cols = slice(b * 128, (b + 1) * 128)
                    block = raw[at, cols].astype(F32) * power_of(scale[b, 0, c * 2 + side])
                    deq[half, to, cols] = block.astype(BF16)
            return carry

        lax.fori_loop(lo, hi, body, 0)

    def scaled_down(raw, scale, deq, lo=0, hi=16):
        def body(c, carry):
            for half in range(2):
                side = k if half == 0 else 1 - k
                at = pl.ds(pl.multiple_of(c * 256 + side * 128, 128), 128)
                to = pl.ds(pl.multiple_of(c * 128, 128), 128)
                for b in range(3):
                    rows = slice(b * 128, (b + 1) * 128)
                    block = raw[rows, at].astype(F32) * power_of(scale[b, 0, c * 2 + side])
                    deq[half, rows, to] = block.astype(BF16)
            return carry

        lax.fori_loop(lo, hi, body, 0)

    remote(give, wb.at[1 - k, z], *pair("one", 2), partner).wait_recv()
    ring_start(w_block(2), "w", 2)
    for q in range(3):
        shared.append((wb.at[0, pl.ds(0, 7), pl.ds(0, 256)], "w", q))
    shared.append((wb.at[0, pl.ds(0, 7), pl.ds(0, 256)], "ws", 0))

    bias = r["bias"]
    own_place = order_ref[me.ctx]
    for j in range(16):
        seen = order_ref[j] * 128 + col <= own_place * 128 + row
        bias[:, j * 128 : (j + 1) * 128] = jnp.where(seen, 0.0, -1e30)

    loads[0].wait()
    scaled(r["raw_g"], gs_ref, r["deq_g"])
    for offset in (1, 7, 2, 6, 3, 5, 4):
        arrived(kv_at(8 - offset, 0), "kv", offset)
        post(kv_across(8 - offset))
    start(kv_pass(0))
    w_step(1)
    arrived(mt.at[pl.ds(0, 7), k], "mt", 0)
    start(mt_pass(k))
    arrived(kv_side(1, k), "kva", 0)
    start(kv_pass(1))
    w_step(2, range(2))
    for side in range(2):
        remote(kv_side(side, 1 - k), kv_side(side, 1 - k), *pair("kvp", side), partner).wait_recv()

    ab = r["ab"]
    keys, values = kv[0].reshape(2048, 128), kv[1].reshape(2048, 128)
    over = me.at_plane(0, 1)[0]

    def a_part(core, side, n):
        return ab.at[core, yh if side == 0 else 1 - yh, :, pl.ds(n * 256, 256)]

    def a_start(n):
        own = a_part(k, 0, n)
        start(remote(own, own, *pair("a", n * 3 + 1), over))
        start(remote(own, own, *pair("a", n * 3), partner))

    for h in range(4):
        to = slice(h * 128, (h + 1) * 128)
        scores = contract_last(q_ref[:, to], keys) * (1.0 / math.sqrt(HEAD_SIZE) * math.log2(math.e))
        scores = scores + bias[...]
        exps = jnp.exp2(scores - jnp.max(scores, axis=1, keepdims=True))
        total = jnp.sum(exps, axis=1, keepdims=True)
        ab[k, yh, :, to] = (mul(exps.astype(BF16), values) / total).astype(BF16)
        if h == 0:
            w_step(2, range(2, 3))
        if h == 2:
            w_step(3, range(2))
        if h % 2 == 1:
            a_start(h // 2)
    w_step(3, range(2, 3))
    mt_pass(1 - k).wait_recv()
    tables = r["tables"]
    for n in range(16):
        for kind in range(2):
            block = jnp.transpose(mt[n // 2, n % 2, kind])
            tables[kind, n * 16 : (n + 1) * 16, 0:8] = block[0:16, :]
    ids, rw = tables[0], tables[1]
    slot = lax.broadcasted_iota(jnp.int32, (256, 384), 1)
    token = lax.broadcasted_iota(jnp.int32, (256, 384), 0)
    expert = slot // 48
    named = ((expert // 4) * 32 + z * 4 + expert % 4).astype(F32)
    member = jnp.zeros((256, 384), F32)
    weights = jnp.zeros((256, 384), F32)
    for n in range(8):
        hit = ids[:, n : n + 1] == named
        member = jnp.where(hit, 1.0, member)
        weights = jnp.where(hit, rw[:, n : n + 1], weights)
    first = lax.broadcasted_iota(jnp.int32, (256, 256), 0)
    second = lax.broadcasted_iota(jnp.int32, (256, 256), 1)
    earlier = (second < first) & (second // 16 == first // 16)
    number = mul(jnp.where(earlier, 1.0, 0.0).astype(BF16), member.astype(BF16))
    here = (number == (slot % 48 // 16).astype(F32)) & (slot % 16 == token // 16)
    weights = jnp.where(here, weights, 0.0)
    select, weights_hi, weights_lo = r["sel"], r["whi"], r["wlo"]
    select[...] = jnp.transpose(jnp.where(here, member, 0.0)).astype(BF16)
    weights_hi[...] = weights.astype(BF16)
    weights_lo[...] = (weights - weights.astype(BF16).astype(F32)).astype(BF16)

    for n in range(2):
        came = a_part(k, 1, n)
        remote(came, came, *pair("a", n * 3 + 1), over).wait_recv()
        start(remote(came, came, *pair("a", n * 3 + 2), partner))
    for n in range(2):
        for i in (0, 2):
            came = a_part(1 - k, i // 2, n)
            remote(came, came, *pair("a", n * 3 + i), partner).wait_recv()

    px, rx = r["px"], r["rx"]
    attended = [ab[core].reshape(256, 512) for core in range(2)]
    for g, (lo, hi) in enumerate(GROUPS):
        if g == len(GROUPS) - 1:
            loads[1].wait()
            scaled(r["raw_u"], us_ref, r["deq_u"])
            w_step(4)
        for step in ((1,), (2,), (3, 4))[g]:
            w_shared(step)
        for n in range(lo, hi):
            at = (z + OFFSETS[n]) % 8
            part = mul(attended[0], wb[0, at]) + mul(attended[1], wb[1, at])
            part = part.astype(BF16).reshape(2, 4, 32, 128)
            for side in range(2):
                for to in range(4):
                    px[side * 4 + to, n] = part[side, to]
        cut = pl.ds(lo, hi - lo)
        for d in range(1, 8):
            device, there = me.at_plane(*PLANE[d])
            post(remote(px.at[there, cut], rx.at[d, cut], *pair("x", g), device))
        shared.append((rx.at[pl.ds(1, 7), cut], "x", g))

    remote(res_give, res.at[1 - k], *pair("one", 3), partner).wait_recv()
    for g, (lo, hi) in enumerate(GROUPS):
        arrived(rx.at[pl.ds(1, 7), pl.ds(lo, hi - lo)], "x", g)
        for n in range(lo, hi):
            for side in range(2):
                total = (px[me.plane, n] if side == 0 else rx[4, n]).astype(F32)
                for dx in range(1, 4):
                    total = total + rx[side * 4 + dx, n].astype(F32)
                at = ((yh if side == 0 else 1 - yh) * 8 + (z + OFFSETS[n]) % 8) * 128
                st[:, pl.ds(pl.multiple_of(at, 128), 128)] = total
    st[...] = st[...] + res[...].reshape(32, 2048).astype(F32)
    squares = jnp.sum(st[...] * st[...], axis=1, keepdims=True)
    r["sq"][0] = jnp.broadcast_to(squares, (32, 128))
    swap = remote(r["sq"].at[0], r["sq"].at[1], *pair("one", 5), partner)
    start(swap)
    swap.wait_recv()
    mean = (r["sq"][0, :, 0:1] + r["sq"][1, :, 0:1]) / 4096.0
    normed = (st[...] * lax.rsqrt(mean + 1e-6) * gain[...]).astype(BF16)

    for q in range(NQ):
        xg[q, z] = normed[:, q * ch : (q + 1) * ch]

    def z_copy(q, source, to):
        block = xg.at[q, (z + source) % 8]
        offset = (source - to) % 8
        sems = shares("z", q, q * 3 + {2: 1, 6: 2}.get(offset, 0))
        return remote(block, block, *sems, me.at_z(to % 8))

    def z_first(q):
        for to in (2, -2, 1, -1):
            post(z_copy(q, 0, to))
        shared.append((xg.at[q, pl.ds(0, 7)], "z", q))

    def z_second(q):
        for side in (1, -1):
            arrived(xg.at[q, (z + 8 - 2 * side) % 8], "z", q * 3 + (2 if side == 1 else 1))
            post(z_copy(q, -2 * side, side))
            if (side == 1) == (q % 2 == 0):
                post(z_copy(q, -2 * side, 2 * side))

    def plane_start(bufs, bufr, name, q, g):
        slots = pl.ds(*SLOTS[g])
        for d in range(1, 8):
            device, there = me.at_plane(*PLANE[d])
            src, dst = bufs.at[q, there, slots], bufr.at[q, me.plane, slots]
            post(remote(src, dst, *pair(name, q * 2 + g), device))
        shared.append((bufs.at[q, pl.ds(0, 7), slots], name, q * 2 + g))

    def plane_end(bufr, name, q, g):
        arrived(bufr.at[q, pl.ds(0, 7), pl.ds(*SLOTS[g])], name, q * 2 + g)

    ys, yr, xo = r["ys"], r["yr"], r["xo"]

    def pick(q):
        picked = mul(select[...], xg[q].reshape(256, ch)).astype(BF16)
        ys[q] = picked.reshape(8, 3, 16, ch)
        plane_start(ys, yr, "pd", q, 0)
        if q < NQ // 2:
            plane_start(ys, yr, "pd", q, 1)
        if q == NQ - 1:
            for late in range(NQ // 2, NQ):
                plane_start(ys, yr, "pd", late, 1)
        yr[q, me.plane] = ys[q, me.plane]

    ahead = 2
    for q in range(min(ahead, NQ)):
        z_first(q)
    loads[2].wait()
    for turn in range(NQ + 1):
        if turn < NQ:
            if turn < 2:
                scaled_down(r["raw_d"], ds_ref, r["deq_d"], turn * 8, turn * 8 + 8)
            z_second(turn)
            if turn + ahead < NQ:
                z_first(turn + ahead)
        if turn:
            arrived(xg.at[turn - 1, pl.ds(0, 5)], "z", (turn - 1) * 3)
            pick(turn - 1)
    start(remote(r["deq_d"].at[1], r["down_in"], *pair("one", 0), partner))

    es, er = r["es"], r["er"]

    def swap_rows(q, g):
        slots = pl.ds(*SLOTS[g])
        return remote(yr.at[q, :, slots], xo.at[q, :, slots], *pair("fw", q * 2 + g), partner)

    def swap_start(q, g):
        plane_end(yr, "pd", q, g)
        start(swap_rows(q, g))

    def hidden(g):
        lo, count = SLOTS[g]
        rows = 128 * count
        gate = jnp.zeros((rows, 384), F32)
        up = jnp.zeros((rows, 384), F32)
        for q in range(0 if g == 0 else NQ // 2, NQ - 1):
            swap_start(q, g)
        for q in range(NQ):
            if q == NQ - 1:
                swap_start(q, g)
                for early in range(NQ // 2 if g == 0 else 0):
                    swap_start(early, 1)
            swap_rows(q, g).wait_recv()
            cols = slice(q * ch, (q + 1) * ch)
            for half, buf in ((0, yr), (1, xo)):
                block = buf[q, :, lo : lo + count].reshape(rows, ch)
                gate = gate + mul(block, r["deq_g"][half, cols, :])
                up = up + mul(block, r["deq_u"][half, cols, :])
        r["hid%d" % g][...] = (gate / (1.0 + jnp.exp(-gate)) * up).astype(BF16)

    def results(g):
        lo, count = SLOTS[g]
        mine, came = r["hid%d" % g], r["hid_in%d" % g]
        swap = remote(mine, came, *pair("one", 1 + 5 * g), partner)
        start(swap)
        if g == 0:
            remote(r["deq_d"].at[1], r["down_in"], *pair("one", 0), partner).wait_recv()
        ahead = mul(mine[...], r["deq_d"][0, :, 0:ch])
        swap.wait_recv()
        for q in range(NQ):
            cols = slice(q * ch, (q + 1) * ch)
            result = ahead if q == 0 else mul(mine[...], r["deq_d"][0, :, cols])
            result = result + mul(came[...], r["down_in"][:, cols])
            es[q, :, lo : lo + count] = result.astype(BF16).reshape(8, count, 16, ch)
            plane_start(es, er, "ps", q, g)
            er[q, me.plane, lo : lo + count] = es[q, me.plane, lo : lo + count]

    for g in range(2):
        hidden(g)
        results(g)

    comb = r["comb"]

    towards = {1: 1, 7: -1, 3: 1, 5: -1, 2: 2, 6: -2}
    back_out, back_in = r["back_out"], r["back_in"]

    def back_kind(q, offset):
        if offset in (3, 5):
            return q * 3 + (1 if offset == 3 else 2)
        if offset == 4:
            return q * 3 + (1 if q % 2 == 0 else 2)
        return q * 3

    def back_slot(q, offset):
        return {3: 0, 5: 2, 4: 1, 1: 3, 7: 4, 2: 5, 6: 6}[offset]

    def back_start(q, offset, came=None):
        part = comb[q, (z + offset) % 8]
        if came is not None:
            lo, count = came
            arrived(back_in.at[q, pl.ds(lo, count)], "b", back_kind(q, 3 if offset == 2 else 5))
            for n in range(lo, lo + count):
                part = part + back_in[q, n].astype(F32)
        slot = back_slot(q, offset)
        back_out[q, slot] = part.astype(BF16)
        to = towards.get(offset, 2 if q % 2 == 0 else -2)
        sems = shares("b", q, back_kind(q, offset))
        post(remote(back_out.at[q, slot], back_in.at[q, slot], *sems, me.at_z(to % 8)))

    def back_second(q):
        back_start(q, 2, (0, 2) if q % 2 == 0 else (0, 1))
        back_start(q, 6, (2, 1) if q % 2 == 0 else (1, 2))
        shared.append((back_out.at[q, pl.ds(0, 7)], "b", q))

    fin, fin_in = r["fin"], r["fin_in"]
    for turn in range(NQ + 1):
        if turn < NQ:
            for g in range(2):
                plane_end(er, "ps", turn, g)
            rows = er[turn].reshape(384, ch)
            total = mul(weights_hi[...], rows) + mul(weights_lo[...], rows)
            comb[turn] = total.reshape(8, 32, ch)
            for offset in (4, 3, 5, 1, 7):
                back_start(turn, offset)
        if turn:
            back_second(turn - 1)
    for q in range(NQ):
        total = comb[q, z] + st[:, q * ch : (q + 1) * ch]
        arrived(back_in.at[q, pl.ds(3, 4)], "b", q * 3)
        for n in range(3, 7):
            total = total + back_in[q, n].astype(F32)
        fin[q] = total.astype(BF16).reshape(2, 16, ch)
        start(remote(fin.at[q, 1 - k], fin_in.at[q], *pair("fn", q), partner))
    for q in range(NQ):
        remote(fin.at[q, 1 - k], fin_in.at[q], *pair("fn", q), partner).wait_recv()
        own, got = fin[q, k], fin_in[q]
        for c in range(ch // 128):
            at = (q * (ch // 128) + c) * 256
            piece = slice(c * 128, (c + 1) * 128)
            out_ref[:, pl.ds(pl.multiple_of(at + k * 128, 128), 128)] = own[:, piece]
            out_ref[:, pl.ds(pl.multiple_of(at + (1 - k) * 128, 128), 128)] = got[:, piece]
    for copy in sends:
        copy.wait_send()
    for buf, name, send in shared:
        remote(buf, buf, *shares(name, send, 0), partner).wait_send()


def scratch():
    ch = 2048 // NQ
    shapes = {
        "kv": ((2, 16, 128, 128), BF16),
        "wb": ((2, 8, 512, 128), BF16),
        "res": ((2, 16, 2048), BF16),
        "res_give": ((16, 2048), BF16),
        "gain": ((1, 2048), F32),
        "bias": ((128, 2048), F32),
        "ab": ((2, 2, 128, 512), BF16),
        "px": ((8, 8, 32, 128), BF16),
        "rx": ((8, 8, 32, 128), BF16),
        "st": ((32, 2048), F32),
        "sq": ((2, 32, 128), F32),
        "mt": ((8, 2, 2, 8, 128), F32),
        "tables": ((2, 256, 128), F32),
        "sel": ((384, 256), BF16),
        "whi": ((256, 384), BF16),
        "wlo": ((256, 384), BF16),
        "xg": ((NQ, 8, 32, ch), BF16),
        "ys": ((NQ, 8, 3, 16, ch), BF16),
        "yr": ((NQ, 8, 3, 16, ch), BF16),
        "xo": ((NQ, 8, 3, 16, ch), BF16),
        "raw_g": ((4096, 384), BF16),
        "raw_u": ((4096, 384), BF16),
        "raw_d": ((384, 4096), BF16),
        "deq_g": ((2, 2048, 384), BF16),
        "deq_u": ((2, 2048, 384), BF16),
        "deq_d": ((2, 384, 2048), BF16),
        "down_in": ((384, 2048), BF16),
        "hid0": ((128, 384), BF16),
        "hid_in0": ((128, 384), BF16),
        "hid1": ((256, 384), BF16),
        "hid_in1": ((256, 384), BF16),
        "es": ((NQ, 8, 3, 16, ch), BF16),
        "er": ((NQ, 8, 3, 16, ch), BF16),
        "comb": ((NQ, 8, 32, ch), F32),
        "back_out": ((NQ, 8, 32, ch), BF16),
        "back_in": ((NQ, 8, 32, ch), BF16),
        "fin": ((NQ, 2, 16, ch), BF16),
        "fin_in": ((NQ, 16, ch), BF16),
    }
    made = {name: pltpu.VMEM(*what) for name, what in shapes.items()}
    made["w_sem"] = pltpu.SemaphoreType.DMA((3,))
    copies = {
        "kv": (1, 8),
        "kva": (1, 1),
        "kvp": (2, 2),
        "mt": (1, 1),
        "one": (7, 7),
        "w": (3, 24),
        "ws": (1, 5),
        "a": (6, 6),
        "x": (len(GROUPS), len(GROUPS)),
        "z": (NQ, 3 * NQ),
        "pd": (2 * NQ, 2 * NQ),
        "fw": (2 * NQ, 2 * NQ),
        "ps": (2 * NQ, 2 * NQ),
        "b": (NQ, 3 * NQ),
        "fn": (NQ, NQ),
    }
    for name, (sent, received) in copies.items():
        made[name + "_s"] = pltpu.SemaphoreType.DMA((sent,))
        made[name + "_r"] = pltpu.SemaphoreType.DMA((received,))
    return made


SCRATCH = tuple(scratch())


def layer(*operands):
    vmem = pl.BlockSpec(memory_space=pltpu.VMEM)
    smem = pl.BlockSpec(memory_space=pltpu.SMEM)
    hbm = pl.BlockSpec(memory_space=pl.ANY)
    return pl.pallas_call(
        layer_kernel,
        out_shape=jax.ShapeDtypeStruct((16, 4096), BF16),
        in_specs=[vmem] * 3 + [smem] * 3 + [vmem] * 5 + [hbm] * 3 + [smem] * 3,
        out_specs=vmem,
        scratch_shapes=list(scratch().values()),
        compiler_params=pltpu.CompilerParams(
            collective_id=1, has_side_effects=True, vmem_limit_bytes=58 * 1024 * 1024
        ),
        name="layer",
    )(*operands)


def shards(
    residual,
    encoded_query_rows,
    quantized_key_rows,
    quantized_value_rows,
    key_block_exponent,
    value_block_exponent,
    block_order,
    out_weight,
    norm_gain,
    expert_ids,
    route_weight,
    gate_weight,
    gate_scale,
    up_weight,
    up_scale,
    down_weight,
    down_scale,
):
    return layer(
        encoded_query_rows,
        quantized_key_rows,
        quantized_value_rows,
        key_block_exponent,
        value_block_exponent,
        block_order,
        out_weight,
        residual,
        norm_gain.reshape(1, -1),
        expert_ids.T,
        route_weight.T,
        gate_weight[0],
        up_weight[0],
        down_weight[0],
        gate_scale.transpose(2, 0, 1),
        up_scale.transpose(2, 0, 1),
        down_scale.transpose(1, 0, 2),
    )


def solution(mesh):
    return jax.shard_map(
        shards,
        mesh=mesh,
        in_specs=(
            P(("dp", "ctx", "exp"), None),
            P(("dp", "ctx"), "exp"),
            P(("dp", "ctx"), None),
            P(("dp", "ctx"), None),
            P(("dp", "ctx"), None),
            P(("dp", "ctx"), None),
            P(),
            P("exp", "ctx"),
            P(),
            P(("dp", "ctx", "exp"), None),
            P(("dp", "ctx", "exp"), None),
            P(("ctx", "exp"), None, None),
            P(("ctx", "exp"), None, None),
            P(("ctx", "exp"), None, None),
            P(("ctx", "exp"), None, None),
            P(("ctx", "exp"), None, None),
            P(("ctx", "exp"), None, None),
        ),
        out_specs=P(("dp", "ctx", "exp"), None),
        check_vma=False,
    )
```
